32 devices in a mesh: wide: 8 (over z, y), narrow: 4 (over x, core).
Axes of the slice: x: 2, y: 2, z: 4, core: 2. Of those that a mesh axis runs over, the one named last changes fastest.
Arguments:
- hidden_in: bfloat16 [3072, 2048], P('wide', 'narrow'), may hold values from -6 to 6
- gain_attn: bfloat16 [2048], P('wide'), may hold values from 0.25 to 1.75
- w_query: bfloat16 [2048, 2048], P('wide', 'narrow'), may hold values from -0.37565048 to 0.37565048
- w_key: bfloat16 [2048, 2048], P('wide', 'narrow'), may hold values from -0.125 to 0.125
- w_value: bfloat16 [2048, 2048], P('wide', 'narrow'), may hold values from -0.125 to 0.125
- w_out: bfloat16 [2048, 2048], P('narrow', 'wide'), may hold values from -1 to 1
- gain_ffn: bfloat16 [2048], P('wide'), may hold values from 0.25 to 1.75
- w_gate: bfloat16 [2048, 8192], P('wide', 'narrow'), may hold values from -0.125 to 0.125
- w_up: bfloat16 [2048, 8192], P('wide', 'narrow'), may hold values from -0.125 to 0.125
- w_down: bfloat16 [8192, 2048], P('narrow', 'wide'), may hold values from -0.0625 to 0.0625
- cotangent: bfloat16 [3072, 2048], P('wide', 'narrow'), may hold values from -6 to 6
- segment_ids: int32 [3072], replicated, may hold values from 0 to 12, as said below
- parents: int32 [13], replicated, may hold values from 0 to 11, as said below
Outputs:
- hidden_out: bfloat16 [3072, 2048], P('wide', 'narrow')
- grad_in: bfloat16 [3072, 2048], P('wide', 'narrow')
- grad_query: float32 [2048, 2048], P('wide', 'narrow')
- grad_key: float32 [2048, 2048], P('wide', 'narrow')
- grad_value: float32 [2048, 2048], P('wide', 'narrow')
- grad_wout: float32 [2048, 2048], P('narrow', 'wide')
- grad_gate: float32 [2048, 8192], P('wide', 'narrow')
- grad_up: float32 [2048, 8192], P('wide', 'narrow')
- grad_down: float32 [8192, 2048], P('narrow', 'wide')
- grad_gainattn: float32 [2048], P('wide')
- grad_gainffn: float32 [2048], P('wide')
- clipped_query: float32 [2048, 2048], P('wide', 'narrow')
- clipped_key: float32 [2048, 2048], P('wide', 'narrow')
- logit_peaks: float32 [32], P('narrow')
The draws below stay inside these ranges and needn't reach their ends.
Inputs may be any that keep to these rules, and one draw needn't show every extreme that they name: `segment_ids`: segment numbers never fall along the tokens; segment 0 starts at token 0 and every segment holds at least one token. parents[0] = 0; for s >= 1, parents[s] < s and parents[parents[parents[s]]] = 0, so all segments form one tree of depth two at most.
All inputs are finite; a program needn't handle non-finite values.
Results may differ from the reference program's by a relative error of at most 0.03.
Values may be sent and summed in bfloat16 or wider, within the bound.
No kernel may reach another device: no remote copies, remote signals or barrier semaphores. Data moves between devices by JAX's collectives and lax.ppermute only.
A program may use at most 320 MiB of HBM per device.

```python
import math
import jax
import jax.numpy as jnp
from jax import lax

D = 2048
HEADS = 32
HDIM = 64
FF = 8192
NSEG = 13
TOKENS = 3072


def draw_w_query(key, part):
    order = jax.random.permutation(jax.random.fold_in(key, 10), HEADS).astype(jnp.float32)
    jitter = jax.random.uniform(jax.random.fold_in(key, 11), (HEADS,), jnp.float32, 0.0, 1.0)
    spread = 0.6 * jnp.exp((order + jitter) / HEADS * math.log(2.8 / 0.6))
    column_scale = jnp.repeat(spread, HDIM)
    values = jax.random.truncated_normal(jax.random.fold_in(key, 12), -6.0, 6.0, (D, D), jnp.float32)
    return (values * D ** (-0.5) * column_scale[None, :]).astype(jnp.bfloat16)


def draw_segment_ids(key, part):
    leading = jax.random.randint(jax.random.fold_in(key, 21), (1,), 48, 81, dtype=jnp.int32)
    others = jax.random.randint(jax.random.fold_in(key, 22), (NSEG - 1,), 8, 25, dtype=jnp.int32)
    weights = jnp.concatenate([leading, others])
    lengths = TOKENS * weights // jnp.sum(weights, dtype=jnp.int32)
    lengths = lengths.at[0].add(TOKENS - jnp.sum(lengths, dtype=jnp.int32))
    bounds = jnp.cumsum(lengths, dtype=jnp.int32)
    positions = jnp.arange(TOKENS, dtype=jnp.int32)
    return jnp.sum((positions[:, None] >= bounds[None, :NSEG - 1]).astype(jnp.int32), axis=1, dtype=jnp.int32)


def draw_parents(key, part):
    parent_of = jnp.zeros((NSEG,), jnp.int32)
    depth_of = jnp.zeros((NSEG,), jnp.int32)
    for member in range(1, NSEG):
        candidate = jax.random.randint(jax.random.fold_in(key, 40 + member), (), 0, member, dtype=jnp.int32)
        if member == NSEG - 2:
            candidate = jnp.zeros((), jnp.int32)
        if member == NSEG - 1:
            candidate = jnp.full((), NSEG - 2, jnp.int32)
        chosen = jnp.where(depth_of[candidate] >= 2, parent_of[candidate], candidate)
        parent_of = parent_of.at[member].set(chosen)
        depth_of = depth_of.at[member].set(depth_of[chosen] + 1)
    return parent_of


def with_spikes(values, own_key, source, target, shards_of, factor):
    owner, partner = [(jnp.arange(values.shape[axis_at]) // (values.shape[axis_at] // shards_of)).reshape([-1 if axis == axis_at else 1 for axis in range(values.ndim)]) for axis_at in (source, target)]
    chosen = jax.random.permutation(own_key, shards_of)[partner]
    strong = (owner == chosen) | (owner == (partner + shards_of // 2) % shards_of)
    return jnp.where(strong, factor * values, values)


def shard_levels(rng, shape, shards, least, largest):
    def one(position, parts):
        heights = jax.random.uniform(jax.random.fold_in(jax.random.fold_in(rng, 6), position), (parts,), jnp.float32, least / len(shards), largest / len(shards))
        return jnp.repeat(jnp.exp(heights), shape[position] // parts).reshape((-1,) + (1,) * (len(shape) - position - 1))

    gain = one(*shards[0])
    for cut in shards[1:]:
        gain = gain * one(*cut)
    return gain


def scatter_about(rng, shape, scale, reach, cuts=(), held_as=jnp.bfloat16):
    result = jax.random.normal(rng, shape, jnp.float32) * scale
    if len(cuts) > 0:
        result = shard_levels(rng, shape, cuts, -0.22, 0.18) * result
    return jnp.clip(result, min=-reach, max=reach).astype(held_as)


def bell_draw_with(stream_key, shape, scale, limit, shards, heavy, kind=jnp.bfloat16):
    array = scale * jax.random.normal(stream_key, shape, jnp.float32)
    if shards:
        array = array * shard_levels(stream_key, shape, shards, -0.22, 0.18)
    return jnp.clip(with_spikes(array, jax.random.fold_in(stream_key, 3), *heavy), -limit, limit).astype(kind)


def setup_inputs(seed: int = 0) -> dict:
    key_list = jax.random.split(jax.random.key(seed), 14)
    hidden_in = scatter_about(key_list[0], (TOKENS, D), 1.0, 6.0, ((0, 8), (1, 4)))
    gain_attn = jnp.clip(1.0 + 0.15 * jax.random.normal(key_list[1], (D,), jnp.float32), 0.25, 1.75).astype(jnp.bfloat16)
    w_query = draw_w_query(jax.random.fold_in(key_list[13], 71), 0)
    w_key = scatter_about(key_list[3], (D, D), D ** -0.5, 0.125, ((0, 8), (1, 4)))
    w_value = scatter_about(key_list[4], (D, D), D ** -0.5, 0.125, ((0, 8), (1, 4)))
    w_out = scatter_about(key_list[5], (D, D), (D // 64) ** -0.5, 1.0, ((0, 4), (1, 8)))
    gain_ffn = jnp.clip(1.0 + 0.15 * jax.random.normal(key_list[6], (D,), jnp.float32), 0.25, 1.75).astype(jnp.bfloat16)
    w_gate = scatter_about(key_list[7], (D, FF), D ** -0.5, 0.125, ((0, 8), (1, 4)))
    w_up = scatter_about(key_list[8], (D, FF), D ** -0.5, 0.125, ((0, 8), (1, 4)))
    w_down = scatter_about(key_list[9], (FF, D), FF ** -0.5, 0.0625, ((0, 4), (1, 8)))
    cotangent = bell_draw_with(key_list[10], (TOKENS, D), 1.0, 6.0, ((0, 8), (1, 4)), (0, 1, 8, 2.0))
    segment_ids = draw_segment_ids(jax.random.fold_in(key_list[13], 71), 0)
    parents = draw_parents(jax.random.fold_in(key_list[13], 71), 0)
    return dict(hidden_in=hidden_in, gain_attn=gain_attn, w_query=w_query, w_key=w_key, w_value=w_value, w_out=w_out, gain_ffn=gain_ffn, w_gate=w_gate, w_up=w_up, w_down=w_down, cotangent=cotangent, segment_ids=segment_ids, parents=parents)


eps_norm = 1e-05
rope_base = 130000.0
clip_limit = 5.0
masked_fill = -1e+30

@jax.custom_vjp
def low(v):
    return lax.optimization_barrier(v.astype(jnp.bfloat16)).astype(jnp.float32)

@jax.custom_vjp
def low_back(v):
    return v

def low_keep(v):
    return (low(v), None)

def low_pass(kept, grad):
    return (grad,)

def back_keep(v):
    return (v, None)

def back_low(kept, grad):
    return (low(grad),)
low.defvjp(low_keep, low_pass)
low_back.defvjp(back_keep, back_low)

def lookup(lookup_table, indices):
    labels = jnp.arange(lookup_table.shape[0], dtype=jnp.int32)
    return lax.optimization_barrier(jnp.sum(jnp.where(indices[:, None] == labels[None, :], lookup_table[None, :], 0), axis=1, dtype=jnp.int32))

def segment_tables(segment_ids, parents):
    labels = jnp.arange(NSEG, dtype=jnp.int32)
    counts = lax.optimization_barrier(jnp.sum((segment_ids[:, None] == labels[None, :]).astype(jnp.int32), axis=0, dtype=jnp.int32))
    starts = jnp.cumsum(counts, dtype=jnp.int32) - counts
    ancestor = lookup(parents, parents)
    parent_len = jnp.where(parents != labels, lookup(counts, parents), 0).astype(jnp.int32)
    ancestor_len = jnp.where(ancestor != parents, lookup(counts, ancestor), 0).astype(jnp.int32)
    return (ancestor, starts, parent_len, ancestor_len)

def token_tables(seg_rows, first_row, parents, tables):
    ancestor, starts, parent_len, ancestor_len = tables
    row_index = first_row + jnp.arange(seg_rows.shape[0], dtype=jnp.int32)
    parent_tok = lookup(parents, seg_rows)
    ancestor_tok = lookup(ancestor, seg_rows)
    places = row_index - lookup(starts, seg_rows) + lookup(parent_len, seg_rows) + lookup(ancestor_len, seg_rows)
    return (row_index, parent_tok, ancestor_tok, places)

def allowed_pairs(query_index, query_seg, parent_tok, ancestor_tok, key_index, key_seg):
    same_tree = (key_seg[None, :] == query_seg[:, None]) | (key_seg[None, :] == parent_tok[:, None]) | (key_seg[None, :] == ancestor_tok[:, None])
    return same_tree & (key_index[None, :] <= query_index[:, None])

def rotary_tables(places):
    frequency = rope_base ** (-2.0 * jnp.arange(HDIM // 2, dtype=jnp.float32) / HDIM)
    angles = places.astype(jnp.float32)[:, None] * frequency[None, :]
    return (jnp.cos(angles), jnp.sin(angles))

def rotate(values, cos_table, sin_table):
    halfway = values.shape[-1] // 2
    leading = values[..., :halfway]
    trailing = values[..., halfway:]
    cosine = cos_table[:, None, :]
    sine_part = sin_table[:, None, :]
    return jnp.concatenate([leading * cosine - trailing * sine_part, trailing * cosine + leading * sine_part], axis=-1)

def product(left, right):
    return jnp.dot(left, right, precision=lax.Precision.HIGHEST)

def rms_normalize(values, norm_gain):
    factor = lax.rsqrt(lax.optimization_barrier(jnp.mean(values * values, axis=-1, keepdims=True)) + eps_norm)
    return values * factor * norm_gain

def attend_block(query_block, offset, key_heads, value_heads, segment_ids, parent_tok, ancestor_tok):
    block_rows = query_block.shape[0]
    query_index = offset + jnp.arange(block_rows, dtype=jnp.int32)
    query_seg = lax.dynamic_slice_in_dim(segment_ids, offset, block_rows)
    query_parent = lax.dynamic_slice_in_dim(parent_tok, offset, block_rows)
    query_ancestor = lax.dynamic_slice_in_dim(ancestor_tok, offset, block_rows)
    key_index = jnp.arange(TOKENS, dtype=jnp.int32)
    allowed = allowed_pairs(query_index, query_seg, query_parent, query_ancestor, key_index, segment_ids)
    scores = low_back(jnp.einsum('qhd,khd->hqk', query_block, key_heads, precision=lax.Precision.HIGHEST) * HDIM ** (-0.5))
    masked = jnp.where(allowed[None], scores, masked_fill)
    highest = lax.optimization_barrier(jnp.max(masked, axis=-1, keepdims=True))
    weights = jnp.where(allowed[None], jnp.exp(masked - highest), 0.0)
    probs_low = low(weights / lax.optimization_barrier(jnp.sum(weights, axis=-1, keepdims=True)))
    mixed_heads = jnp.einsum('hqk,khd->qhd', probs_low, value_heads, precision=lax.Precision.HIGHEST)
    return (mixed_heads.reshape(block_rows, D), lax.optimization_barrier(jnp.max(masked, axis=(1, 2))))

def attention(queries, keys, values, segment_ids, parent_tok, ancestor_tok):
    block_rows = min(512, TOKENS)
    block_count = TOKENS // block_rows
    query_blocks = queries.reshape(block_count, block_rows, HEADS, HDIM)
    key_heads = keys.reshape(TOKENS, HEADS, HDIM)
    value_heads = values.reshape(TOKENS, HEADS, HDIM)
    offsets = jnp.arange(block_count, dtype=jnp.int32) * block_rows
    checked = jax.checkpoint(attend_block)

    def one_block(inputs):
        return checked(inputs[0], inputs[1], key_heads, value_heads, segment_ids, parent_tok, ancestor_tok)
    mixed_heads, maxima = lax.map(one_block, (query_blocks, offsets))
    return (mixed_heads.reshape(TOKENS, D), lax.optimization_barrier(jnp.max(maxima, axis=0)))

def layer_forward(hidden_in, gain_attn, w_query, w_key, w_value, w_out, gain_ffn, w_gate, w_up, w_down, side_tables):
    segment_ids, parent_tok, ancestor_tok, cos_table, sin_table = side_tables
    normed_attn = low(rms_normalize(hidden_in, gain_attn))
    query_lin = low_back(product(normed_attn, w_query)).reshape(TOKENS, HEADS, HDIM)
    key_lin = low_back(product(normed_attn, w_key)).reshape(TOKENS, HEADS, HDIM)
    queries = low(rotate(query_lin, cos_table, sin_table)).reshape(TOKENS, D)
    keys = low(rotate(key_lin, cos_table, sin_table)).reshape(TOKENS, D)
    values = low(low_back(product(normed_attn, w_value)))
    mixed_heads, head_peaks = attention(queries, keys, values, segment_ids, parent_tok, ancestor_tok)
    attended = low(low_back(mixed_heads))
    middle = hidden_in + low_back(product(attended, w_out))
    normed_ffn = low(rms_normalize(low(middle), gain_ffn))
    gate_lin = low_back(product(normed_ffn, w_gate))
    up_lin = low_back(product(normed_ffn, w_up))
    hidden_low = low(jax.nn.silu(gate_lin) * up_lin)
    return (middle + low_back(product(hidden_low, w_down)), head_peaks)

def reference(hidden_in, gain_attn, w_query, w_key, w_value, w_out, gain_ffn, w_gate, w_up, w_down, cotangent, segment_ids, parents):
    tables = segment_tables(segment_ids, parents)
    row_index, parent_tok, ancestor_tok, places = token_tables(segment_ids, 0, parents, tables)
    cos_table, sin_table = rotary_tables(places)
    side_tables = (segment_ids, parent_tok, ancestor_tok, cos_table, sin_table)
    inputs = [hidden_in, gain_attn, w_query, w_key, w_value, w_out, gain_ffn, w_gate, w_up, w_down]
    floats = [argument.astype(jnp.float32) for argument in inputs]

    def forward(hidden, g_attn, wq_in, wk_in, wv_in, wo_in, g_ffn, wg_in, wu_in, wd_in):
        return layer_forward(hidden, g_attn, wq_in, wk_in, wv_in, wo_in, g_ffn, wg_in, wu_in, wd_in, side_tables)
    output, pullback, head_peaks = jax.vjp(forward, *floats, has_aux=True)
    gradients = pullback(cotangent.astype(jnp.float32))
    factor = jnp.sqrt(clip_limit / jnp.maximum(head_peaks, clip_limit))
    column_factor = jnp.repeat(factor, HDIM)
    return (output.astype(jnp.bfloat16), gradients[0].astype(jnp.bfloat16), gradients[2], gradients[3], gradients[4], gradients[5], gradients[7], gradients[8], gradients[9], gradients[1], gradients[6], floats[2] * column_factor[None, :], floats[3] * column_factor[None, :], head_peaks)
```

```python
import functools

import jax
import jax.numpy as jnp
from jax import lax
from jax.experimental import pallas as pl
from jax.experimental.pallas import tpu as pltpu
from jax.sharding import Mesh
from jax.sharding import PartitionSpec as P

HDIM = 64
HALF = HDIM // 2

eps_norm = 1e-05
rope_base = 130000.0
clip_limit = 5.0
masked_fill = -1e30

F32 = jnp.float32
BF16 = jnp.bfloat16
WIDE = ("z", "q", "y")
GROUP = ("q", "y")
NARROW = ("x", "c")
VMEM_BYTES = 48 * 2**20
EXTRA = 16


def lookup(lookup_table, indices):
    labels = jnp.arange(lookup_table.shape[0], dtype=jnp.int32)
    return jnp.sum(
        jnp.where(indices[:, None] == labels[None, :], lookup_table[None, :], 0),
        axis=1,
        dtype=jnp.int32,
    )


def segment_tables(segment_ids, parents):
    labels = jnp.arange(parents.shape[0], dtype=jnp.int32)
    counts = jnp.sum(
        (segment_ids[:, None] == labels[None, :]).astype(jnp.int32), axis=0, dtype=jnp.int32
    )
    starts = jnp.sum(
        jnp.where(labels[None, :] < labels[:, None], counts[None, :], 0), axis=1, dtype=jnp.int32
    )
    ancestor = lookup(parents, parents)
    parent_len = jnp.where(parents != labels, lookup(counts, parents), 0)
    ancestor_len = jnp.where(ancestor != parents, lookup(counts, ancestor), 0)
    return (ancestor, starts, parent_len, ancestor_len)


def dot(left, right, left_dim, right_dim):
    return lax.dot_general(
        left, right, (((left_dim,), (right_dim,)), ((), ())), preferred_element_type=F32
    )


def take(array, index, axis=0):
    return lax.dynamic_index_in_dim(array, index, axis, keepdims=False)


def swap(array, axis):
    return lax.ppermute(array, axis, [(0, 1), (1, 0)])


def ring(array, size):
    return lax.ppermute(array, "z", [(i, (i + 1) % size) for i in range(size)])


def pick(flag, first, second):
    return jnp.where(flag == 0, first, second)


def in_order(flag, own, theirs, axis=0):
    return jnp.stack([pick(flag, own, theirs), pick(flag, theirs, own)], axis=axis)


def params():
    return pltpu.CompilerParams(vmem_limit_bytes=VMEM_BYTES)


def shape(dims, dtype):
    return jax.ShapeDtypeStruct(dims, dtype)


def full(dims):
    return pl.BlockSpec(dims, lambda *_: (0,) * len(dims))


def columns_of(where, k, cols):
    return pl.ds(pl.multiple_of((where[0] ^ k) * cols, cols), cols)


def fill_keys(keys, mask, k_ext, values_t):
    for t in range(keys.shape[0]):
        tile = keys[t].astype(F32)
        spare = k_ext.shape[2] - HDIM - mask.shape[1]
        parts = [tile[HDIM : 2 * HDIM], mask[t].astype(F32)]
        parts.append(jnp.zeros((spare, tile.shape[1]), F32))
        k_ext[t] = jnp.concatenate(parts, axis=0).T.astype(BF16)
        if values_t is not None:
            values_t[t] = jnp.concatenate(
                [tile[2 * HDIM :], jnp.zeros((HDIM, tile.shape[1]), F32)], axis=0
            ).T.astype(BF16)


def query_ext(queries, mask, depth):
    q = queries[0, :HDIM]
    spare = depth - HDIM - mask.shape[1]
    return jnp.concatenate([q, mask[0], jnp.zeros((spare, q.shape[1]), BF16)], axis=0)


def attend_kernel(
    visible, counts, q_pos, k_pos, queries, q_mask, keys, k_mask, low, out, log_norm, peak, k_ext
):
    i = pl.program_id(0)
    tiles, _, width = keys.shape

    @pl.when(i == 0)
    def _():
        fill_keys(keys, k_mask, k_ext, None)

    q_tile = query_ext(queries, q_mask, k_ext.shape[2])
    relative = lax.broadcasted_iota(jnp.int32, (width, width), 0) - lax.broadcasted_iota(
        jnp.int32, (width, width), 1
    )

    def step(n, carry):
        high, total, acc = carry
        j = visible[i * tiles + n]
        scores = dot(k_ext[j], q_tile, 1, 0)
        scores = jnp.where(relative <= (q_pos[i] - k_pos[j]) * width, scores, masked_fill)
        new_high = jnp.maximum(high, jnp.max(scores, axis=0, keepdims=True))
        weights = jnp.exp(scores - new_high)
        shrink = jnp.exp(high - new_high)
        total = total * shrink + jnp.sum(weights, axis=0, keepdims=True)
        acc = acc * shrink + dot(keys[j, 2 * HDIM :], weights.astype(BF16), 1, 0)
        return new_high, total, acc

    high, total, acc = lax.fori_loop(
        0,
        counts[i],
        step,
        (
            jnp.full((1, width), masked_fill, F32),
            jnp.zeros((1, width), F32),
            jnp.zeros((HDIM, width), F32),
        ),
    )
    result = acc / total
    out[0] = result
    low[0] = result.astype(BF16)
    log_norm[0] = high + jnp.log(total)
    peak[0] = high


def attend(tables, queries, q_mask, keys, k_mask):
    q_tiles, features, width = queries.shape
    k_tiles, labels = keys.shape[0], q_mask.shape[1]
    part = lambda i, *_: (i, 0, 0)
    placed = lambda i, visible, counts, q_pos, k_pos: (q_pos[i + q_tiles], 0, 0)
    return pl.pallas_call(
        attend_kernel,
        grid_spec=pltpu.PrefetchScalarGridSpec(
            num_scalar_prefetch=4,
            grid=(q_tiles,),
            in_specs=[
                pl.BlockSpec((1, features, width), part),
                pl.BlockSpec((1, labels, width), part),
                full(keys.shape),
                full(k_mask.shape),
            ],
            out_specs=[
                pl.BlockSpec((1, HDIM, width), placed),
                pl.BlockSpec((1, HDIM, width), part),
                pl.BlockSpec((1, 1, width), part),
                pl.BlockSpec((1, 1, width), part),
            ],
            scratch_shapes=[pltpu.VMEM((k_tiles, width, 2 * HDIM), BF16)],
        ),
        out_shape=[
            shape((q_tiles, HDIM, width), BF16),
            shape((q_tiles, HDIM, width), F32),
            shape((q_tiles, 1, width), F32),
            shape((q_tiles, 1, width), F32),
        ],
        compiler_params=params(),
        cost_estimate=pl.CostEstimate(
            flops=q_tiles * k_tiles * width * width * 3 * HDIM,
            bytes_accessed=(q_tiles + k_tiles) * width * 8 * HDIM,
            transcendentals=q_tiles * k_tiles * width * width // 2,
        ),
        name="attend",
    )(*tables, queries, q_mask, keys, k_mask)


def attend_back_kernel(
    visible,
    counts,
    q_pos,
    k_pos,
    queries,
    q_mask,
    keys,
    k_mask,
    grads,
    out,
    log_norm,
    cosine,
    sine,
    grad_q,
    grad_kv,
    k_ext,
    values_t,
    acc_k,
    acc_v,
):
    i = pl.program_id(0)
    tiles, _, width = keys.shape

    @pl.when(i == 0)
    def _():
        fill_keys(keys, k_mask, k_ext, values_t)
        acc_k[...] = jnp.zeros_like(acc_k)
        acc_v[...] = jnp.zeros_like(acc_v)

    q_tile = query_ext(queries, q_mask, k_ext.shape[2])
    q_rows = q_tile[:HDIM]
    g_tile = grads[0]
    g_ext = jnp.concatenate([g_tile, jnp.zeros_like(g_tile)], axis=0)
    lse = log_norm[0]
    delta = jnp.sum(g_tile.astype(F32) * out[0], axis=0, keepdims=True)
    relative = lax.broadcasted_iota(jnp.int32, (width, width), 0) - lax.broadcasted_iota(
        jnp.int32, (width, width), 1
    )

    def step(n, acc):
        j = visible[i * tiles + n]
        scores = dot(k_ext[j], q_tile, 1, 0)
        scores = jnp.where(relative <= (q_pos[i] - k_pos[j]) * width, scores, masked_fill)
        probs = jnp.exp(scores - lse)
        grad_probs = dot(values_t[j], g_ext, 1, 0)
        grad_scores = (probs * (grad_probs - delta)).astype(BF16)
        acc_v[j] += dot(g_tile, probs.astype(BF16), 1, 1)
        acc_k[j] += dot(q_rows, grad_scores, 1, 1)
        return acc + dot(keys[j, HDIM : 2 * HDIM], grad_scores, 1, 0)

    acc = lax.fori_loop(0, counts[i], step, jnp.zeros((HDIM, width), F32))

    def unrotate(grad, t):
        first, second, c, s = grad[:HALF], grad[HALF:], cosine[t], sine[t]
        return first * c + second * s, second * c - first * s

    mine = q_pos[pl.num_programs(0) * 2]
    first, second = unrotate(acc * HDIM ** (-0.5), mine + i)
    grad_q[0, :HALF] = first.astype(BF16)
    grad_q[0, HALF:] = second.astype(BF16)

    @pl.when(i == pl.num_programs(0) - 1)
    def _():
        for t in range(tiles):
            first, second = unrotate(acc_k[t], t)
            grad_kv[t, :HALF] = first.astype(BF16)
            grad_kv[t, HALF:HDIM] = second.astype(BF16)
            grad_kv[t, HDIM:] = acc_v[t].astype(BF16)


def attend_back(tables, queries, q_mask, keys, k_mask, grads, out, log_norm, cosine, sine):
    q_tiles, features, width = queries.shape
    k_tiles, labels = keys.shape[0], q_mask.shape[1]
    part = lambda i, *_: (i, 0, 0)
    placed = lambda i, visible, counts, q_pos, k_pos: (q_pos[i + q_tiles], 0, 0)
    return pl.pallas_call(
        attend_back_kernel,
        grid_spec=pltpu.PrefetchScalarGridSpec(
            num_scalar_prefetch=4,
            grid=(q_tiles,),
            in_specs=[
                pl.BlockSpec((1, features, width), part),
                pl.BlockSpec((1, labels, width), part),
                full(keys.shape),
                full(k_mask.shape),
                pl.BlockSpec((1, HDIM, width), placed),
                pl.BlockSpec((1, HDIM, width), part),
                pl.BlockSpec((1, 1, width), part),
                full(cosine.shape),
                full(sine.shape),
            ],
            out_specs=[
                pl.BlockSpec((1, HDIM, width), part),
                full((k_tiles, 2 * HDIM, width)),
            ],
            scratch_shapes=[
                pltpu.VMEM((k_tiles, width, 2 * HDIM), BF16),
                pltpu.VMEM((k_tiles, width, 2 * HDIM), BF16),
                pltpu.VMEM((k_tiles, HDIM, width), F32),
                pltpu.VMEM((k_tiles, HDIM, width), F32),
            ],
        ),
        out_shape=[
            shape((q_tiles, HDIM, width), BF16),
            shape((k_tiles, 2 * HDIM, width), BF16),
        ],
        compiler_params=params(),
        cost_estimate=pl.CostEstimate(
            flops=q_tiles * k_tiles * width * width * 6 * HDIM,
            bytes_accessed=(q_tiles + k_tiles) * width * 16 * HDIM,
            transcendentals=q_tiles * k_tiles * width * width // 2,
        ),
        name="attend_back",
    )(*tables, queries, q_mask, keys, k_mask, grads, out, log_norm, cosine, sine)


def row_scale(pieces, width):
    squares = 0.0
    for piece in pieces:
        values = piece[...].astype(F32)
        squares = squares + jnp.sum(values * values, axis=1, keepdims=True)
    return lax.rsqrt(squares / width + eps_norm)


def qkv_kernel(where, *refs):
    pieces, (gain, weights, cosine, sine) = refs[:4], refs[4:8]
    normed, mine, other, scale = refs[-4:]
    rows, cols = pieces[0].shape
    rstd = row_scale(pieces, 4 * cols)
    scale[...] = rstd
    for k, piece in enumerate(pieces):
        span = columns_of(where, k, cols)
        normed[:, span] = (piece[...].astype(F32) * rstd * gain[:, span]).astype(BF16)
    c, s = cosine[...], sine[...]
    features = 3 * HDIM
    for head, out in enumerate((mine, other)):
        lin = dot(weights[head * features : (head + 1) * features, :], normed[...], 1, 1)
        for part, factor in ((0, HDIM ** (-0.5)), (1, 1.0)):
            base = part * HDIM
            first, second = lin[base : base + HALF], lin[base + HALF : base + HDIM]
            out[base : base + HALF] = ((first * c - second * s) * factor).astype(BF16)
            out[base + HALF : base + HDIM] = ((second * c + first * s) * factor).astype(BF16)
        out[2 * HDIM :] = lin[2 * HDIM :].astype(BF16)


def chunk_call(kernel, name, where, inputs, buffers, whole_shapes, out_shapes, cost):
    rows = whole_shapes[0][0] // 4
    in_specs = [full(a.shape) for a in inputs]
    aliases = {}
    extra = []
    if buffers is not None:
        for n, buffer in enumerate(buffers):
            aliases[1 + len(inputs) + n] = n
            in_specs.append(pl.BlockSpec(memory_space=pl.ANY))
            extra.append(buffer)
    chunk = lambda i, where: (where[1], 0)
    out_specs = [pl.BlockSpec((rows, dims[1]), chunk) for dims in whole_shapes]
    out_specs += [full(s.shape) for s in out_shapes]
    return pl.pallas_call(
        kernel,
        grid_spec=pltpu.PrefetchScalarGridSpec(
            num_scalar_prefetch=1, grid=(1,), in_specs=in_specs, out_specs=out_specs
        ),
        out_shape=[shape(dims, BF16) for dims in whole_shapes] + list(out_shapes),
        input_output_aliases=aliases,
        compiler_params=params(),
        cost_estimate=pl.CostEstimate(flops=cost, bytes_accessed=2**23, transcendentals=2**18),
        name=name,
    )(where, *inputs, *extra)


def ffn_kernel(where, *refs):
    mids, cots, (gain, w_gate, w_up, w_down) = refs[:4], refs[4:8], refs[8:12]
    (normed, cot_rows, hidden, grad_gate, grad_up) = refs[-11:-6]
    (keep_out, send_out, keep_back, send_back, gain_term, scale) = refs[-6:]
    rows, cols = mids[0].shape
    width, units = w_gate.shape
    rstd = row_scale(mids, width)
    scale[...] = rstd
    for k in range(4):
        span = columns_of(where, k, cols)
        normed[:, span] = (mids[k][...].astype(F32) * rstd * gain[:, span]).astype(BF16)
        cot_rows[:, span] = cots[k][...]
    step = 256
    for n in range(0, units, step):
        gate = dot(normed[...], w_gate[:, n : n + step], 1, 0)
        up = dot(normed[...], w_up[:, n : n + step], 1, 0)
        grad_hidden = dot(cot_rows[...], w_down[n : n + step, :], 1, 1)
        sigmoid = jax.nn.sigmoid(gate)
        activated = gate * sigmoid
        hidden[:, n : n + step] = (activated * up).astype(BF16)
        grad_gate[:, n : n + step] = (
            grad_hidden * up * sigmoid * (1.0 + gate * (1.0 - sigmoid))
        ).astype(BF16)
        grad_up[:, n : n + step] = (grad_hidden * activated).astype(BF16)
    row_term = 0.0
    for k in range(4):
        span = columns_of(where, k, cols)
        out, back = ((keep_out, keep_back), (send_out, send_back))[k % 2]
        out[k // 2] = dot(hidden[...], w_down[:, span], 1, 0).astype(BF16)
        partial = dot(grad_gate[...], w_gate[span, :], 1, 1)
        partial = partial + dot(grad_up[...], w_up[span, :], 1, 1)
        back[k // 2, :rows] = partial.astype(BF16)
        terms = partial * (mids[k][...].astype(F32) * rstd)
        gain_term[:, span] = jnp.sum(terms, axis=0, keepdims=True)
        row_term = row_term + jnp.sum(terms * gain[:, span], axis=1, keepdims=True)
    put_row_term(row_term, cols, keep_back, send_back)


def put_row_term(row_term, cols, keep, send):
    rows = row_term.shape[0]
    line = jnp.broadcast_to(row_term, (rows, 128)).T[:EXTRA]
    line = jnp.concatenate([line, jnp.zeros((EXTRA, cols - rows), F32)], axis=1).astype(BF16)
    for ref in (keep, send):
        ref[0, rows:] = line
        ref[1, rows:] = line


def qkv_back_kernel(where, *refs):
    pieces, (scale, gain, weights, mine, other) = refs[:4], refs[4:9]
    keep, send, gain_term = refs[-3:]
    rows, cols = pieces[0].shape
    rstd = scale[...]
    features = 3 * HDIM
    row_term = 0.0
    for k in range(4):
        span = columns_of(where, k, cols)
        back = (keep, send)[k % 2]
        partial = dot(mine[...], weights[:features, span], 0, 0)
        partial = partial + dot(other[...], weights[features:, span], 0, 0)
        back[k // 2, :rows] = partial.astype(BF16)
        terms = partial * (pieces[k][...].astype(F32) * rstd)
        gain_term[:, span] = jnp.sum(terms, axis=0, keepdims=True)
        row_term = row_term + jnp.sum(terms * gain[:, span], axis=1, keepdims=True)
    put_row_term(row_term, cols, keep, send)


def project_kernel(where, attended, weights, keep, send):
    cols = keep.shape[2]
    for k in range(4):
        span = columns_of(where, k, cols)
        (keep, send)[k % 2][k // 2] = dot(attended[...], weights[:, span], 0, 0).astype(BF16)


def project_back_kernel(where, p0, p1, p2, p3, attended, weights, grad_att, grad_weights):
    cols = p0.shape[1]
    total = 0.0
    for k, piece in enumerate((p0, p1, p2, p3)):
        span = columns_of(where, k, cols)
        total = total + dot(weights[:, span], piece[...], 1, 1)
        grad_weights[:, span] = dot(attended[...], piece[...], 1, 0).astype(BF16)
    grad_att[...] = total.astype(BF16)


def small_call(kernel, name, where, inputs, out_shapes, cost):
    return pl.pallas_call(
        kernel,
        grid_spec=pltpu.PrefetchScalarGridSpec(
            num_scalar_prefetch=1,
            grid=(1,),
            in_specs=[full(a.shape) for a in inputs],
            out_specs=[full(s.shape) for s in out_shapes],
        ),
        out_shape=list(out_shapes),
        compiler_params=params(),
        cost_estimate=pl.CostEstimate(flops=cost, bytes_accessed=2**22, transcendentals=0),
        name=name,
    )(where, *inputs)


def on_device(
    sizes,
    hidden_in,
    gain_attn,
    w_query,
    w_key,
    w_value,
    w_out,
    gain_ffn,
    w_gate,
    w_up,
    w_down,
    cotangent,
    segment_ids,
    parents,
):
    nz, nq, ny, nx, nc = sizes
    rows, cols = hidden_in.shape
    groups = nq * ny
    group_rows = nz * rows
    width = cols * nx * nc
    slab = gain_attn.shape[0]
    head = 3 * HDIM
    units = w_gate.shape[1] // nz

    zi, qi, yi, xi, ci = [lax.axis_index(a) for a in ("z", "q", "y", "x", "c")]
    group = qi * ny + yi
    own_columns = xi * nc + ci
    zs = [(zi - s) % nz for s in range(nz)]
    where = [jnp.stack([own_columns, z]).astype(jnp.int32) for z in zs]

    def gather_chunks(block):
        held = [block]
        for _ in range(nz - 1):
            held.append(ring(held[-1], nz))
        chunks = []
        for mine in held:
            other = swap(mine, "x")
            chunks.append([mine, swap(mine, "c"), other, swap(other, "c")])
        return chunks, held[-1]

    def scatter_narrow(keep, send):
        held = keep.astype(F32) + swap(send, "c").astype(F32)
        return held[0] + swap(held[1].astype(BF16), "x").astype(F32)

    def scatter_chunks(parts):
        carried = None
        for s in list(range(1, nz)) + [0]:
            own = scatter_narrow(*parts[s])
            if carried is not None:
                own = own + ring(carried, nz).astype(F32)
            carried = own.astype(BF16)
        return own

    def spread_z(parts):
        return lax.all_to_all(parts, "z", split_axis=0, concat_axis=0, tiled=True)

    def gather_group(parts):
        if nq > 1:
            return lax.all_gather(parts, GROUP, axis=0, tiled=False)
        return in_order(yi, parts, swap(parts, "y"))

    def scatter_groups(parts):
        if nq > 1:
            return lax.psum_scatter(parts, GROUP, scatter_dimension=0, tiled=False)
        return take(parts, yi).astype(F32) + swap(take(parts, 1 - yi), "y").astype(F32)

    def sum_small(values, axes):
        for axis in axes:
            if axis == "z":
                for bit in (1, 2):
                    values = values + lax.ppermute(values, "z", [(i, i ^ bit) for i in range(nz)])
            elif axis == "q":
                values = lax.psum(values, "q") if nq > 1 else values
            else:
                values = values + swap(values, axis)
        return values

    gain_slots = jnp.zeros((nz * groups, 2, slab), F32)
    both_gains = jnp.stack([gain_attn, gain_ffn]).astype(F32)
    gain_slots = lax.dynamic_update_slice(gain_slots, both_gains[None], (zi * groups + group, 0, 0))
    gains = sum_small(gain_slots, ("y", "z", "q")).transpose(1, 0, 2).reshape(2, width)
    gain1, gain2 = gains[:1], gains[1:]

    x_chunks, x_last = gather_chunks(hidden_in)
    stacked = jnp.stack([w_query, w_key, w_value]).reshape(3, slab, nz, ny, HDIM)
    stacked = stacked.transpose(2, 3, 0, 4, 1).reshape(nz, ny * head, slab)
    w_qkv = gather_group(spread_z(stacked))
    w_qkv = w_qkv.transpose(2, 1, 0, 3).reshape(ny, head, width)
    w_qkv = jnp.concatenate([take(w_qkv, yi), take(w_qkv, 1 - yi)], axis=0)

    late = lax.optimization_barrier((w_gate, w_up, w_down, w_out, cotangent, x_last))
    w_gate_, w_up_, w_down_, w_out_, cotangent_ = late[:5]

    def gather_rows(weight):
        got = gather_group(spread_z(weight.reshape(slab, nz, units).transpose(1, 0, 2)))
        return got.transpose(1, 0, 2, 3).reshape(width, units)

    wo = lax.all_gather(w_out_, WIDE, axis=0, tiled=False)
    wo = wo.transpose(1, 0, 2).reshape(w_out.shape[0], width)
    wg, wu = gather_rows(w_gate_), gather_rows(w_up_)
    wd = gather_group(spread_z(w_down_.reshape(nz, units, slab)))
    wd = wd.transpose(2, 1, 0, 3).reshape(units, width)
    cot_chunks, _ = gather_chunks(cotangent_)

    ancestor, starts, parent_len, ancestor_len = segment_tables(segment_ids, parents)
    q_blocks = [(z * nq + qi) * ny + (yi ^ dy) for dy in range(ny) for z in zs]
    k_blocks = [(z * nq + q) * ny + (yi ^ dy) for q in range(nq) for dy in range(ny) for z in zs]
    segments = segment_ids.reshape(-1, rows)
    k_seg = jnp.stack([take(segments, b) for b in k_blocks])
    k_pos = jnp.stack(k_blocks).astype(jnp.int32)
    q_tiles, k_tiles = len(q_blocks), len(k_blocks)
    of_queries = lambda a: lax.dynamic_slice_in_dim(a, qi * q_tiles, q_tiles, 0)
    flat = k_seg.reshape(-1)
    labels = jnp.arange(-(-parents.shape[0] // 16) * 16, dtype=jnp.int32)[None, :, None]
    places = k_pos[:, None] * rows + jnp.arange(rows, dtype=jnp.int32)[None]
    places = places + lookup(parent_len + ancestor_len - starts, flat).reshape(k_tiles, rows)
    k_own = labels == k_seg[:, None]
    q_seen = of_queries(
        k_own
        | (labels == lookup(parents, flat).reshape(k_tiles, 1, rows))
        | (labels == lookup(ancestor, flat).reshape(k_tiles, 1, rows))
    )
    q_mask = jnp.where(q_seen, 0.0, masked_fill).astype(BF16)
    k_mask = k_own.astype(BF16)
    q_pos = of_queries(k_pos)
    shown = jnp.any(jnp.any(q_seen, axis=2)[:, None] & jnp.any(k_own, axis=2)[None], axis=2)
    shown = shown & (k_pos[None, :] <= q_pos[:, None])
    number = jnp.arange(k_tiles, dtype=jnp.int32)
    earlier = number[None, None, :] < number[None, :, None]
    before = jnp.sum((shown[:, None, :] & earlier).astype(jnp.int32), axis=2)
    chosen = shown[:, None, :] & (before[:, None, :] == number[None, :, None])
    visible = jnp.sum(jnp.where(chosen, number[None, None, :], 0), axis=2, dtype=jnp.int32)
    slots = jnp.stack([z * ny + (yi ^ dy) for dy in range(ny) for z in zs]).astype(jnp.int32)
    q_info = jnp.concatenate([q_pos, slots, (qi * q_tiles).reshape(1).astype(jnp.int32)])
    tables = (
        visible.reshape(-1),
        jnp.sum(shown.astype(jnp.int32), axis=1, dtype=jnp.int32),
        q_info,
        k_pos,
    )
    frequency = rope_base ** (-2.0 * jnp.arange(HALF, dtype=F32) / HDIM)
    angles = places.astype(F32)[:, None, :] * frequency[None, :, None]
    cosine, sine = jnp.cos(angles), jnp.sin(angles)
    cos_q, sin_q = of_queries(cosine), of_queries(sine)

    buffers, mine, theirs, scale1 = None, [], [], []
    for s in range(nz):
        inputs = (*x_chunks[s], gain1, w_qkv, cos_q[s], sin_q[s])
        normed1, own, other, scale = chunk_call(
            qkv_kernel,
            "qkv",
            where[s],
            inputs,
            buffers,
            [(group_rows, width)],
            [shape((head, rows), BF16), shape((head, rows), BF16), shape((rows, 1), F32)],
            4 * rows * width * head,
        )
        buffers = [normed1]
        mine.append(own)
        theirs.append(swap(other, "y"))
        scale1.append(scale)
    queries = jnp.stack(mine + theirs)
    keys = queries
    if nq > 1:
        keys = lax.all_gather(queries, "q", axis=0, tiled=True)
    att_low, att, log_norm, peak = attend(tables, queries, q_mask, keys, k_mask)

    att_t = lax.all_to_all(att_low, ("z", "y"), split_axis=0, concat_axis=0, tiled=True)
    att_t = att_t.reshape(nz * ny * HDIM, rows)
    keep, send = small_call(
        project_kernel,
        "project",
        where[0],
        (att_t, wo),
        [shape((2, rows, cols), BF16)] * 2,
        2 * rows * width * att_t.shape[0],
    )
    residual_mid = hidden_in.astype(F32) + scatter_narrow(keep, send)
    mid_block = residual_mid.astype(BF16)
    mid_chunks, _ = gather_chunks(mid_block)

    buffers, out_parts, back_parts, gain2_term = None, [], [], 0.0
    whole = [(group_rows, width)] * 2 + [(group_rows, units)] * 3
    for s in range(nz):
        results = chunk_call(
            ffn_kernel,
            "feed_forward",
            where[s],
            (*mid_chunks[s], *cot_chunks[s], gain2, wg, wu, wd),
            buffers,
            whole,
            [shape((2, rows, cols), BF16)] * 2
            + [shape((2, rows + EXTRA, cols), BF16)] * 2
            + [shape((1, width), F32), shape((rows, 1), F32)],
            12 * rows * width * units,
        )
        buffers = results[:5]
        out_parts.append(results[5:7])
        back_parts.append(results[7:9])
        gain2_term = gain2_term + results[9]
        if s == 0:
            scale2 = results[10]
    normed2, cot_rows, hidden, grad_gate_lin, grad_up_lin = buffers
    summed2 = scatter_chunks(back_parts)
    hidden_out = (residual_mid + scatter_chunks(out_parts)).astype(BF16)

    def norm_back(summed, gain, block, rstd):
        gain = lax.dynamic_slice_in_dim(gain, own_columns * cols, cols, 1)
        mean = summed[rows, :rows].reshape(rows, 1) / width
        return rstd * (summed[:rows] * gain - block.astype(F32) * rstd * mean)

    grad_mid = cotangent.astype(F32) + norm_back(summed2, gain2, mid_block, scale2)
    branch = grad_mid.astype(BF16)
    branch_x = swap(branch, "x")
    pieces = (branch, swap(branch, "c"), branch_x, swap(branch_x, "c"))

    grad_att, wo_back = small_call(
        project_back_kernel,
        "project_back",
        where[0],
        (*pieces, att_t, wo),
        [shape(att_t.shape, BF16), shape(wo.shape, BF16)],
        4 * rows * width * att_t.shape[0],
    )
    grad_att = grad_att.reshape(nz * ny, HDIM, rows)
    grad_att = lax.all_to_all(grad_att, ("z", "y"), split_axis=0, concat_axis=0, tiled=True)
    grad_q, grad_kv = attend_back(
        tables, queries, q_mask, keys, k_mask, grad_att, att, log_norm, cosine, sine
    )
    if nq > 1:
        grad_kv = lax.psum_scatter(grad_kv, "q", scatter_dimension=0, tiled=True)
    back = jnp.concatenate([grad_q, grad_kv], axis=1)
    order = list(range(1, nz)) + [0]
    other_back = {s: swap(back[nz + s], "y") for s in order}
    parts, gain1_term = [None] * nz, 0.0
    for s in order:
        keep, send, term = small_call(
            qkv_back_kernel,
            "qkv_back",
            where[s],
            (*x_chunks[s], scale1[s], gain1, w_qkv, back[s], other_back[s]),
            [shape((2, rows + EXTRA, cols), BF16)] * 2 + [shape((1, width), F32)],
            4 * rows * width * head,
        )
        parts[s] = (keep, send)
        gain1_term = gain1_term + term
    summed1 = scatter_chunks(parts)
    grad_in = (grad_mid + norm_back(summed1, gain1, hidden_in, scale1[0])).astype(BF16)

    def units_back(grad):
        parts = grad.astype(BF16).reshape(nz, groups, slab, units).transpose(1, 0, 2, 3)
        parts = spread_z(scatter_groups(parts).astype(BF16))
        return parts.transpose(1, 0, 2).reshape(slab, nz * units).astype(F32)

    grad_wg = units_back(dot(normed2, grad_gate_lin, 0, 0))
    grad_wu = units_back(dot(normed2, grad_up_lin, 0, 0))
    down = dot(hidden, cot_rows, 0, 0).astype(BF16).reshape(units, nz, groups, slab)
    down = spread_z(scatter_groups(down.transpose(2, 1, 0, 3)).astype(BF16))
    grad_wd = down.reshape(nz * units, slab).astype(F32)
    wo_back = wo_back.reshape(-1, nz * groups, slab).transpose(1, 0, 2)
    grad_wo = lax.psum_scatter(wo_back, WIDE, scatter_dimension=0, tiled=False).astype(F32)

    def absolute(chunks):
        stacked = jnp.stack([chunks[-s % nz] for s in range(nz)])
        return jnp.roll(stacked, zi, axis=0)

    back_own = absolute([back[s] for s in range(nz)])
    back_other = absolute([other_back[s] for s in range(nz)])
    back_abs = jnp.stack([pick(yi, back_own, back_other), pick(yi, back_other, back_own)])
    back_abs = back_abs.transpose(0, 2, 1, 3).reshape(ny * head, group_rows)
    grad_qkv = dot(back_abs, normed1, 1, 0).astype(BF16).reshape(ny * head, nz, groups, slab)
    grad_qkv = spread_z(scatter_groups(grad_qkv.transpose(2, 1, 0, 3)).astype(BF16))
    grad_qkv = grad_qkv.reshape(nz, ny, 3, HDIM, slab).transpose(2, 4, 0, 1, 3)
    grad_qkv = grad_qkv.reshape(3, slab, nz * ny * HDIM).astype(F32)

    terms = jnp.concatenate([gain1_term, gain2_term], axis=0)
    terms = sum_small(terms, ("c", "x", "y", "z", "q"))
    terms = lax.dynamic_slice_in_dim(terms, (zi * groups + group) * slab, slab, 1)

    peak_slots = jnp.zeros((nz * groups,), F32)
    peak_slots = lax.dynamic_update_slice(
        peak_slots, jnp.max(peak).reshape(1), (zi * groups + group,)
    )
    peaks = sum_small(peak_slots, ("y", "z", "q")).reshape(nz, nq, ny)
    head_peaks = jnp.max(peaks, axis=1).reshape(nz * ny)
    factor = jnp.sqrt(clip_limit / jnp.maximum(head_peaks, clip_limit))
    column_factor = jnp.repeat(factor, HDIM)
    return (
        hidden_out,
        grad_in,
        grad_qkv[0],
        grad_qkv[1],
        grad_qkv[2],
        grad_wo,
        grad_wg,
        grad_wu,
        grad_wd,
        terms[0],
        terms[1],
        w_query.astype(F32) * column_factor[None, :],
        w_key.astype(F32) * column_factor[None, :],
        head_peaks,
    )


def solution(mesh):
    wide, narrow = mesh.devices.shape
    sizes = (4, wide // 8, 2, narrow // 2, 2)
    fine = Mesh(mesh.devices.reshape(sizes), ("z", "q", "y", "x", "c"))
    both = P(WIDE, NARROW)
    turned = P(NARROW, WIDE)
    return jax.shard_map(
        functools.partial(on_device, sizes),
        mesh=fine,
        in_specs=(
            both, P(WIDE), both, both, both, turned, P(WIDE), both, both, turned, both, P(), P()
        ),
        out_specs=(
            both, both, both, both, both, turned, both, both, turned,
            P(WIDE), P(WIDE), both, both, P(NARROW),
        ),
        check_vma=False,
    )
```

```python
import functools

import jax
import jax.numpy as jnp
from jax import lax
from jax.experimental import pallas as pl
from jax.experimental.pallas import tpu as pltpu
from jax.sharding import Mesh
from jax.sharding import PartitionSpec as P

HDIM = 64
HALF = HDIM // 2

eps_norm = 1e-05
rope_base = 130000.0
clip_limit = 5.0
masked_fill = -1e30

F32 = jnp.float32
BF16 = jnp.bfloat16
WIDE = ("z", "q", "y")
GROUP = ("q", "y")
NARROW = ("x", "c")
VMEM_BYTES = 60 * 2**20
EXTRA = 16


def lookup(lookup_table, indices):
    labels = jnp.arange(lookup_table.shape[0], dtype=jnp.int32)
    return jnp.sum(
        jnp.where(indices[:, None] == labels[None, :], lookup_table[None, :], 0),
        axis=1,
        dtype=jnp.int32,
    )


def segment_tables(segment_ids, parents):
    labels = jnp.arange(parents.shape[0], dtype=jnp.int32)
    counts = jnp.sum(
        (segment_ids[:, None] == labels[None, :]).astype(jnp.int32), axis=0, dtype=jnp.int32
    )
    starts = jnp.sum(
        jnp.where(labels[None, :] < labels[:, None], counts[None, :], 0), axis=1, dtype=jnp.int32
    )
    ancestor = lookup(parents, parents)
    parent_len = jnp.where(parents != labels, lookup(counts, parents), 0)
    ancestor_len = jnp.where(ancestor != parents, lookup(counts, ancestor), 0)
    return (ancestor, starts, parent_len, ancestor_len)


def dot(left, right, left_dim, right_dim):
    return lax.dot_general(
        left, right, (((left_dim,), (right_dim,)), ((), ())), preferred_element_type=F32
    )


def take(array, index, axis=0):
    return lax.dynamic_index_in_dim(array, index, axis, keepdims=False)


def swap(array, axis):
    return lax.ppermute(array, axis, [(0, 1), (1, 0)])


def ring(array, size):
    return lax.ppermute(array, "z", [(i, (i + 1) % size) for i in range(size)])


def pick(flag, first, second):
    return jnp.where(flag == 0, first, second)


def together(*values):
    return lax.optimization_barrier(values)


def params():
    return pltpu.CompilerParams(vmem_limit_bytes=VMEM_BYTES)


def cost(time):
    return pl.CostEstimate(flops=int(time * 1e9), bytes_accessed=1000, transcendentals=0)


def shape(dims, dtype):
    return jax.ShapeDtypeStruct(dims, dtype)


def full(dims):
    return pl.BlockSpec(dims, lambda *_: (0,) * len(dims))


def fill_tiles(sources, mask, held, k_ext, values_t):
    if len(sources) == 1:
        held[...] = sources[0][...]
    else:
        for t, source in enumerate(sources):
            held[t] = source[...]
    for t in range(held.shape[0]):
        tile = held[t].astype(F32)
        spare = k_ext.shape[2] - HDIM - mask.shape[1]
        parts = [tile[HDIM : 2 * HDIM], mask[t].astype(F32)]
        parts.append(jnp.zeros((spare, tile.shape[1]), F32))
        k_ext[t] = jnp.concatenate(parts, axis=0).T.astype(BF16)
        if values_t is not None:
            values_t[t] = jnp.concatenate(
                [tile[2 * HDIM :], jnp.zeros((HDIM, tile.shape[1]), F32)], axis=0
            ).T.astype(BF16)


def query_ext(q, mask, depth):
    spare = depth - HDIM - mask.shape[1]
    return jnp.concatenate([q, mask[0], jnp.zeros((spare, q.shape[1]), BF16)], axis=0)


def attend_kernel(visible, counts, q_pos, k_pos, *refs):
    q_mask, k_mask, low, out, log_norm, peak, held, k_ext = refs[-8:]
    i = pl.program_id(0)
    tiles, _, width = held.shape

    @pl.when(i == 0)
    def _():
        fill_tiles(refs[:-8], k_mask, held, k_ext, None)

    mine = q_pos[pl.num_programs(0) * 2]
    q_tile = query_ext(held[mine + i, :HDIM], q_mask, k_ext.shape[2])
    relative = lax.broadcasted_iota(jnp.int32, (width, width), 0) - lax.broadcasted_iota(
        jnp.int32, (width, width), 1
    )

    def step(n, carry):
        high, total, acc = carry
        j = visible[i * tiles + n]
        scores = dot(k_ext[j], q_tile, 1, 0)
        scores = jnp.where(relative <= (q_pos[i] - k_pos[j]) * width, scores, masked_fill)
        new_high = jnp.maximum(high, jnp.max(scores, axis=0, keepdims=True))
        weights = jnp.exp(scores - new_high)
        shrink = jnp.exp(high - new_high)
        total = total * shrink + jnp.sum(weights, axis=0, keepdims=True)
        acc = acc * shrink + dot(held[j, 2 * HDIM :], weights.astype(BF16), 1, 0)
        return new_high, total, acc

    high, total, acc = lax.fori_loop(
        0,
        counts[i],
        step,
        (
            jnp.full((1, width), masked_fill, F32),
            jnp.zeros((1, width), F32),
            jnp.zeros((HDIM, width), F32),
        ),
    )
    result = acc / total
    out[0] = result
    low[0] = result.astype(BF16)
    log_norm[0] = high + jnp.log(total)
    peak[0] = high


def attend(tables, tiles, q_mask, k_mask):
    q_tiles, labels, width = q_mask.shape
    k_tiles = k_mask.shape[0]
    part = lambda i, *_: (i, 0, 0)
    placed = lambda i, visible, counts, q_pos, k_pos: (q_pos[i + q_tiles], 0, 0)
    return pl.pallas_call(
        attend_kernel,
        grid_spec=pltpu.PrefetchScalarGridSpec(
            num_scalar_prefetch=4,
            grid=(q_tiles,),
            in_specs=[full(a.shape) for a in tiles]
            + [pl.BlockSpec((1, labels, width), part), full(k_mask.shape)],
            out_specs=[
                pl.BlockSpec((1, HDIM, width), placed),
                pl.BlockSpec((1, HDIM, width), part),
                pl.BlockSpec((1, 1, width), part),
                pl.BlockSpec((1, 1, width), part),
            ],
            scratch_shapes=[
                pltpu.VMEM((k_tiles, 3 * HDIM, width), BF16),
                pltpu.VMEM((k_tiles, width, 2 * HDIM), BF16),
            ],
        ),
        out_shape=[
            shape((q_tiles, HDIM, width), BF16),
            shape((q_tiles, HDIM, width), F32),
            shape((q_tiles, 1, width), F32),
            shape((q_tiles, 1, width), F32),
        ],
        compiler_params=params(),
        cost_estimate=cost(18),
        name="attend",
    )(*tables, *tiles, q_mask, k_mask)


def attend_back_kernel(visible, counts, q_pos, k_pos, *refs):
    q_mask, k_mask, grads, out, log_norm, cosine, sine, back = refs[-13:-5]
    held, k_ext, values_t, acc_k, acc_v = refs[-5:]
    i = pl.program_id(0)
    tiles, _, width = held.shape

    @pl.when(i == 0)
    def _():
        fill_tiles(refs[:-13], k_mask, held, k_ext, values_t)
        acc_k[...] = jnp.zeros_like(acc_k)
        acc_v[...] = jnp.zeros_like(acc_v)

    mine = q_pos[pl.num_programs(0) * 2]
    q_rows = held[mine + i, :HDIM]
    q_tile = query_ext(q_rows, q_mask, k_ext.shape[2])
    g_tile = grads[0]
    g_ext = jnp.concatenate([g_tile, jnp.zeros_like(g_tile)], axis=0)
    lse = log_norm[0]
    delta = jnp.sum(g_tile.astype(F32) * out[0], axis=0, keepdims=True)
    relative = lax.broadcasted_iota(jnp.int32, (width, width), 0) - lax.broadcasted_iota(
        jnp.int32, (width, width), 1
    )

    def step(n, acc):
        j = visible[i * tiles + n]
        scores = dot(k_ext[j], q_tile, 1, 0)
        scores = jnp.where(relative <= (q_pos[i] - k_pos[j]) * width, scores, masked_fill)
        probs = jnp.exp(scores - lse)
        grad_probs = dot(values_t[j], g_ext, 1, 0)
        grad_scores = (probs * (grad_probs - delta)).astype(BF16)
        acc_v[j] += dot(g_tile, probs.astype(BF16), 1, 1)
        acc_k[j] += dot(q_rows, grad_scores, 1, 1)
        return acc + dot(held[j, HDIM : 2 * HDIM], grad_scores, 1, 0)

    acc = lax.fori_loop(0, counts[i], step, jnp.zeros((HDIM, width), F32))

    def put_unrotated(grad, t, base):
        first, second, c, s = grad[:HALF], grad[HALF:], cosine[t], sine[t]
        back[t, base : base + HALF] = (first * c + second * s).astype(BF16)
        back[t, base + HALF : base + HDIM] = (second * c - first * s).astype(BF16)

    put_unrotated(acc * HDIM ** (-0.5), mine + i, 0)

    @pl.when(i == pl.num_programs(0) - 1)
    def _():
        for t in range(tiles):
            put_unrotated(acc_k[t], t, HDIM)
            back[t, 2 * HDIM :] = acc_v[t].astype(BF16)


def attend_back(tables, tiles, q_mask, k_mask, grads, out, log_norm, cosine, sine):
    q_tiles, labels, width = q_mask.shape
    k_tiles = k_mask.shape[0]
    part = lambda i, *_: (i, 0, 0)
    placed = lambda i, visible, counts, q_pos, k_pos: (q_pos[i + q_tiles], 0, 0)
    return pl.pallas_call(
        attend_back_kernel,
        grid_spec=pltpu.PrefetchScalarGridSpec(
            num_scalar_prefetch=4,
            grid=(q_tiles,),
            in_specs=[full(a.shape) for a in tiles]
            + [
                pl.BlockSpec((1, labels, width), part),
                full(k_mask.shape),
                pl.BlockSpec((1, HDIM, width), placed),
                pl.BlockSpec((1, HDIM, width), part),
                pl.BlockSpec((1, 1, width), part),
                full(cosine.shape),
                full(sine.shape),
            ],
            out_specs=full((k_tiles, 3 * HDIM, width)),
            scratch_shapes=[
                pltpu.VMEM((k_tiles, 3 * HDIM, width), BF16),
                pltpu.VMEM((k_tiles, width, 2 * HDIM), BF16),
                pltpu.VMEM((k_tiles, width, 2 * HDIM), BF16),
                pltpu.VMEM((k_tiles, HDIM, width), F32),
                pltpu.VMEM((k_tiles, HDIM, width), F32),
            ],
        ),
        out_shape=shape((k_tiles, 3 * HDIM, width), BF16),
        compiler_params=params(),
        cost_estimate=cost(22),
        name="attend_back",
    )(*tables, *tiles, q_mask, k_mask, grads, out, log_norm, cosine, sine)


def row_scale(pieces, width):
    squares = 0.0
    for piece in pieces:
        values = piece[...].astype(F32)
        squares = squares + jnp.sum(values * values, axis=1, keepdims=True)
    return lax.rsqrt(squares / width + eps_norm)


def aligned(start, size):
    return pl.ds(pl.multiple_of(start, size), size)


def block_of(where, k):
    return where[0] ^ k


def half_columns(where, h, wide):
    return aligned((h ^ where[1]) * wide, wide)


def put_normed(where, pieces, rstd, gain, normed):
    cols = pieces[0].shape[1]
    half = cols // 2
    for k, piece in enumerate(pieces):
        block = block_of(where, k)
        values = piece[...].astype(F32) * rstd * gain[:, aligned(block * cols, cols)]
        for part in range(2):
            columns = aligned((part * 4 + block) * half, half)
            normed[:, columns] = values[:, part * half : (part + 1) * half].astype(BF16)


def qkv_kernel(where, *refs):
    pieces, (gain, w_first, w_second, cosine, sine) = refs[:4], refs[4:9]
    normed, mine, other, scale = refs[-4:]
    rows, cols = pieces[0].shape
    half = cols // 2
    rstd = row_scale(pieces, 4 * cols)
    scale[...] = rstd
    put_normed(where, pieces, rstd, gain, normed)
    c, s = cosine[...], sine[...]
    features = 3 * HDIM
    for out, head in ((mine, where[2]), (other, 1 - where[2])):
        span = aligned(head * features, features)
        lin = 0.0
        for h, weights in enumerate((w_first, w_second)):
            for z in range(4):
                columns = aligned(((h ^ where[1]) * 4 + z) * half, half)
                lin = lin + dot(weights[z, span, :], normed[:, columns], 1, 1)
        for part, factor in ((0, HDIM ** (-0.5)), (1, 1.0)):
            base = part * HDIM
            first, second = lin[base : base + HALF], lin[base + HALF : base + HDIM]
            out[base : base + HALF] = ((first * c - second * s) * factor).astype(BF16)
            out[base + HALF : base + HDIM] = ((second * c + first * s) * factor).astype(BF16)
        out[2 * HDIM :] = lin[2 * HDIM :].astype(BF16)


def chunk_call(kernel, name, time, where, s, inputs, buffers, whole_shapes, out_shapes, held=False):
    def spec(dims, how):
        rest = (0,) * (len(dims) - 1)
        if how == "whole":
            return full(dims)
        if how == "there":
            return pl.BlockSpec(memory_space=pl.ANY)
        block = (dims[0] // 4, *dims[1:])
        if how == "chunk":
            return pl.BlockSpec(block, lambda i, where: (s, *rest))
        return pl.BlockSpec(block, lambda i, where: (where[3], *rest))

    in_specs = [spec(a.shape, how) for a, how in inputs]
    arrays = [a for a, _ in inputs]
    aliases = {}
    if buffers is not None:
        for n, buffer in enumerate(buffers):
            aliases[1 + len(arrays)] = n
            in_specs.append(pl.BlockSpec(memory_space=pl.ANY))
            arrays.append(buffer)
    out_specs = [spec(dims, how) for dims, how in whole_shapes]
    out_specs += [full(a.shape) for a in out_shapes]
    scratch = []
    if held:
        there = [a for a, how in inputs if how == "there"]
        rows = sum(a.shape[0] for a in there)
        scratch = [
            pltpu.VMEM((rows, there[0].shape[1]), BF16),
            pltpu.SemaphoreType.DMA((len(there),)),
        ]
    return pl.pallas_call(
        kernel,
        grid_spec=pltpu.PrefetchScalarGridSpec(
            num_scalar_prefetch=1,
            grid=(1,),
            in_specs=in_specs,
            out_specs=out_specs,
            scratch_shapes=scratch,
        ),
        out_shape=[shape(dims, BF16) for dims, _ in whole_shapes] + list(out_shapes),
        input_output_aliases=aliases,
        compiler_params=params(),
        cost_estimate=cost(time),
        name=name,
    )(where, *arrays)


def fetch(weights, held, sems):
    copies, start = [], 0
    for n, weight in enumerate(weights):
        rows = weight.shape[0]
        copies.append(pltpu.make_async_copy(weight, held.at[pl.ds(start, rows)], sems.at[n]))
        copies[-1].start()
        start += rows
    return copies


def ffn_kernel(where, *refs):
    normed, hidden, gates, ups, scale, held, sems = refs[-7:]
    mids, gain, weights = refs[:4], refs[4], refs[5 : 5 + sems.shape[0]]
    rows, cols = mids[0].shape
    units, wide = hidden.shape[1], 2 * cols
    copies = fetch(weights, held, sems)
    rstd = row_scale(mids, 4 * cols)
    scale[...] = rstd
    put_normed(where, mids, rstd, gain, normed)
    for copy in copies:
        copy.wait()
    step = 256
    for n in range(0, units, step):
        span = slice(n, n + step)
        gate = up = 0.0
        for h in range(2):
            values = normed[:, half_columns(where, h, wide)]
            gate = gate + dot(values, held[h * wide : (h + 1) * wide, span], 1, 0)
            up = up + dot(values, held[(h + 2) * wide : (h + 3) * wide, span], 1, 0)
        hidden[:, span] = (gate * jax.nn.sigmoid(gate) * up).astype(BF16)
        gates[:, span] = gate
        ups[:, span] = up


def ffn_back_kernel(where, *refs):
    cots, normed, hidden, gates, ups = refs[:5]
    cot_rows, grad_gate, grad_up, out, keep_back, send_back, gain_term, held, sems = refs[-9:]
    count = sems.shape[0]
    rows, units = hidden.shape
    cols = cots.shape[2]
    half, wide = cols // 2, 2 * cols
    copies = fetch(refs[5 : 5 + count], held, sems)
    for block in range(4):
        for part in range(2):
            start = (part * 4 + block) * half
            cot_rows[:, start : start + half] = cots[block, :, part * half : (part + 1) * half]
    for copy in copies[: count // 2]:
        copy.wait()
    step = 256
    for n in range(0, units, step):
        span = slice(n, n + step)
        grad_hidden = 0.0
        for h in range(2):
            grad_hidden = grad_hidden + dot(
                cot_rows[:, half_columns(where, h, wide)], held[h * wide : (h + 1) * wide, span], 1, 0
            )
        gate, up = gates[:, span], ups[:, span]
        sigmoid = jax.nn.sigmoid(gate)
        grad_gate[:, span] = (
            grad_hidden * up * sigmoid * (1.0 + gate * (1.0 - sigmoid))
        ).astype(BF16)
        grad_up[:, span] = (grad_hidden * (gate * sigmoid)).astype(BF16)
    for copy in copies[count // 2 :]:
        copy.wait()
    row_term = 0.0
    for k in range(4):
        block = block_of(where, k)
        back = (keep_back, send_back)[k % 2]
        for h in range(2):
            part = aligned((h ^ where[1]) * half, half)
            of_down, of_gate, of_up = [
                held[aligned((n + h) * wide + block * half, half), :] for n in (0, 2, 4)
            ]
            out[block, :, part] = dot(hidden[...], of_down, 1, 1).astype(BF16)
            partial = dot(grad_gate[...], of_gate, 1, 1) + dot(grad_up[...], of_up, 1, 1)
            back[k // 2, :rows, part] = partial.astype(BF16)
            columns = aligned(((h ^ where[1]) * 4 + block) * half, half)
            terms = partial * normed[:, columns].astype(F32)
            gain_term[:, columns] = jnp.sum(terms, axis=0, keepdims=True)
            row_term = row_term + jnp.sum(terms, axis=1, keepdims=True)
    put_row_term(row_term, cols, keep_back, send_back)


def put_row_term(row_term, cols, keep, send):
    rows = row_term.shape[0]
    line = jnp.broadcast_to(row_term, (rows, 128)).T[:EXTRA]
    line = jnp.concatenate([line, jnp.zeros((EXTRA, cols - rows), F32)], axis=1).astype(BF16)
    for ref in (keep, send):
        ref[0, rows:] = line
        ref[1, rows:] = line


def qkv_back_kernel(where, normed, mine, other, w_first, w_second, keep, send, gain_term):
    rows, cols = normed.shape[0], keep.shape[2]
    half = cols // 2
    features = 3 * HDIM
    row_term = 0.0
    for k in range(4):
        block = block_of(where, k)
        back = (keep, send)[k % 2]
        for h, weights in enumerate((w_first, w_second)):
            part = aligned((h ^ where[1]) * half, half)
            partial = 0.0
            for grads, head in ((mine, where[2]), (other, 1 - where[2])):
                span = aligned(head * features, features)
                partial = partial + dot(grads[0], weights[block, span, :], 0, 0)
            back[k // 2, :rows, part] = partial.astype(BF16)
            columns = aligned(((h ^ where[1]) * 4 + block) * half, half)
            terms = partial * normed[:, columns].astype(F32)
            gain_term[:, columns] = jnp.sum(terms, axis=0, keepdims=True)
            row_term = row_term + jnp.sum(terms, axis=1, keepdims=True)
    put_row_term(row_term, cols, keep, send)


def qkv_weights_kernel(where, normed, *refs):
    own, other, outs = refs[0], refs[1], refs[2:]
    count = other.shape[0]
    half = outs[0].shape[2]
    rows, features = own.shape[2], 3 * HDIM
    for h, out in enumerate(outs):
        for z in range(4):
            columns = aligned(((h ^ where[1]) * 4 + z) * half, half)
            for grads, head in ((own, where[2]), (other, 1 - where[2])):
                total = 0.0
                for s in range(count):
                    total = total + dot(
                        grads[s], normed[s * rows : (s + 1) * rows, columns], 1, 0
                    )
                out[z, aligned(head * features, features), :] = total.astype(BF16)


def project_kernel(where, attended, weights, keep, send):
    half = weights.shape[2]
    for k in range(4):
        for part in range(2):
            (keep, send)[k % 2][k // 2, :, part * half : (part + 1) * half] = dot(
                attended[...], weights[block_of(where, k) * 2 + part], 0, 0
            ).astype(BF16)


def project_back_kernel(where, p0, p1, p2, p3, attended, weights, grad_att, grad_weights):
    half = weights.shape[2]
    total = 0.0
    for k, piece in enumerate((p0, p1, p2, p3)):
        for part in range(2):
            b = block_of(where, k) * 2 + part
            values = piece[:, part * half : (part + 1) * half]
            total = total + dot(weights[b], values, 1, 1)
            grad_weights[b] = dot(attended[...], values, 1, 0).astype(BF16)
    grad_att[...] = total.astype(BF16)


def columns_kernel(where, parts, out):
    for z in range(parts.shape[0]):
        out[:, z * parts.shape[2] : (z + 1) * parts.shape[2]] = parts[z].astype(F32)


def turned_kernel(where, parts, out):
    size = parts.shape[2]
    for z in range(parts.shape[0]):
        out[z * size : (z + 1) * size, :] = parts[z].astype(F32).T


def qkv_out_kernel(where, parts, *outs):
    features = 3 * HDIM
    for z in range(parts.shape[0]):
        for n, out in enumerate(outs):
            heads = [parts[z, h * features + n * HDIM : h * features + (n + 1) * HDIM] for h in (0, 1)]
            both = jnp.concatenate(heads, axis=0).astype(F32)
            out[:, z * 2 * HDIM : (z + 1) * 2 * HDIM] = both.T


def small_call(kernel, name, time, where, inputs, out_shapes, specs=None):
    specs = specs or {}
    return pl.pallas_call(
        kernel,
        grid_spec=pltpu.PrefetchScalarGridSpec(
            num_scalar_prefetch=1,
            grid=(1,),
            in_specs=[specs.get(n) or full(a.shape) for n, a in enumerate(inputs)],
            out_specs=[full(s.shape) for s in out_shapes],
        ),
        out_shape=list(out_shapes),
        compiler_params=params(),
        cost_estimate=cost(time),
        name=name,
    )(where, *inputs)


def on_device(
    sizes,
    hidden_in,
    gain_attn,
    w_query,
    w_key,
    w_value,
    w_out,
    gain_ffn,
    w_gate,
    w_up,
    w_down,
    cotangent,
    segment_ids,
    parents,
):
    nz, nq, ny, nx, nc = sizes
    rows, cols = hidden_in.shape
    groups = nq * ny
    group_rows = nz * rows
    width = cols * nx * nc
    half = cols // 2
    slab = gain_attn.shape[0]
    head = 3 * HDIM
    units = w_gate.shape[1] // nz

    zi, qi, yi, xi, ci = [lax.axis_index(a) for a in ("z", "q", "y", "x", "c")]
    group = qi * ny + yi
    own_columns = xi * nc + ci
    zs = [(zi - s) % nz for s in range(nz)]
    flip = yi if nq == 1 else 0 * yi
    where = [jnp.stack([own_columns, flip, yi, z]).astype(jnp.int32) for z in zs]

    def scatter_narrow(keep, send):
        held = keep.astype(F32) + swap(send, "c").astype(F32)
        return held[0] + swap(held[1].astype(BF16), "x").astype(F32)

    def first_sum(keep, received):
        held = keep.astype(F32) + received.astype(F32)
        return held[0], held[1].astype(BF16)

    def spread_z(parts):
        return lax.all_to_all(parts, "z", split_axis=0, concat_axis=0, tiled=True)

    def gather_rows(parts):
        n = parts.shape[2]
        if nq == 1:
            return parts.reshape(-1, n), swap(parts, "y").reshape(-1, n)
        got = lax.all_gather(parts, GROUP, axis=0, tiled=False)
        got = got.reshape(2, groups // 2, nz, slab, n).transpose(0, 2, 1, 3, 4)
        return tuple(got.reshape(2, nz * half, n))

    def swap_part(parts, n):
        part = parts[n * nz // 2 : (n + 1) * nz // 2]
        return swap(part, "y") if nq == 1 else part

    def join_rows(parts, swapped):
        if nq > 1:
            return gather_rows(parts)
        return [a.reshape(-1, units) for a in (parts, *swapped)]

    def gather_lanes(parts):
        n = parts.shape[1]
        if nq == 1:
            return parts, swap(parts, "y")
        got = lax.all_gather(parts, GROUP, axis=0, tiled=False)
        got = got.reshape(2, groups // 2, nz, n, slab).transpose(0, 2, 3, 1, 4)
        return tuple(got.reshape(2, nz, n, half))

    def exchange_rows(grad):
        if nq == 1:
            return swap(take(grad.reshape(2, -1, grad.shape[1]), 1 - yi), "y")
        n = grad.shape[1]
        parts = grad.reshape(2, nz, groups // 2, slab, n).transpose(0, 2, 1, 3, 4)
        return lax.psum_scatter(
            parts.reshape(groups, nz, slab, n), GROUP, scatter_dimension=0, tiled=False
        )

    def add_rows(grad, received):
        if nq == 1:
            own = take(grad.reshape(2, -1, grad.shape[1]), yi)
            received = (own.astype(F32) + received.astype(F32)).astype(BF16)
        return received.reshape(nz, slab, -1)

    def exchange_lanes(second):
        return swap(second, "y") if nq == 1 else second

    def scatter_lanes(first, second):
        n = first.shape[1]
        if nq == 1:
            return (first.astype(F32) + second.astype(F32)).astype(BF16)
        both = jnp.stack([first, second]).reshape(2, nz, n, groups // 2, slab)
        both = both.transpose(0, 3, 1, 2, 4).reshape(groups, nz, n, slab)
        return lax.psum_scatter(both, GROUP, scatter_dimension=0, tiled=False)

    def sum_small(values, axes):
        for axis in axes:
            if axis == "z":
                for bit in (1, 2):
                    values = values + lax.ppermute(values, "z", [(i, i ^ bit) for i in range(nz)])
            elif axis == "q":
                values = lax.psum(values, "q") if nq > 1 else values
            else:
                values = values + swap(values, axis)
        return values

    stacked = jnp.stack([w_query, w_key, w_value]).reshape(3, slab, nz, ny, HDIM)
    stacked = stacked.transpose(2, 3, 0, 4, 1).reshape(nz, ny * head, slab)
    both_gains = jnp.concatenate(
        [gain_attn[None], gain_ffn[None], jnp.zeros((EXTRA - 2, slab), BF16)], axis=0
    )
    both_gains = jnp.broadcast_to(both_gains[None], (nz, EXTRA, slab))
    stacked = jnp.concatenate([stacked, both_gains], axis=1)
    z1, x0, c0, stacked, segment_ids, parents = together(
        ring(hidden_in, nz),
        swap(hidden_in, "x"),
        swap(hidden_in, "c"),
        stacked,
        segment_ids,
        parents,
    )

    ancestor, starts, parent_len, ancestor_len = segment_tables(segment_ids, parents)
    q_blocks = [(z * nq + qi) * ny + (yi ^ dy) for dy in range(ny) for z in zs]
    k_blocks = [(z * nq + q) * ny + (yi ^ dy) for q in range(nq) for dy in range(ny) for z in zs]
    segments = segment_ids.reshape(-1, rows)
    k_seg = jnp.stack([take(segments, b) for b in k_blocks])
    k_pos = jnp.stack(k_blocks).astype(jnp.int32)
    q_tiles, k_tiles = len(q_blocks), len(k_blocks)
    of_queries = lambda a: lax.dynamic_slice_in_dim(a, qi * q_tiles, q_tiles, 0)
    flat = k_seg.reshape(-1)
    labels = jnp.arange(-(-parents.shape[0] // 16) * 16, dtype=jnp.int32)[None, :, None]
    places = k_pos[:, None] * rows + jnp.arange(rows, dtype=jnp.int32)[None]
    places = places + lookup(parent_len + ancestor_len - starts, flat).reshape(k_tiles, rows)
    k_own = labels == k_seg[:, None]
    q_seen = of_queries(
        k_own
        | (labels == lookup(parents, flat).reshape(k_tiles, 1, rows))
        | (labels == lookup(ancestor, flat).reshape(k_tiles, 1, rows))
    )
    q_mask = jnp.where(q_seen, 0.0, masked_fill).astype(BF16)
    k_mask = k_own.astype(BF16)
    q_pos = of_queries(k_pos)
    shown = jnp.any(jnp.any(q_seen, axis=2)[:, None] & jnp.any(k_own, axis=2)[None], axis=2)
    shown = shown & (k_pos[None, :] <= q_pos[:, None])
    number = jnp.arange(k_tiles, dtype=jnp.int32)
    earlier = number[None, None, :] < number[None, :, None]
    before = jnp.sum((shown[:, None, :] & earlier).astype(jnp.int32), axis=2)
    chosen = shown[:, None, :] & (before[:, None, :] == number[None, :, None])
    visible = jnp.sum(jnp.where(chosen, number[None, None, :], 0), axis=2, dtype=jnp.int32)
    slots = jnp.stack([z * ny + (yi ^ dy) for dy in range(ny) for z in zs]).astype(jnp.int32)
    q_info = jnp.concatenate([q_pos, slots, (qi * q_tiles).reshape(1).astype(jnp.int32)])
    tables = (
        visible.reshape(-1),
        jnp.sum(shown.astype(jnp.int32), axis=1, dtype=jnp.int32),
        q_info,
        k_pos,
    )
    frequency = rope_base ** (-2.0 * jnp.arange(HALF, dtype=F32) / HDIM)
    angles = places.astype(F32)[:, None, :] * frequency[None, :, None]
    cosine, sine = jnp.cos(angles), jnp.sin(angles)
    cos_q, sin_q = of_queries(cosine), of_queries(sine)

    z2, x1, c1, cx0, w_qkv, (tables, q_mask, k_mask, cosine, sine, cos_q, sin_q) = together(
        ring(z1, nz),
        swap(z1, "x"),
        swap(z1, "c"),
        swap(x0, "c"),
        spread_z(stacked),
        (tables, q_mask, k_mask, cosine, sine, cos_q, sin_q),
    )
    z3, x2, c2, cx1, w_qkv, w_gate_, cotangent_, w_out_ = together(
        ring(z2, nz),
        swap(z2, "x"),
        swap(z2, "c"),
        swap(x1, "c"),
        gather_lanes(w_qkv),
        w_gate,
        cotangent,
        w_out,
    )
    x3, c3, cx2 = swap(z3, "x"), swap(z3, "c"), swap(x2, "c")
    x_chunks = [
        (hidden_in, c0, x0, cx0),
        (z1, c1, x1, cx1),
        (z2, c2, x2, cx2),
        (z3, c3, x3, swap(x3, "c")),
    ]
    gains = [w[:, ny * head : ny * head + 2].astype(F32) for w in w_qkv]
    gains = jnp.stack([pick(flip, *gains), pick(flip, gains[1], gains[0])], axis=1)
    gains = gains.transpose(2, 0, 1, 3).reshape(2, width)
    gain1, gain2 = gains[:1], gains[1:]

    wo = lax.all_gather(w_out_, WIDE, axis=0, tiled=False)
    if nq > 1:
        wo = wo.reshape(nz * 2, groups // 2, -1, slab).transpose(0, 2, 1, 3)
        wo = wo.reshape(nz * 2, -1, half)
    of_units = lambda w: spread_z(w.reshape(slab, nz, units).transpose(1, 0, 2))
    cot = lax.all_gather(cotangent_, ("z", *NARROW), axis=0, tiled=False)

    buffers, mine, theirs, scale1 = None, [], [], []
    for s in range(nz):
        normed1, own, other, scale = chunk_call(
            qkv_kernel,
            "qkv",
            5,
            where[s],
            s,
            [(a, "whole") for a in (*x_chunks[s], gain1, *w_qkv, cos_q[s], sin_q[s])],
            buffers,
            [((group_rows, width), "chunk")],
            [shape((head, rows), BF16), shape((head, rows), BF16), shape((rows, 1), F32)],
        )
        buffers = [normed1]
        mine.append(own)
        theirs.append(swap(other, "y"))
        scale1.append(scale)
    tiles, gate_parts, w_up_, w_down_ = together(
        mine + theirs, of_units(w_gate_), w_up, w_down.T
    )
    if nq > 1:
        tiles = [lax.all_gather(jnp.stack(tiles), "q", axis=0, tiled=True)]
    (att_low, att, log_norm, peak), up_parts, w_gates, w_down_ = together(
        attend(tables, tiles, q_mask, k_mask), of_units(w_up_), gather_rows(gate_parts), w_down_
    )

    att_t = lax.all_to_all(att_low, ("z", "y"), split_axis=0, concat_axis=0, tiled=True)
    att_t, w_down_ = together(att_t, w_down_)
    att_t = att_t.reshape(nz * ny * HDIM, rows)
    keep, send = small_call(
        project_kernel,
        "project",
        4,
        where[0],
        (att_t, wo),
        [shape((2, rows, cols), BF16)] * 2,
    )
    residual_mid = hidden_in.astype(F32) + scatter_narrow(keep, send)
    down_parts = of_units(w_down_)
    mid_block = residual_mid.astype(BF16)

    def forward(s, pieces, buffers):
        results = chunk_call(
            ffn_kernel,
            "feed_forward",
            7,
            where[s],
            s,
            [(a, "whole") for a in (*pieces, gain2)] + [(w, "there") for w in (*w_gates, *w_ups)],
            buffers,
            [((group_rows, width), "chunk"), ((group_rows, units), "chunk")],
            [shape((rows, units), F32)] * 2 + [shape((rows, 1), F32)],
            held=True,
        )
        return results[:2], results[2:]

    def backward(s, normed2, hidden, kept, buffers):
        results = chunk_call(
            ffn_back_kernel,
            "feed_forward_back",
            10,
            where[s],
            s,
            [(cot, "place"), (normed2, "chunk"), (hidden, "chunk")]
            + [(a, "whole") for a in kept[:2]]
            + [(w, "there") for w in (*w_downs, *w_gates, *w_ups)],
            buffers,
            [
                ((group_rows, width), "chunk"),
                ((group_rows, units), "chunk"),
                ((group_rows, units), "chunk"),
                ((nz * nx * nc, rows, cols), "place"),
            ],
            [shape((2, rows + EXTRA, cols), BF16)] * 2 + [shape((1, width), F32)],
            held=True,
        )
        return results[:4], results[4:]

    z0 = mid_block
    z1, x0, c0, up_a = together(
        ring(z0, nz), swap(z0, "x"), swap(z0, "c"), swap_part(up_parts, 0)
    )
    z2, x1, c1, cx0, up_b, down_parts = together(
        ring(z1, nz),
        swap(z1, "x"),
        swap(z1, "c"),
        swap(x0, "c"),
        swap_part(up_parts, 1),
        down_parts,
    )
    w_ups = join_rows(up_parts, (up_a, up_b))
    z3, x2, c2, cx1, down_a, (saved, kept0) = together(
        ring(z2, nz),
        swap(z2, "x"),
        swap(z2, "c"),
        swap(x1, "c"),
        swap_part(down_parts, 0),
        forward(0, (z0, c0, x0, cx0), None),
    )
    x3, c3, cx2, down_b, (saved, kept1) = together(
        swap(z3, "x"),
        swap(z3, "c"),
        swap(x2, "c"),
        swap_part(down_parts, 1),
        forward(1, (z1, c1, x1, cx1), saved),
    )
    w_downs = join_rows(down_parts, (down_a, down_b))
    saved, kept2 = forward(2, (z2, c2, x2, cx2), saved)
    cx3, saved, kept2, (buffers, part1) = together(
        swap(x3, "c"), saved, kept2, backward(1, *saved, kept1, None)
    )
    saved, kept3 = forward(3, (z3, c3, x3, cx3), saved)
    got1, saved, kept3, (buffers, part2) = together(
        swap(part1[1], "c"), saved, kept3, backward(2, *saved, kept2, buffers)
    )
    normed2, hidden = saved
    own1, send1 = first_sum(part1[0], got1)
    own1, got1, got2, (buffers, part3) = together(
        own1,
        swap(send1, "x"),
        swap(part2[1], "c"),
        backward(3, *saved, kept3, buffers),
    )
    own2, send2 = first_sum(part2[0], got2)
    sum1 = (own1 + got1.astype(F32)).astype(BF16)
    carried, own2, got2, got3, (buffers, part0) = together(
        ring(sum1, nz),
        own2,
        swap(send2, "x"),
        swap(part3[1], "c"),
        backward(0, *saved, kept0, buffers),
    )
    cot_rows, grad_gate_lin, grad_up_lin, out_parts = buffers
    own3, send3 = first_sum(part3[0], got3)
    sum2 = (own2 + got2.astype(F32) + carried.astype(F32)).astype(BF16)
    carried, own3, got3, got0, down = together(
        ring(sum2, nz),
        own3,
        swap(send3, "x"),
        swap(part0[1], "c"),
        dot(cot_rows, hidden, 0, 0).astype(BF16),
    )
    own0, send0 = first_sum(part0[0], got0)
    sum3 = (own3 + got3.astype(F32) + carried.astype(F32)).astype(BF16)
    carried, own0, got0, gate, down_got, grad_up_lin = together(
        ring(sum3, nz),
        own0,
        swap(send0, "x"),
        dot(normed2, grad_gate_lin, 0, 0).astype(BF16),
        exchange_rows(down),
        grad_up_lin,
    )
    summed2 = own0 + got0.astype(F32) + carried.astype(F32)
    scale2 = kept0[2]
    terms2 = part0[2] + part1[2] + part2[2] + part3[2]

    def norm_back(summed, gain, block, rstd):
        gain = lax.dynamic_slice_in_dim(gain, own_columns * cols, cols, 1)
        mean = summed[rows, :rows].reshape(rows, 1) / width
        return rstd * (summed[:rows] * gain - block.astype(F32) * rstd * mean)

    grad_mid = cotangent.astype(F32) + norm_back(summed2, gain2, mid_block, scale2)
    branch = grad_mid.astype(BF16)
    branch_x = swap(branch, "x")
    branch_c, branch_cx = swap(branch, "c"), swap(branch_x, "c")
    branch_x, branch_c, branch_cx, gate_got, up, terms2 = together(
        branch_x,
        branch_c,
        branch_cx,
        exchange_rows(gate),
        dot(normed2, grad_up_lin, 0, 0).astype(BF16),
        terms2,
    )
    down = add_rows(down, down_got)
    gate = add_rows(gate, gate_got)
    pieces = (branch, branch_c, branch_x, branch_cx)

    grad_att, wo_back = small_call(
        project_back_kernel,
        "project_back",
        6,
        where[0],
        (*pieces, att_t, wo),
        [shape(att_t.shape, BF16), shape(wo.shape, BF16)],
    )
    grad_att = grad_att.reshape(nz * ny, HDIM, rows)
    grad_att, up, terms2, got2, down, gate = together(
        lax.all_to_all(grad_att, ("z", "y"), split_axis=0, concat_axis=0, tiled=True),
        up,
        terms2,
        swap(terms2, "c"),
        down,
        gate,
    )
    terms2 = terms2 + got2
    back, down, up_got, gate, terms2, got2 = together(
        attend_back(tables, tiles, q_mask, k_mask, grad_att, att, log_norm, cosine, sine),
        spread_z(down),
        exchange_rows(up),
        gate,
        terms2,
        swap(terms2, "x"),
    )
    up = add_rows(up, up_got)
    peak_slots = jnp.zeros((1, nz * groups), F32)
    peak_slots = lax.dynamic_update_slice(
        peak_slots, jnp.max(peak).reshape(1, 1), (0, zi * groups + group)
    )
    terms2 = sum_small(jnp.concatenate([terms2 + got2, peak_slots], axis=1), ("q",))
    if nq > 1:
        grad_q = of_queries(back)[:, :HDIM]
        grad_kv = lax.psum_scatter(back[:, HDIM:], "q", scatter_dimension=0, tiled=True)
        back = jnp.concatenate([grad_q, grad_kv], axis=1)
    def qkv_back(s, place):
        chunk = pl.BlockSpec((1, head, rows), lambda i, where: (s, 0, 0))
        specs = {0: pl.BlockSpec((rows, width), lambda i, where: (s, 0)), 1: chunk, 2: chunk}
        return small_call(
            qkv_back_kernel,
            "qkv_back",
            5,
            place,
            (normed1, back, other_back, *w_qkv),
            [shape((2, rows + EXTRA, cols), BF16)] * 2 + [shape((1, width), F32)],
            specs,
        )

    other_back, place, gate, got2 = together(
        swap(back[nz:], "y"), where[1], gate, swap(terms2, "y")
    )
    terms2 = terms2 + got2
    part1, place = together(qkv_back(1, place), where[2])
    got1, part2, gate, up, place, got2 = together(
        swap(part1[1], "c"),
        qkv_back(2, place),
        spread_z(gate),
        up,
        where[3],
        lax.ppermute(terms2, "z", [(i, i ^ 1) for i in range(nz)]),
    )
    terms2 = terms2 + got2
    own1, send1 = first_sum(part1[0], got1)
    own1, got1, got2, part3, qkv_grads, place, got_terms = together(
        own1,
        swap(send1, "x"),
        swap(part2[1], "c"),
        qkv_back(3, place),
        small_call(
            qkv_weights_kernel,
            "qkv_weights",
            8,
            place,
            (normed1, back, other_back),
            [shape((nz, ny * head, half), BF16)] * 2,
        ),
        where[0],
        lax.ppermute(terms2, "z", [(i, i ^ 2) for i in range(nz)]),
    )
    terms2 = terms2 + got_terms
    terms2, peaks = terms2[:, :width], terms2[0, width:]
    own2, send2 = first_sum(part2[0], got2)
    sum1 = (own1 + got1.astype(F32)).astype(BF16)
    carried, own2, got2, got3, part0, qkv_own, qkv_got, up = together(
        ring(sum1, nz),
        own2,
        swap(send2, "x"),
        swap(part3[1], "c"),
        qkv_back(0, place),
        qkv_grads[0],
        exchange_lanes(qkv_grads[1]),
        spread_z(up),
    )
    qkv_grads = spread_z(scatter_lanes(qkv_own, qkv_got))
    own3, send3 = first_sum(part3[0], got3)
    sum2 = (own2 + got2.astype(F32) + carried.astype(F32)).astype(BF16)
    terms1 = part0[2] + part1[2] + part2[2] + part3[2]
    terms1 = terms1 + swap(terms1, "c")
    carried, own3, got3, got0, terms1, terms1_x = together(
        ring(sum2, nz),
        own3,
        swap(send3, "x"),
        swap(part0[1], "c"),
        terms1,
        swap(terms1, "x"),
    )
    own0, send0 = first_sum(part0[0], got0)
    sum3 = (own3 + got3.astype(F32) + carried.astype(F32)).astype(BF16)
    terms1 = sum_small(terms1 + terms1_x, ("y", "q"))
    terms1_z = lax.ppermute(terms1, "z", [(i, i ^ 1) for i in range(nz)])
    carried, own0, got0, terms1, terms1_z = together(
        ring(sum3, nz), own0, swap(send0, "x"), terms1, terms1_z
    )
    terms1 = terms1 + terms1_z
    terms1 = terms1 + lax.ppermute(terms1, "z", [(i, i ^ 2) for i in range(nz)])
    summed1 = own0 + got0.astype(F32) + carried.astype(F32)
    grad_in = (grad_mid + norm_back(summed1, gain1, hidden_in, scale1[0])).astype(BF16)

    def laid_out(kernel, time, parts, *dims):
        return small_call(kernel, "lay_out", time, where[0], (parts,), [shape(d, F32) for d in dims])

    [grad_wd] = laid_out(turned_kernel, 3, down, (nz * units, slab))
    [grad_wg] = laid_out(columns_kernel, 2, gate, (slab, nz * units))
    [grad_wu] = laid_out(columns_kernel, 2, up, (slab, nz * units))
    branch_ffn = lax.psum_scatter(out_parts, ("z", *NARROW), scatter_dimension=0, tiled=False)
    hidden_out = (residual_mid + branch_ffn.astype(F32)).astype(BF16)
    if nq > 1:
        wo_back = wo_back.reshape(nz * 2, -1, groups // 2, slab).transpose(0, 2, 1, 3)
        wo_back = wo_back.reshape(nz * groups, -1, slab)
    grad_wo = lax.psum_scatter(wo_back, WIDE, scatter_dimension=0, tiled=False).astype(F32)
    grad_qkv = laid_out(qkv_out_kernel, 3, qkv_grads, *[(slab, nz * ny * HDIM)] * 3)

    gain_terms = jnp.concatenate([terms1, terms2], axis=0).reshape(2, 2, nz, half)
    gain_terms = gain_terms.transpose(0, 2, 1, 3).reshape(2, width) / gains
    terms = lax.dynamic_slice_in_dim(gain_terms, (zi * groups + group) * slab, slab, 1)
    peaks = peaks.reshape(nz, nq, ny)
    head_peaks = jnp.max(peaks, axis=1).reshape(nz * ny)
    factor = jnp.sqrt(clip_limit / jnp.maximum(head_peaks, clip_limit))
    column_factor = jnp.repeat(factor, HDIM)
    return (
        hidden_out,
        grad_in,
        grad_qkv[0],
        grad_qkv[1],
        grad_qkv[2],
        grad_wo,
        grad_wg,
        grad_wu,
        grad_wd,
        terms[0],
        terms[1],
        w_query.astype(F32) * column_factor[None, :],
        w_key.astype(F32) * column_factor[None, :],
        head_peaks,
    )


def solution(mesh):
    wide, narrow = mesh.devices.shape
    sizes = (4, wide // 8, 2, narrow // 2, 2)
    fine = Mesh(mesh.devices.reshape(sizes), ("z", "q", "y", "x", "c"))
    both = P(WIDE, NARROW)
    turned = P(NARROW, WIDE)
    return jax.shard_map(
        functools.partial(on_device, sizes),
        mesh=fine,
        in_specs=(
            both, P(WIDE), both, both, both, turned, P(WIDE), both, both, turned, both, P(), P()
        ),
        out_specs=(
            both, both, both, both, both, turned, both, both, turned,
            P(WIDE), P(WIDE), both, both, P(NARROW),
        ),
        check_vma=False,
    )
```

```python
import functools

import jax
import jax.numpy as jnp
from jax import lax
from jax.experimental import pallas as pl
from jax.experimental.pallas import tpu as pltpu
from jax.sharding import Mesh
from jax.sharding import PartitionSpec as P

HDIM = 64
HALF = HDIM // 2

eps_norm = 1e-05
rope_base = 130000.0
clip_limit = 5.0
masked_fill = -1e30

F32 = jnp.float32
BF16 = jnp.bfloat16
WIDE = ("z", "q", "y")
GROUP = ("q", "y")
NARROW = ("x", "c")
VMEM_BYTES = 60 * 2**20
EXTRA = 16


def lookup(lookup_table, indices):
    labels = jnp.arange(lookup_table.shape[0], dtype=jnp.int32)
    return jnp.sum(
        jnp.where(indices[:, None] == labels[None, :], lookup_table[None, :], 0),
        axis=1,
        dtype=jnp.int32,
    )


def segment_tables(segment_ids, parents):
    labels = jnp.arange(parents.shape[0], dtype=jnp.int32)
    counts = jnp.sum(
        (segment_ids[:, None] == labels[None, :]).astype(jnp.int32), axis=0, dtype=jnp.int32
    )
    starts = jnp.sum(
        jnp.where(labels[None, :] < labels[:, None], counts[None, :], 0), axis=1, dtype=jnp.int32
    )
    ancestor = lookup(parents, parents)
    parent_len = jnp.where(parents != labels, lookup(counts, parents), 0)
    ancestor_len = jnp.where(ancestor != parents, lookup(counts, ancestor), 0)
    return (ancestor, starts, parent_len, ancestor_len)


def dot(left, right, left_dim, right_dim):
    return lax.dot_general(
        left, right, (((left_dim,), (right_dim,)), ((), ())), preferred_element_type=F32
    )


def take(array, index, axis=0):
    return lax.dynamic_index_in_dim(array, index, axis, keepdims=False)


def swap(array, axis):
    return lax.ppermute(array, axis, [(0, 1), (1, 0)])


def ring(array, size):
    return lax.ppermute(array, "z", [(i, (i + 1) % size) for i in range(size)])


def pick(flag, first, second):
    return jnp.where(flag == 0, first, second)


def together(*values):
    return lax.optimization_barrier(values)


def params():
    return pltpu.CompilerParams(vmem_limit_bytes=VMEM_BYTES)


def cost(time):
    return pl.CostEstimate(flops=int(time * 1e9), bytes_accessed=1000, transcendentals=0)


def shape(dims, dtype):
    return jax.ShapeDtypeStruct(dims, dtype)


def full(dims):
    return pl.BlockSpec(dims, lambda *_: (0,) * len(dims))


def fill_tiles(sources, mask, held, k_ext, values_t):
    if len(sources) == 1:
        held[...] = sources[0][...]
    else:
        for t, source in enumerate(sources):
            held[t] = source[...]
    for t in range(held.shape[0]):
        tile = held[t].astype(F32)
        spare = k_ext.shape[2] - HDIM - mask.shape[1]
        parts = [tile[HDIM : 2 * HDIM], mask[t].astype(F32)]
        parts.append(jnp.zeros((spare, tile.shape[1]), F32))
        k_ext[t] = jnp.concatenate(parts, axis=0).T.astype(BF16)
        if values_t is not None:
            values_t[t] = jnp.concatenate(
                [tile[2 * HDIM :], jnp.zeros((HDIM, tile.shape[1]), F32)], axis=0
            ).T.astype(BF16)


def query_ext(q, mask, depth):
    spare = depth - HDIM - mask.shape[1]
    return jnp.concatenate([q, mask[0], jnp.zeros((spare, q.shape[1]), BF16)], axis=0)


def attend_kernel(visible, counts, q_pos, k_pos, *refs):
    q_mask, k_mask, low, out, log_norm, peak, held, k_ext = refs[-8:]
    i = pl.program_id(0)
    tiles, _, width = held.shape

    @pl.when(i == 0)
    def _():
        fill_tiles(refs[:-8], k_mask, held, k_ext, None)

    mine = q_pos[pl.num_programs(0) * 2]
    q_tile = query_ext(held[mine + i, :HDIM], q_mask, k_ext.shape[2])
    relative = lax.broadcasted_iota(jnp.int32, (width, width), 0) - lax.broadcasted_iota(
        jnp.int32, (width, width), 1
    )

    def step(n, carry):
        high, total, acc = carry
        j = visible[i * tiles + n]
        scores = dot(k_ext[j], q_tile, 1, 0)
        scores = jnp.where(relative <= (q_pos[i] - k_pos[j]) * width, scores, masked_fill)
        new_high = jnp.maximum(high, jnp.max(scores, axis=0, keepdims=True))
        weights = jnp.exp(scores - new_high)
        shrink = jnp.exp(high - new_high)
        total = total * shrink + jnp.sum(weights, axis=0, keepdims=True)
        acc = acc * shrink + dot(held[j, 2 * HDIM :], weights.astype(BF16), 1, 0)
        return new_high, total, acc

    high, total, acc = lax.fori_loop(
        0,
        counts[i],
        step,
        (
            jnp.full((1, width), masked_fill, F32),
            jnp.zeros((1, width), F32),
            jnp.zeros((HDIM, width), F32),
        ),
    )
    result = acc / total
    out[0] = result
    low[0] = result.astype(BF16)
    log_norm[0] = high + jnp.log(total)
    peak[0] = high


def attend(tables, tiles, q_mask, k_mask):
    q_tiles, labels, width = q_mask.shape
    k_tiles = k_mask.shape[0]
    part = lambda i, *_: (i, 0, 0)
    placed = lambda i, visible, counts, q_pos, k_pos: (q_pos[i + q_tiles], 0, 0)
    return pl.pallas_call(
        attend_kernel,
        grid_spec=pltpu.PrefetchScalarGridSpec(
            num_scalar_prefetch=4,
            grid=(q_tiles,),
            in_specs=[full(a.shape) for a in tiles]
            + [pl.BlockSpec((1, labels, width), part), full(k_mask.shape)],
            out_specs=[
                pl.BlockSpec((1, HDIM, width), placed),
                pl.BlockSpec((1, HDIM, width), part),
                pl.BlockSpec((1, 1, width), part),
                pl.BlockSpec((1, 1, width), part),
            ],
            scratch_shapes=[
                pltpu.VMEM((k_tiles, 3 * HDIM, width), BF16),
                pltpu.VMEM((k_tiles, width, 2 * HDIM), BF16),
            ],
        ),
        out_shape=[
            shape((q_tiles, HDIM, width), BF16),
            shape((q_tiles, HDIM, width), F32),
            shape((q_tiles, 1, width), F32),
            shape((q_tiles, 1, width), F32),
        ],
        compiler_params=params(),
        cost_estimate=cost(18),
        name="attend",
    )(*tables, *tiles, q_mask, k_mask)


def attend_back_kernel(visible, counts, q_pos, k_pos, *refs):
    q_mask, k_mask, grads, out, log_norm, cosine, sine, back = refs[-13:-5]
    held, k_ext, values_t, acc_k, acc_v = refs[-5:]
    i = pl.program_id(0)
    tiles, _, width = held.shape

    @pl.when(i == 0)
    def _():
        fill_tiles(refs[:-13], k_mask, held, k_ext, values_t)
        acc_k[...] = jnp.zeros_like(acc_k)
        acc_v[...] = jnp.zeros_like(acc_v)

    mine = q_pos[pl.num_programs(0) * 2]
    q_rows = held[mine + i, :HDIM]
    q_tile = query_ext(q_rows, q_mask, k_ext.shape[2])
    g_tile = grads[0]
    g_ext = jnp.concatenate([g_tile, jnp.zeros_like(g_tile)], axis=0)
    lse = log_norm[0]
    delta = jnp.sum(g_tile.astype(F32) * out[0], axis=0, keepdims=True)
    relative = lax.broadcasted_iota(jnp.int32, (width, width), 0) - lax.broadcasted_iota(
        jnp.int32, (width, width), 1
    )

    def step(n, acc):
        j = visible[i * tiles + n]
        scores = dot(k_ext[j], q_tile, 1, 0)
        scores = jnp.where(relative <= (q_pos[i] - k_pos[j]) * width, scores, masked_fill)
        probs = jnp.exp(scores - lse)
        grad_probs = dot(values_t[j], g_ext, 1, 0)
        grad_scores = (probs * (grad_probs - delta)).astype(BF16)
        acc_v[j] += dot(g_tile, probs.astype(BF16), 1, 1)
        acc_k[j] += dot(q_rows, grad_scores, 1, 1)
        return acc + dot(held[j, HDIM : 2 * HDIM], grad_scores, 1, 0)

    acc = lax.fori_loop(0, counts[i], step, jnp.zeros((HDIM, width), F32))

    def put_unrotated(grad, t, base):
        first, second, c, s = grad[:HALF], grad[HALF:], cosine[t], sine[t]
        back[t, base : base + HALF] = (first * c + second * s).astype(BF16)
        back[t, base + HALF : base + HDIM] = (second * c - first * s).astype(BF16)

    put_unrotated(acc * HDIM ** (-0.5), mine + i, 0)

    @pl.when(i == pl.num_programs(0) - 1)
    def _():
        for t in range(tiles):
            put_unrotated(acc_k[t], t, HDIM)
            back[t, 2 * HDIM :] = acc_v[t].astype(BF16)


def attend_back(tables, tiles, q_mask, k_mask, grads, out, log_norm, cosine, sine):
    q_tiles, labels, width = q_mask.shape
    k_tiles = k_mask.shape[0]
    part = lambda i, *_: (i, 0, 0)
    placed = lambda i, visible, counts, q_pos, k_pos: (q_pos[i + q_tiles], 0, 0)
    return pl.pallas_call(
        attend_back_kernel,
        grid_spec=pltpu.PrefetchScalarGridSpec(
            num_scalar_prefetch=4,
            grid=(q_tiles,),
            in_specs=[full(a.shape) for a in tiles]
            + [
                pl.BlockSpec((1, labels, width), part),
                full(k_mask.shape),
                pl.BlockSpec((1, HDIM, width), placed),
                pl.BlockSpec((1, HDIM, width), part),
                pl.BlockSpec((1, 1, width), part),
                full(cosine.shape),
                full(sine.shape),
            ],
            out_specs=full((k_tiles, 3 * HDIM, width)),
            scratch_shapes=[
                pltpu.VMEM((k_tiles, 3 * HDIM, width), BF16),
                pltpu.VMEM((k_tiles, width, 2 * HDIM), BF16),
                pltpu.VMEM((k_tiles, width, 2 * HDIM), BF16),
                pltpu.VMEM((k_tiles, HDIM, width), F32),
                pltpu.VMEM((k_tiles, HDIM, width), F32),
            ],
        ),
        out_shape=shape((k_tiles, 3 * HDIM, width), BF16),
        compiler_params=params(),
        cost_estimate=cost(22),
        name="attend_back",
    )(*tables, *tiles, q_mask, k_mask, grads, out, log_norm, cosine, sine)


def row_scale(pieces, width):
    squares = 0.0
    for piece in pieces:
        values = piece[...].astype(F32)
        squares = squares + jnp.sum(values * values, axis=1, keepdims=True)
    return lax.rsqrt(squares / width + eps_norm)


def aligned(start, size):
    return pl.ds(pl.multiple_of(start, size), size)


def block_of(where, k):
    return where[0] ^ k


def half_columns(where, h, wide):
    return aligned((h ^ where[1]) * wide, wide)


def put_normed(where, pieces, rstd, gain, normed):
    cols = pieces[0].shape[1]
    half = cols // 2
    for k, piece in enumerate(pieces):
        block = block_of(where, k)
        values = piece[...].astype(F32) * rstd * gain[:, aligned(block * cols, cols)]
        for part in range(2):
            columns = aligned((part * 4 + block) * half, half)
            normed[:, columns] = values[:, part * half : (part + 1) * half].astype(BF16)


def qkv_kernel(where, *refs):
    pieces, (gain, w_first, w_second, cosine, sine) = refs[:4], refs[4:9]
    normed, mine, other, scale = refs[-4:]
    rows, cols = pieces[0].shape
    half = cols // 2
    rstd = row_scale(pieces, 4 * cols)
    scale[...] = rstd
    put_normed(where, pieces, rstd, gain, normed)
    c, s = cosine[...], sine[...]
    features = 3 * HDIM
    for out, head in ((mine, where[2]), (other, 1 - where[2])):
        span = aligned(head * features, features)
        lin = 0.0
        for h, weights in enumerate((w_first, w_second)):
            for z in range(4):
                columns = aligned(((h ^ where[1]) * 4 + z) * half, half)
                lin = lin + dot(weights[z, span, :], normed[:, columns], 1, 1)
        for part, factor in ((0, HDIM ** (-0.5)), (1, 1.0)):
            base = part * HDIM
            first, second = lin[base : base + HALF], lin[base + HALF : base + HDIM]
            out[base : base + HALF] = ((first * c - second * s) * factor).astype(BF16)
            out[base + HALF : base + HDIM] = ((second * c + first * s) * factor).astype(BF16)
        out[2 * HDIM :] = lin[2 * HDIM :].astype(BF16)


def chunk_call(
    kernel, name, time, where, s, inputs, buffers, whole_shapes, out_shapes, scratch=(), out_there=0
):
    def spec(dims, how):
        rest = (0,) * (len(dims) - 1)
        if how == "whole":
            return full(dims)
        if how == "there":
            return pl.BlockSpec(memory_space=pl.ANY)
        block = (dims[0] // 4, *dims[1:])
        if how == "chunk":
            return pl.BlockSpec(block, lambda i, where: (s, *rest))
        return pl.BlockSpec(block, lambda i, where: (where[3], *rest))

    in_specs = [spec(a.shape, how) for a, how in inputs]
    arrays = [a for a, _ in inputs]
    aliases = {}
    if buffers is not None:
        for n, buffer in enumerate(buffers):
            aliases[1 + len(arrays)] = n
            in_specs.append(pl.BlockSpec(memory_space=pl.ANY))
            arrays.append(buffer)
    out_specs = [spec(dims, how) for dims, how in whole_shapes]
    out_specs += [
        pl.BlockSpec(memory_space=pl.ANY) if n < out_there else full(a.shape)
        for n, a in enumerate(out_shapes)
    ]
    return pl.pallas_call(
        kernel,
        grid_spec=pltpu.PrefetchScalarGridSpec(
            num_scalar_prefetch=1,
            grid=(1,),
            in_specs=in_specs,
            out_specs=out_specs,
            scratch_shapes=list(scratch),
        ),
        out_shape=[shape(dims, BF16) for dims, _ in whole_shapes] + list(out_shapes),
        input_output_aliases=aliases,
        compiler_params=params(),
        cost_estimate=cost(time),
        name=name,
    )(where, *arrays)


def fetch(weights, held, sems, first=0, start=0):
    copies = []
    for n, weight in enumerate(weights):
        rows = weight.shape[0]
        copies.append(
            pltpu.make_async_copy(weight, held.at[pl.ds(start, rows)], sems.at[first + n])
        )
        copies[-1].start()
        start += rows
    return copies


class Sends:
    def __init__(self, sems):
        self.sems, self.copies = sems, []

    def start(self, source, target):
        self.copies.append(pltpu.make_async_copy(source, target, self.sems.at[len(self.copies)]))
        self.copies[-1].start()

    def wait(self):
        for copy in self.copies:
            copy.wait()


def load(pairs, sems, first):
    copies = [
        pltpu.make_async_copy(source, target, sems.at[first + n])
        for n, (source, target) in enumerate(pairs)
    ]
    for copy in copies:
        copy.start()
    return copies


def wait_all(copies):
    for copy in copies:
        copy.wait()


def ffn_kernel(chunks, count, where, *refs):
    pieces, gain, weights = refs[:8], refs[8], refs[9 : 9 + count]
    outs = refs[-16:-8]
    mids, normed_all, hidden_all, gates_all, ups_all, held, sems, out_sems = refs[-8:]
    normed_out, hidden_out, scales = outs[0], outs[1], outs[6:]
    rows, cols = mids.shape[2:]
    units, wide = hidden_all.shape[2], 2 * cols
    come = [
        load([(pieces[4 * i + k], mids.at[i, k]) for k in range(4)], sems, count + 4 * i)
        for i in range(2)
    ]
    copies = fetch(weights, held, sems)
    sends = Sends(out_sems)
    step = 256
    for i in range(2):
        chunk = pl.ds(chunks[i] * rows, rows)
        normed, hidden = normed_all.at[i], hidden_all.at[i]
        gates, ups = gates_all.at[i], ups_all.at[i]
        gates_out, ups_out = outs[2 + 2 * i], outs[3 + 2 * i]
        wait_all(come[i])
        blocks = [mids.at[i, k] for k in range(4)]
        rstd = row_scale(blocks, 4 * cols)
        scales[i][...] = rstd
        put_normed(where, blocks, rstd, gain, normed)
        sends.start(normed, normed_out.at[chunk])
        if i == 0:
            wait_all(copies)
        for n in range(0, units, step):
            span = slice(n, n + step)
            columns = pl.ds(n, step)
            gate = up = 0.0
            for h in range(2):
                values = normed[:, half_columns(where, h, wide)]
                gate = gate + dot(values, held[h * wide : (h + 1) * wide, span], 1, 0)
                up = up + dot(values, held[(h + 2) * wide : (h + 3) * wide, span], 1, 0)
            gates[:, span] = gate
            ups[:, span] = up
            sends.start(gates.at[:, columns], gates_out.at[:, columns])
            sends.start(ups.at[:, columns], ups_out.at[:, columns])
            hidden[:, span] = (gate * jax.nn.sigmoid(gate) * up).astype(BF16)
            sends.start(hidden.at[:, columns], hidden_out.at[chunk, columns])
    sends.wait()


def arrange_kernel(zs, cots, cot_rows):
    cols = cots.shape[2]
    half = cols // 2
    for block in range(4):
        for part in range(2):
            start = (part * 4 + block) * half
            cot_rows[:, start : start + half] = cots[block, :, part * half : (part + 1) * half]


def arrange(cot, zs):
    blocks, rows, cols = cot.shape
    return pl.pallas_call(
        arrange_kernel,
        grid_spec=pltpu.PrefetchScalarGridSpec(
            num_scalar_prefetch=1,
            grid=(4,),
            in_specs=[pl.BlockSpec((blocks // 4, rows, cols), lambda s, zs: (zs[s], 0, 0))],
            out_specs=pl.BlockSpec((rows, 4 * cols), lambda s, zs: (s, 0)),
        ),
        out_shape=shape((4 * rows, 4 * cols), BF16),
        compiler_params=params(),
        cost_estimate=cost(5),
        name="arrange",
    )(zs, cot)


def ffn_back_kernel(chunks, downs, count, where, *refs):
    weights, kept = refs[:count], refs[count : count + 4]
    all_cot, all_hidden, all_normed = refs[count + 4 : count + 7]
    grad_gate_out, grad_up_out, out = refs[-21:-18]
    backs, gain_term = refs[-18:-14], refs[-14]
    held, cot_all, gate_up, hidden_in, normed_in, sems = refs[-13:-7]
    grad_gates, grad_ups, out_held, back_held, lines, out_sems, line_sems = refs[-7:]
    rows, units = grad_gates.shape[1:]
    cols = out_held.shape[3]
    half, wide = cols // 2, 2 * cols
    step = 256
    spans = [pl.ds(s * rows, rows) for s in chunks]
    early = load([(all_cot.at[spans[0]], cot_all.at[0])], sems, count)
    early += fetch(weights[:downs], held, sems)
    early += load([(kept[0], gate_up.at[0, 0]), (kept[1], gate_up.at[0, 1])], sems, count + 1)
    late = load(
        [(all_hidden.at[spans[0]], hidden_in.at[0]), (all_normed.at[spans[0]], normed_in.at[0])],
        sems,
        count + 3,
    )
    late += fetch(weights[downs:], held, sems, downs, 2 * wide)
    second = load(
        [
            (all_cot.at[spans[1]], cot_all.at[1]),
            (kept[2], gate_up.at[1, 0]),
            (kept[3], gate_up.at[1, 1]),
            (all_hidden.at[spans[1]], hidden_in.at[1]),
            (all_normed.at[spans[1]], normed_in.at[1]),
        ],
        sems,
        count + 5,
    )
    sends, tails = Sends(out_sems), Sends(line_sems)
    for i in range(2):
        cot_rows, hidden, normed = cot_all.at[i], hidden_in.at[i], normed_in.at[i]
        gates, ups = gate_up.at[i, 0], gate_up.at[i, 1]
        grad_gate, grad_up = grad_gates.at[i], grad_ups.at[i]
        place = where[3 + i]
        wait_all(early if i == 0 else second)
        for n in range(0, units, step):
            span = slice(n, n + step)
            columns = pl.ds(n, step)
            grad_hidden = 0.0
            for h in range(2):
                grad_hidden = grad_hidden + dot(
                    cot_rows[:, half_columns(where, h, wide)],
                    held[h * wide : (h + 1) * wide, span],
                    1,
                    0,
                )
            gate, up = gates[:, span], ups[:, span]
            sigmoid = jax.nn.sigmoid(gate)
            grad_gate[:, span] = (
                grad_hidden * up * sigmoid * (1.0 + gate * (1.0 - sigmoid))
            ).astype(BF16)
            grad_up[:, span] = (grad_hidden * (gate * sigmoid)).astype(BF16)
            sends.start(grad_gate.at[:, columns], grad_gate_out.at[spans[i], columns])
            sends.start(grad_up.at[:, columns], grad_up_out.at[spans[i], columns])
        if i == 0:
            wait_all(late)
        row_term = 0.0
        for k in range(4):
            block = block_of(where, k)
            back = backs[2 * i + k % 2]
            for h in range(2):
                part = aligned((h ^ where[1]) * half, half)
                of_down, of_gate, of_up = [
                    held[aligned((n + h) * wide + block * half, half), :] for n in (0, 2, 4)
                ]
                out_held[i, k, :, part] = dot(hidden[...], of_down, 1, 1).astype(BF16)
                partial = dot(grad_gate[...], of_gate, 1, 1) + dot(grad_up[...], of_up, 1, 1)
                back_held[i, k, :, part] = partial.astype(BF16)
                columns = aligned(((h ^ where[1]) * 4 + block) * half, half)
                terms = partial * normed[:, columns].astype(F32)
                column_term = jnp.sum(terms, axis=0, keepdims=True)
                if i == 0:
                    gain_term[:, columns] = column_term
                else:
                    gain_term[:, columns] += column_term
                row_term = row_term + jnp.sum(terms, axis=1, keepdims=True)
            sends.start(out_held.at[i, k], out.at[place * 4 + block])
            sends.start(back_held.at[i, k], back.at[k // 2, pl.ds(0, rows)])
        lines[i] = row_line(row_term, cols)
        for back in backs[2 * i : 2 * i + 2]:
            for x in range(2):
                tails.start(lines.at[i], back.at[x, pl.ds(rows, EXTRA)])
    sends.wait()
    tails.wait()


def row_line(row_term, cols):
    rows = row_term.shape[0]
    line = jnp.broadcast_to(row_term, (rows, 128)).T[:EXTRA]
    return jnp.concatenate([line, jnp.zeros((EXTRA, cols - rows), F32)], axis=1).astype(BF16)


def put_row_term(row_term, cols, keep, send):
    rows = row_term.shape[0]
    line = row_line(row_term, cols)
    for ref in (keep, send):
        ref[0, rows:] = line
        ref[1, rows:] = line


def qkv_back_kernel(where, normed, mine, other, w_first, w_second, keep, send, gain_term):
    rows, cols = normed.shape[0], keep.shape[2]
    half = cols // 2
    features = 3 * HDIM
    row_term = 0.0
    for k in range(4):
        block = block_of(where, k)
        back = (keep, send)[k % 2]
        for h, weights in enumerate((w_first, w_second)):
            part = aligned((h ^ where[1]) * half, half)
            partial = 0.0
            for grads, head in ((mine, where[2]), (other, 1 - where[2])):
                span = aligned(head * features, features)
                partial = partial + dot(grads[0], weights[block, span, :], 0, 0)
            back[k // 2, :rows, part] = partial.astype(BF16)
            columns = aligned(((h ^ where[1]) * 4 + block) * half, half)
            terms = partial * normed[:, columns].astype(F32)
            gain_term[:, columns] = jnp.sum(terms, axis=0, keepdims=True)
            row_term = row_term + jnp.sum(terms, axis=1, keepdims=True)
    put_row_term(row_term, cols, keep, send)


def qkv_weights_kernel(where, normed, *refs):
    own, other, outs = refs[0], refs[1], refs[2:]
    count = other.shape[0]
    half = outs[0].shape[2]
    rows, features = own.shape[2], 3 * HDIM
    for h, out in enumerate(outs):
        for z in range(4):
            columns = aligned(((h ^ where[1]) * 4 + z) * half, half)
            for grads, head in ((own, where[2]), (other, 1 - where[2])):
                total = 0.0
                for s in range(count):
                    total = total + dot(
                        grads[s], normed[s * rows : (s + 1) * rows, columns], 1, 0
                    )
                out[z, aligned(head * features, features), :] = total.astype(BF16)


def project_kernel(where, attended, weights, keep, send):
    half = weights.shape[2]
    for k in range(4):
        for part in range(2):
            (keep, send)[k % 2][k // 2, :, part * half : (part + 1) * half] = dot(
                attended[...], weights[block_of(where, k) * 2 + part], 0, 0
            ).astype(BF16)


def project_back_kernel(where, p0, p1, p2, p3, attended, weights, grad_att, grad_weights):
    half = weights.shape[2]
    total = 0.0
    for k, piece in enumerate((p0, p1, p2, p3)):
        for part in range(2):
            b = block_of(where, k) * 2 + part
            values = piece[:, part * half : (part + 1) * half]
            total = total + dot(weights[b], values, 1, 1)
            grad_weights[b] = dot(attended[...], values, 1, 0).astype(BF16)
    grad_att[...] = total.astype(BF16)


def columns_kernel(parts, out):
    out[...] = parts[0].astype(F32)


def turned_kernel(parts, out):
    out[...] = parts[0].astype(F32).T


def lay_out(parts, turned):
    nz, n, m = parts.shape
    if turned:
        kernel, dims, block, place = turned_kernel, (nz * m, n), (m, n), lambda z: (z, 0)
    else:
        kernel, dims, block, place = columns_kernel, (n, nz * m), (n, m), lambda z: (0, z)
    return pl.pallas_call(
        kernel,
        grid=(nz,),
        in_specs=[pl.BlockSpec((1, n, m), lambda z: (z, 0, 0))],
        out_specs=pl.BlockSpec(block, place),
        out_shape=shape(dims, F32),
        compiler_params=params(),
        cost_estimate=cost(2),
        name="lay_out",
    )(parts)


def qkv_out_kernel(where, parts, *outs):
    features = 3 * HDIM
    for z in range(parts.shape[0]):
        for n, out in enumerate(outs):
            heads = [parts[z, h * features + n * HDIM : h * features + (n + 1) * HDIM] for h in (0, 1)]
            both = jnp.concatenate(heads, axis=0).astype(F32)
            out[:, z * 2 * HDIM : (z + 1) * 2 * HDIM] = both.T


def small_call(kernel, name, time, where, inputs, out_shapes, specs=None):
    specs = specs or {}
    return pl.pallas_call(
        kernel,
        grid_spec=pltpu.PrefetchScalarGridSpec(
            num_scalar_prefetch=1,
            grid=(1,),
            in_specs=[specs.get(n) or full(a.shape) for n, a in enumerate(inputs)],
            out_specs=[full(s.shape) for s in out_shapes],
        ),
        out_shape=list(out_shapes),
        compiler_params=params(),
        cost_estimate=cost(time),
        name=name,
    )(where, *inputs)


def on_device(
    sizes,
    hidden_in,
    gain_attn,
    w_query,
    w_key,
    w_value,
    w_out,
    gain_ffn,
    w_gate,
    w_up,
    w_down,
    cotangent,
    segment_ids,
    parents,
):
    nz, nq, ny, nx, nc = sizes
    rows, cols = hidden_in.shape
    groups = nq * ny
    group_rows = nz * rows
    width = cols * nx * nc
    half = cols // 2
    slab = gain_attn.shape[0]
    head = 3 * HDIM
    units = w_gate.shape[1] // nz

    zi, qi, yi, xi, ci = [lax.axis_index(a) for a in ("z", "q", "y", "x", "c")]
    group = qi * ny + yi
    own_columns = xi * nc + ci
    zs = [(zi - s) % nz for s in range(nz)]
    flip = yi if nq == 1 else 0 * yi
    where = [jnp.stack([own_columns, flip, yi, z]).astype(jnp.int32) for z in zs]

    def scatter_narrow(keep, send):
        held = keep.astype(F32) + swap(send, "c").astype(F32)
        return held[0] + swap(held[1].astype(BF16), "x").astype(F32)

    def first_sum(keep, received):
        held = keep.astype(F32) + received.astype(F32)
        return held[0], held[1].astype(BF16)

    def spread_z(parts):
        return lax.all_to_all(parts, "z", split_axis=0, concat_axis=0, tiled=True)

    def gather_rows(parts):
        n = parts.shape[2]
        if nq == 1:
            return parts.reshape(-1, n), swap(parts, "y").reshape(-1, n)
        got = lax.all_gather(parts, GROUP, axis=0, tiled=False)
        got = got.reshape(2, groups // 2, nz, slab, n).transpose(0, 2, 1, 3, 4)
        return tuple(got.reshape(2, nz * half, n))

    def swap_part(parts, n):
        part = parts[n * nz // 2 : (n + 1) * nz // 2]
        return swap(part, "y") if nq == 1 else part

    def join_rows(parts, swapped):
        if nq > 1:
            return gather_rows(parts)
        return [a.reshape(-1, units) for a in (parts, *swapped)]

    def gather_lanes(parts):
        n = parts.shape[1]
        if nq == 1:
            return parts, swap(parts, "y")
        got = lax.all_gather(parts, GROUP, axis=0, tiled=False)
        got = got.reshape(2, groups // 2, nz, n, slab).transpose(0, 2, 3, 1, 4)
        return tuple(got.reshape(2, nz, n, half))

    def exchange_rows(grad):
        if nq == 1:
            return swap(take(grad.reshape(2, -1, grad.shape[1]), 1 - yi), "y")
        n = grad.shape[1]
        parts = grad.reshape(2, nz, groups // 2, slab, n).transpose(0, 2, 1, 3, 4)
        return lax.psum_scatter(
            parts.reshape(groups, nz, slab, n), GROUP, scatter_dimension=0, tiled=False
        )

    def add_rows(grad, received):
        if nq == 1:
            own = take(grad.reshape(2, -1, grad.shape[1]), yi)
            received = (own.astype(F32) + received.astype(F32)).astype(BF16)
        return received.reshape(nz, slab, -1)

    def exchange_lanes(second):
        return swap(second, "y") if nq == 1 else second

    def scatter_lanes(first, second):
        n = first.shape[1]
        if nq == 1:
            return (first.astype(F32) + second.astype(F32)).astype(BF16)
        both = jnp.stack([first, second]).reshape(2, nz, n, groups // 2, slab)
        both = both.transpose(0, 3, 1, 2, 4).reshape(groups, nz, n, slab)
        return lax.psum_scatter(both, GROUP, scatter_dimension=0, tiled=False)

    def sum_small(values, axes):
        for axis in axes:
            if axis == "z":
                for bit in (1, 2):
                    values = values + lax.ppermute(values, "z", [(i, i ^ bit) for i in range(nz)])
            elif axis == "q":
                values = lax.psum(values, "q") if nq > 1 else values
            else:
                values = values + swap(values, axis)
        return values

    stacked = jnp.stack([w_query, w_key, w_value]).reshape(3, slab, nz, ny, HDIM)
    stacked = stacked.transpose(2, 3, 0, 4, 1).reshape(nz, ny * head, slab)
    both_gains = jnp.concatenate(
        [gain_attn[None], gain_ffn[None], jnp.zeros((EXTRA - 2, slab), BF16)], axis=0
    )
    both_gains = jnp.broadcast_to(both_gains[None], (nz, EXTRA, slab))
    stacked = jnp.concatenate([stacked, both_gains], axis=1)
    z1, x0, c0, stacked, segment_ids, parents = together(
        ring(hidden_in, nz),
        swap(hidden_in, "x"),
        swap(hidden_in, "c"),
        stacked,
        segment_ids,
        parents,
    )

    ancestor, starts, parent_len, ancestor_len = segment_tables(segment_ids, parents)
    q_blocks = [(z * nq + qi) * ny + (yi ^ dy) for dy in range(ny) for z in zs]
    k_blocks = [(z * nq + q) * ny + (yi ^ dy) for q in range(nq) for dy in range(ny) for z in zs]
    segments = segment_ids.reshape(-1, rows)
    k_seg = jnp.stack([take(segments, b) for b in k_blocks])
    k_pos = jnp.stack(k_blocks).astype(jnp.int32)
    q_tiles, k_tiles = len(q_blocks), len(k_blocks)
    of_queries = lambda a: lax.dynamic_slice_in_dim(a, qi * q_tiles, q_tiles, 0)
    flat = k_seg.reshape(-1)
    labels = jnp.arange(-(-parents.shape[0] // 16) * 16, dtype=jnp.int32)[None, :, None]
    places = k_pos[:, None] * rows + jnp.arange(rows, dtype=jnp.int32)[None]
    places = places + lookup(parent_len + ancestor_len - starts, flat).reshape(k_tiles, rows)
    k_own = labels == k_seg[:, None]
    q_seen = of_queries(
        k_own
        | (labels == lookup(parents, flat).reshape(k_tiles, 1, rows))
        | (labels == lookup(ancestor, flat).reshape(k_tiles, 1, rows))
    )
    q_mask = jnp.where(q_seen, 0.0, masked_fill).astype(BF16)
    k_mask = k_own.astype(BF16)
    q_pos = of_queries(k_pos)
    shown = jnp.any(jnp.any(q_seen, axis=2)[:, None] & jnp.any(k_own, axis=2)[None], axis=2)
    shown = shown & (k_pos[None, :] <= q_pos[:, None])
    number = jnp.arange(k_tiles, dtype=jnp.int32)
    earlier = number[None, None, :] < number[None, :, None]
    before = jnp.sum((shown[:, None, :] & earlier).astype(jnp.int32), axis=2)
    chosen = shown[:, None, :] & (before[:, None, :] == number[None, :, None])
    visible = jnp.sum(jnp.where(chosen, number[None, None, :], 0), axis=2, dtype=jnp.int32)
    slots = jnp.stack([z * ny + (yi ^ dy) for dy in range(ny) for z in zs]).astype(jnp.int32)
    q_info = jnp.concatenate([q_pos, slots, (qi * q_tiles).reshape(1).astype(jnp.int32)])
    tables = (
        visible.reshape(-1),
        jnp.sum(shown.astype(jnp.int32), axis=1, dtype=jnp.int32),
        q_info,
        k_pos,
    )
    frequency = rope_base ** (-2.0 * jnp.arange(HALF, dtype=F32) / HDIM)
    angles = places.astype(F32)[:, None, :] * frequency[None, :, None]
    cosine, sine = jnp.cos(angles), jnp.sin(angles)
    cos_q, sin_q = of_queries(cosine), of_queries(sine)

    z2, x1, c1, cx0, w_qkv, (tables, q_mask, k_mask, cosine, sine, cos_q, sin_q) = together(
        ring(z1, nz),
        swap(z1, "x"),
        swap(z1, "c"),
        swap(x0, "c"),
        spread_z(stacked),
        (tables, q_mask, k_mask, cosine, sine, cos_q, sin_q),
    )
    z3, x2, c2, cx1, w_qkv, w_gate_, cotangent_, w_out_ = together(
        ring(z2, nz),
        swap(z2, "x"),
        swap(z2, "c"),
        swap(x1, "c"),
        gather_lanes(w_qkv),
        w_gate,
        cotangent,
        w_out,
    )
    x3, c3, cx2 = swap(z3, "x"), swap(z3, "c"), swap(x2, "c")
    x_chunks = [
        (hidden_in, c0, x0, cx0),
        (z1, c1, x1, cx1),
        (z2, c2, x2, cx2),
        (z3, c3, x3, swap(x3, "c")),
    ]
    gains = [w[:, ny * head : ny * head + 2].astype(F32) for w in w_qkv]
    gains = jnp.stack([pick(flip, *gains), pick(flip, gains[1], gains[0])], axis=1)
    gains = gains.transpose(2, 0, 1, 3).reshape(2, width)
    gain1, gain2 = gains[:1], gains[1:]

    wo = lax.all_gather(w_out_, WIDE, axis=0, tiled=False)
    if nq > 1:
        wo = wo.reshape(nz * 2, groups // 2, -1, slab).transpose(0, 2, 1, 3)
        wo = wo.reshape(nz * 2, -1, half)
    of_units = lambda w: spread_z(w.reshape(slab, nz, units).transpose(1, 0, 2))
    cot = lax.all_gather(cotangent_, ("z", *NARROW), axis=0, tiled=False)

    buffers, mine, theirs, scale1 = None, [], [], []
    for s in range(nz):
        normed1, own, other, scale = chunk_call(
            qkv_kernel,
            "qkv",
            5,
            where[s],
            s,
            [(a, "whole") for a in (*x_chunks[s], gain1, *w_qkv, cos_q[s], sin_q[s])],
            buffers,
            [((group_rows, width), "chunk")],
            [shape((head, rows), BF16), shape((head, rows), BF16), shape((rows, 1), F32)],
        )
        buffers = [normed1]
        mine.append(own)
        theirs.append(swap(other, "y"))
        scale1.append(scale)
    tiles, gate_parts, w_up_, w_down_ = together(
        mine + theirs, of_units(w_gate_), w_up, w_down.T
    )
    if nq > 1:
        tiles = [lax.all_gather(jnp.stack(tiles), "q", axis=0, tiled=True)]
    (att_low, att, log_norm, peak), up_parts, w_gates, w_down_ = together(
        attend(tables, tiles, q_mask, k_mask), of_units(w_up_), gather_rows(gate_parts), w_down_
    )

    att_t = lax.all_to_all(att_low, ("z", "y"), split_axis=0, concat_axis=0, tiled=True)
    att_t, w_down_ = together(att_t, w_down_)
    att_t = att_t.reshape(nz * ny * HDIM, rows)
    keep, send = small_call(
        project_kernel,
        "project",
        4,
        where[0],
        (att_t, wo),
        [shape((2, rows, cols), BF16)] * 2,
    )
    residual_mid = hidden_in.astype(F32) + scatter_narrow(keep, send)
    down_parts = of_units(w_down_)
    mid_block = residual_mid.astype(BF16)

    def forward(chunks, pieces, buffers):
        results = chunk_call(
            functools.partial(ffn_kernel, chunks, len(w_gates) + len(w_ups)),
            "feed_forward",
            9,
            where[0],
            0,
            [(a, "there") for a in pieces]
            + [(gain2, "whole")]
            + [(w, "there") for w in (*w_gates, *w_ups)],
            buffers,
            [((group_rows, width), "there"), ((group_rows, units), "there")],
            [shape((rows, units), F32)] * 4 + [shape((rows, 1), F32)] * 2,
            [
                pltpu.VMEM((2, 4, rows, cols), BF16),
                pltpu.VMEM((2, rows, width), BF16),
                pltpu.VMEM((2, rows, units), BF16),
                pltpu.VMEM((2, rows, units), F32),
                pltpu.VMEM((2, rows, units), F32),
                pltpu.VMEM((8 * cols, units), BF16),
                pltpu.SemaphoreType.DMA((len(w_gates) + len(w_ups) + 8,)),
                pltpu.SemaphoreType.DMA((2 + 6 * units // 256,)),
            ],
            4,
        )
        return results[:2], results[2:]

    def backward(chunks, saved, kept, buffers):
        weights = (*w_downs, *w_gates, *w_ups)
        places = jnp.concatenate([where[0][:3], jnp.stack([zs[s] for s in chunks]).astype(jnp.int32)])
        results = chunk_call(
            functools.partial(ffn_back_kernel, chunks, len(w_downs), len(weights)),
            "feed_forward_back",
            15,
            places,
            0,
            [(a, "there") for a in (*weights, *kept, cot_rows, saved[1], saved[0])],
            buffers,
            [
                ((group_rows, units), "there"),
                ((group_rows, units), "there"),
                ((nz * nx * nc, rows, cols), "there"),
            ],
            [shape((2, rows + EXTRA, cols), BF16)] * 4 + [shape((1, width), F32)],
            [
                pltpu.VMEM((12 * cols, units), BF16),
                pltpu.VMEM((2, rows, width), BF16),
                pltpu.VMEM((2, 2, rows, units), F32),
                pltpu.VMEM((2, rows, units), BF16),
                pltpu.VMEM((2, rows, width), BF16),
                pltpu.SemaphoreType.DMA((len(weights) + 10,)),
                pltpu.VMEM((2, rows, units), BF16),
                pltpu.VMEM((2, rows, units), BF16),
                pltpu.VMEM((2, 4, rows, cols), BF16),
                pltpu.VMEM((2, 4, rows, cols), BF16),
                pltpu.VMEM((2, EXTRA, cols), BF16),
                pltpu.SemaphoreType.DMA((16 + 4 * units // 256,)),
                pltpu.SemaphoreType.DMA((8,)),
            ],
            4,
        )
        return results[:3], results[3:7], results[7]

    z0 = mid_block
    z1, x0, c0, up_a = together(
        ring(z0, nz), swap(z0, "x"), swap(z0, "c"), swap_part(up_parts, 0)
    )
    z2, x1, c1, cx0, up_b, down_parts = together(
        ring(z1, nz),
        swap(z1, "x"),
        swap(z1, "c"),
        swap(x0, "c"),
        swap_part(up_parts, 1),
        down_parts,
    )
    w_ups = join_rows(up_parts, (up_a, up_b))
    z3, x2, c2, cx1, down_a, cot_rows = together(
        ring(z2, nz),
        swap(z2, "x"),
        swap(z2, "c"),
        swap(x1, "c"),
        swap_part(down_parts, 0),
        arrange(cot, jnp.stack(zs).astype(jnp.int32)),
    )
    x3, c3, cx2, down_b, (saved, kept01) = together(
        swap(z3, "x"),
        swap(z3, "c"),
        swap(x2, "c"),
        swap_part(down_parts, 1),
        forward((0, 1), (z0, c0, x0, cx0, z1, c1, x1, cx1), None),
    )
    w_downs = join_rows(down_parts, (down_a, down_b))
    cx3 = swap(x3, "c")
    saved, kept23 = forward((2, 3), (z2, c2, x2, cx2, z3, c3, x3, cx3), saved)
    buffers, back12, terms12 = backward((1, 2), saved, (*kept01[2:4], *kept23[:2]), None)
    part1, part2 = back12[:2], back12[2:]
    got1, part1, part2 = together(swap(part1[1], "c"), part1, part2)
    normed2, hidden = saved
    own1, send1 = first_sum(part1[0], got1)
    own1, got1, got2, (buffers, back30, terms30) = together(
        own1,
        swap(send1, "x"),
        swap(part2[1], "c"),
        backward((3, 0), saved, (*kept23[2:4], *kept01[:2]), buffers),
    )
    part3, part0 = back30[:2], back30[2:]
    own2, send2 = first_sum(part2[0], got2)
    sum1 = (own1 + got1.astype(F32)).astype(BF16)
    carried, own2, got2, got3, down = together(
        ring(sum1, nz),
        own2,
        swap(send2, "x"),
        swap(part3[1], "c"),
        dot(cot_rows, hidden, 0, 0).astype(BF16),
    )
    grad_gate_lin, grad_up_lin, out_parts = buffers
    own3, send3 = first_sum(part3[0], got3)
    sum2 = (own2 + got2.astype(F32) + carried.astype(F32)).astype(BF16)
    carried, own3, got3, got0, down_got, gate, grad_up_lin = together(
        ring(sum2, nz),
        own3,
        swap(send3, "x"),
        swap(part0[1], "c"),
        exchange_rows(down),
        dot(normed2, grad_gate_lin, 0, 0).astype(BF16),
        grad_up_lin,
    )
    own0, send0 = first_sum(part0[0], got0)
    sum3 = (own3 + got3.astype(F32) + carried.astype(F32)).astype(BF16)
    down = add_rows(down, down_got)
    gate_got = exchange_rows(gate)
    carried, own0, got0, up = together(
        ring(sum3, nz),
        own0,
        swap(send0, "x"),
        dot(normed2, grad_up_lin, 0, 0).astype(BF16),
    )
    summed2 = own0 + got0.astype(F32) + carried.astype(F32)
    scale2 = kept01[4]
    terms2 = terms12 + terms30

    def norm_back(summed, gain, block, rstd):
        gain = lax.dynamic_slice_in_dim(gain, own_columns * cols, cols, 1)
        mean = summed[rows, :rows].reshape(rows, 1) / width
        return rstd * (summed[:rows] * gain - block.astype(F32) * rstd * mean)

    grad_mid = cotangent.astype(F32) + norm_back(summed2, gain2, mid_block, scale2)
    branch = grad_mid.astype(BF16)
    branch_x = swap(branch, "x")
    branch_c, branch_cx = swap(branch, "c"), swap(branch_x, "c")
    branch_x, branch_c, branch_cx, gate_got, up = together(
        branch_x, branch_c, branch_cx, gate_got, up
    )
    gate = add_rows(gate, gate_got)
    up_got = exchange_rows(up)
    pieces = (branch, branch_c, branch_x, branch_cx)

    grad_att, wo_back = small_call(
        project_back_kernel,
        "project_back",
        6,
        where[0],
        (*pieces, att_t, wo),
        [shape(att_t.shape, BF16), shape(wo.shape, BF16)],
    )
    grad_att = grad_att.reshape(nz * ny, HDIM, rows)
    grad_att, down = together(
        lax.all_to_all(grad_att, ("z", "y"), split_axis=0, concat_axis=0, tiled=True), down
    )
    back, down, up_got, gate = together(
        attend_back(tables, tiles, q_mask, k_mask, grad_att, att, log_norm, cosine, sine),
        spread_z(down),
        up_got,
        gate,
    )
    up = add_rows(up, up_got)
    if nq > 1:
        grad_q = of_queries(back)[:, :HDIM]
        grad_kv = lax.psum_scatter(back[:, HDIM:], "q", scatter_dimension=0, tiled=True)
        back = jnp.concatenate([grad_q, grad_kv], axis=1)
    def qkv_back(s, place):
        chunk = pl.BlockSpec((1, head, rows), lambda i, where: (s, 0, 0))
        specs = {0: pl.BlockSpec((rows, width), lambda i, where: (s, 0)), 1: chunk, 2: chunk}
        return small_call(
            qkv_back_kernel,
            "qkv_back",
            5,
            place,
            (normed1, back, other_back, *w_qkv),
            [shape((2, rows + EXTRA, cols), BF16)] * 2 + [shape((1, width), F32)],
            specs,
        )

    other_back, place = together(swap(back[nz:], "y"), where[1])
    part1, place = together(qkv_back(1, place), where[2])
    got1, part2, qkv_grads, gate, place = together(
        swap(part1[1], "c"),
        qkv_back(2, place),
        small_call(
            qkv_weights_kernel,
            "qkv_weights",
            8,
            place,
            (normed1, back, other_back),
            [shape((nz, ny * head, half), BF16)] * 2,
        ),
        spread_z(gate),
        where[3],
    )
    own1, send1 = first_sum(part1[0], got1)
    own1, got1, got2, part3, qkv_own, qkv_got, place = together(
        own1,
        swap(send1, "x"),
        swap(part2[1], "c"),
        qkv_back(3, place),
        qkv_grads[0],
        exchange_lanes(qkv_grads[1]),
        where[0],
    )
    own2, send2 = first_sum(part2[0], got2)
    sum1 = (own1 + got1.astype(F32)).astype(BF16)
    carried, own2, got2, got3, part0, qkv_grads, up = together(
        ring(sum1, nz),
        own2,
        swap(send2, "x"),
        swap(part3[1], "c"),
        qkv_back(0, place),
        scatter_lanes(qkv_own, qkv_got),
        spread_z(up),
    )
    qkv_grads = spread_z(qkv_grads)
    own3, send3 = first_sum(part3[0], got3)
    sum2 = (own2 + got2.astype(F32) + carried.astype(F32)).astype(BF16)
    terms1 = part0[2] + part1[2] + part2[2] + part3[2]
    terms1 = jnp.concatenate([terms1, terms2], axis=0)
    terms1 = terms1 + swap(terms1, "c")
    carried, own3, got3, got0, terms1, terms1_x = together(
        ring(sum2, nz),
        own3,
        swap(send3, "x"),
        swap(part0[1], "c"),
        terms1,
        swap(terms1, "x"),
    )
    own0, send0 = first_sum(part0[0], got0)
    sum3 = (own3 + got3.astype(F32) + carried.astype(F32)).astype(BF16)
    peak_slots = jnp.zeros((nz * groups, 2 * width // (nz * groups)), F32)
    peak_slots = lax.dynamic_update_slice(
        peak_slots, jnp.broadcast_to(jnp.max(peak), (1, peak_slots.shape[1])), (zi * groups + group, 0)
    )
    terms1 = jnp.stack([terms1 + terms1_x, peak_slots.reshape(2, width)])
    terms1 = sum_small(terms1, ("y", "q"))
    terms1_z = lax.ppermute(terms1, "z", [(i, i ^ 1) for i in range(nz)])
    carried, own0, got0, terms1, terms1_z = together(
        ring(sum3, nz), own0, swap(send0, "x"), terms1, terms1_z
    )
    terms1 = terms1 + terms1_z
    terms1 = terms1 + lax.ppermute(terms1, "z", [(i, i ^ 2) for i in range(nz)])
    summed1 = own0 + got0.astype(F32) + carried.astype(F32)
    grad_in = (grad_mid + norm_back(summed1, gain1, hidden_in, scale1[0])).astype(BF16)

    grad_wd = lay_out(down, True)
    grad_wg = lay_out(gate, False)
    grad_wu = lay_out(up, False)
    branch_ffn = lax.psum_scatter(out_parts, ("z", *NARROW), scatter_dimension=0, tiled=False)
    hidden_out = (residual_mid + branch_ffn.astype(F32)).astype(BF16)
    if nq > 1:
        wo_back = wo_back.reshape(nz * 2, -1, groups // 2, slab).transpose(0, 2, 1, 3)
        wo_back = wo_back.reshape(nz * groups, -1, slab)
    grad_wo = lax.psum_scatter(wo_back, WIDE, scatter_dimension=0, tiled=False).astype(F32)
    grad_qkv = small_call(
        qkv_out_kernel,
        "lay_out_qkv",
        3,
        where[0],
        (qkv_grads,),
        [shape((slab, nz * ny * HDIM), F32)] * 3,
    )

    peaks = terms1[1].reshape(nz * groups, -1)[:, 0]
    gain_terms = terms1[0].reshape(2, 2, nz, half)
    gain_terms = gain_terms.transpose(0, 2, 1, 3).reshape(2, width) / gains
    terms = lax.dynamic_slice_in_dim(gain_terms, (zi * groups + group) * slab, slab, 1)
    peaks = peaks.reshape(nz, nq, ny)
    head_peaks = jnp.max(peaks, axis=1).reshape(nz * ny)
    factor = jnp.sqrt(clip_limit / jnp.maximum(head_peaks, clip_limit))
    column_factor = jnp.repeat(factor, HDIM)
    return (
        hidden_out,
        grad_in,
        grad_qkv[0],
        grad_qkv[1],
        grad_qkv[2],
        grad_wo,
        grad_wg,
        grad_wu,
        grad_wd,
        terms[0],
        terms[1],
        w_query.astype(F32) * column_factor[None, :],
        w_key.astype(F32) * column_factor[None, :],
        head_peaks,
    )


def solution(mesh):
    wide, narrow = mesh.devices.shape
    sizes = (4, wide // 8, 2, narrow // 2, 2)
    fine = Mesh(mesh.devices.reshape(sizes), ("z", "q", "y", "x", "c"))
    both = P(WIDE, NARROW)
    turned = P(NARROW, WIDE)
    return jax.shard_map(
        functools.partial(on_device, sizes),
        mesh=fine,
        in_specs=(
            both, P(WIDE), both, both, both, turned, P(WIDE), both, both, turned, both, P(), P()
        ),
        out_specs=(
            both, both, both, both, both, turned, both, both, turned,
            P(WIDE), P(WIDE), both, both, P(NARROW),
        ),
        check_vma=False,
    )
```

```python
import functools

import jax
import jax.numpy as jnp
from jax import lax
from jax.experimental import pallas as pl
from jax.experimental.pallas import tpu as pltpu
from jax.sharding import Mesh
from jax.sharding import PartitionSpec as P

HDIM = 64
HALF = HDIM // 2

eps_norm = 1e-05
rope_base = 130000.0
clip_limit = 5.0
masked_fill = -1e30

F32 = jnp.float32
BF16 = jnp.bfloat16
WIDE = ("z", "q", "y")
GROUP = ("q", "y")
NARROW = ("x", "c")
VMEM_BYTES = 60 * 2**20
EXTRA = 16


def lookup(lookup_table, indices):
    labels = jnp.arange(lookup_table.shape[0], dtype=jnp.int32)
    return jnp.sum(
        jnp.where(indices[:, None] == labels[None, :], lookup_table[None, :], 0),
        axis=1,
        dtype=jnp.int32,
    )


def segment_tables(segment_ids, parents):
    labels = jnp.arange(parents.shape[0], dtype=jnp.int32)
    counts = jnp.sum(
        (segment_ids[:, None] == labels[None, :]).astype(jnp.int32), axis=0, dtype=jnp.int32
    )
    starts = jnp.sum(
        jnp.where(labels[None, :] < labels[:, None], counts[None, :], 0), axis=1, dtype=jnp.int32
    )
    ancestor = lookup(parents, parents)
    parent_len = jnp.where(parents != labels, lookup(counts, parents), 0)
    ancestor_len = jnp.where(ancestor != parents, lookup(counts, ancestor), 0)
    return (ancestor, starts, parent_len, ancestor_len)


def dot(left, right, left_dim, right_dim):
    return lax.dot_general(
        left, right, (((left_dim,), (right_dim,)), ((), ())), preferred_element_type=F32
    )


def take(array, index, axis=0):
    return lax.dynamic_index_in_dim(array, index, axis, keepdims=False)


def swap(array, axis):
    return lax.ppermute(array, axis, [(0, 1), (1, 0)])


def ring(array, size):
    return lax.ppermute(array, "z", [(i, (i + 1) % size) for i in range(size)])


def pick(flag, first, second):
    return jnp.where(flag == 0, first, second)


def together(*values):
    return lax.optimization_barrier(values)


def params():
    return pltpu.CompilerParams(vmem_limit_bytes=VMEM_BYTES)


def cost(time):
    return pl.CostEstimate(flops=int(time * 1e9), bytes_accessed=1000, transcendentals=0)


def shape(dims, dtype):
    return jax.ShapeDtypeStruct(dims, dtype)


def full(dims):
    return pl.BlockSpec(dims, lambda *_: (0,) * len(dims))


def fill_tiles(sources, mask, held, k_ext, values_t):
    if len(sources) == 1:
        held[...] = sources[0][...]
    else:
        for t, source in enumerate(sources):
            held[t] = source[...]
    for t in range(held.shape[0]):
        tile = held[t].astype(F32)
        spare = k_ext.shape[2] - HDIM - mask.shape[1]
        parts = [tile[HDIM : 2 * HDIM], mask[t].astype(F32)]
        parts.append(jnp.zeros((spare, tile.shape[1]), F32))
        k_ext[t] = jnp.concatenate(parts, axis=0).T.astype(BF16)
        if values_t is not None:
            values_t[t] = jnp.concatenate(
                [tile[2 * HDIM :], jnp.zeros((HDIM, tile.shape[1]), F32)], axis=0
            ).T.astype(BF16)


def query_ext(q, mask, depth):
    spare = depth - HDIM - mask.shape[1]
    return jnp.concatenate([q, mask[0], jnp.zeros((spare, q.shape[1]), BF16)], axis=0)


def attend_kernel(visible, counts, q_pos, k_pos, *refs):
    q_mask, k_mask, low, out, log_norm, peak, held, k_ext = refs[-8:]
    i = pl.program_id(0)
    tiles, _, width = held.shape

    @pl.when(i == 0)
    def _():
        fill_tiles(refs[:-8], k_mask, held, k_ext, None)

    mine = q_pos[pl.num_programs(0) * 2]
    q_tile = query_ext(held[mine + i, :HDIM], q_mask, k_ext.shape[2])
    relative = lax.broadcasted_iota(jnp.int32, (width, width), 0) - lax.broadcasted_iota(
        jnp.int32, (width, width), 1
    )

    def one_tile(j, carry, diagonal):
        high, total, acc = carry
        scores = dot(k_ext[j], q_tile, 1, 0)
        if diagonal:
            scores = jnp.where(relative <= 0, scores, masked_fill)
        new_high = jnp.maximum(high, jnp.max(scores, axis=0, keepdims=True))
        weights = jnp.exp(scores - new_high)
        shrink = jnp.exp(high - new_high)
        total = total * shrink + jnp.sum(weights, axis=0, keepdims=True)
        acc = acc * shrink + dot(held[j, 2 * HDIM :], weights.astype(BF16), 1, 0)
        return new_high, total, acc

    start = (
        jnp.full((1, width), masked_fill, F32),
        jnp.zeros((1, width), F32),
        jnp.zeros((HDIM, width), F32),
    )
    high, total, acc = lax.fori_loop(
        0,
        counts[i],
        lambda n, carry: one_tile(visible[i * tiles + n], carry, False),
        one_tile(mine + i, start, True),
    )
    result = acc / total
    out[0] = result
    low[0] = result.astype(BF16)
    log_norm[0] = high + jnp.log(total)
    peak[0] = high


def attend(tables, tiles, q_mask, k_mask):
    q_tiles, labels, width = q_mask.shape
    k_tiles = k_mask.shape[0]
    part = lambda i, *_: (i, 0, 0)
    placed = lambda i, visible, counts, q_pos, k_pos: (q_pos[i + q_tiles], 0, 0)
    return pl.pallas_call(
        attend_kernel,
        grid_spec=pltpu.PrefetchScalarGridSpec(
            num_scalar_prefetch=4,
            grid=(q_tiles,),
            in_specs=[full(a.shape) for a in tiles]
            + [pl.BlockSpec((1, labels, width), part), full(k_mask.shape)],
            out_specs=[
                pl.BlockSpec((1, HDIM, width), placed),
                pl.BlockSpec((1, HDIM, width), part),
                pl.BlockSpec((1, 1, width), part),
                pl.BlockSpec((1, 1, width), part),
            ],
            scratch_shapes=[
                pltpu.VMEM((k_tiles, 3 * HDIM, width), BF16),
                pltpu.VMEM((k_tiles, width, 2 * HDIM), BF16),
            ],
        ),
        out_shape=[
            shape((q_tiles, HDIM, width), BF16),
            shape((q_tiles, HDIM, width), F32),
            shape((q_tiles, 1, width), F32),
            shape((q_tiles, 1, width), F32),
        ],
        compiler_params=params(),
        cost_estimate=cost(18),
        name="attend",
    )(*tables, *tiles, q_mask, k_mask)


def attend_back_kernel(visible, counts, q_pos, k_pos, *refs):
    q_mask, k_mask, grads, out, log_norm, cosine, sine, back = refs[-13:-5]
    held, k_ext, values_t, acc_k, acc_v = refs[-5:]
    i = pl.program_id(0)
    tiles, _, width = held.shape

    @pl.when(i == 0)
    def _():
        fill_tiles(refs[:-13], k_mask, held, k_ext, values_t)
        acc_k[...] = jnp.zeros_like(acc_k)
        acc_v[...] = jnp.zeros_like(acc_v)

    mine = q_pos[pl.num_programs(0) * 2]
    q_rows = held[mine + i, :HDIM]
    q_tile = query_ext(q_rows, q_mask, k_ext.shape[2])
    g_tile = grads[0]
    g_ext = jnp.concatenate([g_tile, jnp.zeros_like(g_tile)], axis=0)
    lse = log_norm[0]
    delta = jnp.sum(g_tile.astype(F32) * out[0], axis=0, keepdims=True)
    relative = lax.broadcasted_iota(jnp.int32, (width, width), 0) - lax.broadcasted_iota(
        jnp.int32, (width, width), 1
    )

    def one_tile(j, acc, diagonal):
        scores = dot(k_ext[j], q_tile, 1, 0)
        if diagonal:
            scores = jnp.where(relative <= 0, scores, masked_fill)
        probs = jnp.exp(scores - lse)
        grad_probs = dot(values_t[j], g_ext, 1, 0)
        grad_scores = (probs * (grad_probs - delta)).astype(BF16)
        acc_v[j] += dot(g_tile, probs.astype(BF16), 1, 1)
        acc_k[j] += dot(q_rows, grad_scores, 1, 1)
        return acc + dot(held[j, HDIM : 2 * HDIM], grad_scores, 1, 0)

    acc = lax.fori_loop(
        0,
        counts[i],
        lambda n, acc: one_tile(visible[i * tiles + n], acc, False),
        one_tile(mine + i, jnp.zeros((HDIM, width), F32), True),
    )

    def put_unrotated(grad, t, base):
        first, second, c, s = grad[:HALF], grad[HALF:], cosine[t], sine[t]
        back[t, base : base + HALF] = (first * c + second * s).astype(BF16)
        back[t, base + HALF : base + HDIM] = (second * c - first * s).astype(BF16)

    put_unrotated(acc * HDIM ** (-0.5), mine + i, 0)

    @pl.when(i == pl.num_programs(0) - 1)
    def _():
        for t in range(tiles):
            put_unrotated(acc_k[t], t, HDIM)
            back[t, 2 * HDIM :] = acc_v[t].astype(BF16)


def attend_back(tables, tiles, q_mask, k_mask, grads, out, log_norm, cosine, sine):
    q_tiles, labels, width = q_mask.shape
    k_tiles = k_mask.shape[0]
    part = lambda i, *_: (i, 0, 0)
    placed = lambda i, visible, counts, q_pos, k_pos: (q_pos[i + q_tiles], 0, 0)
    return pl.pallas_call(
        attend_back_kernel,
        grid_spec=pltpu.PrefetchScalarGridSpec(
            num_scalar_prefetch=4,
            grid=(q_tiles,),
            in_specs=[full(a.shape) for a in tiles]
            + [
                pl.BlockSpec((1, labels, width), part),
                full(k_mask.shape),
                pl.BlockSpec((1, HDIM, width), placed),
                pl.BlockSpec((1, HDIM, width), part),
                pl.BlockSpec((1, 1, width), part),
                full(cosine.shape),
                full(sine.shape),
            ],
            out_specs=full((k_tiles, 3 * HDIM, width)),
            scratch_shapes=[
                pltpu.VMEM((k_tiles, 3 * HDIM, width), BF16),
                pltpu.VMEM((k_tiles, width, 2 * HDIM), BF16),
                pltpu.VMEM((k_tiles, width, 2 * HDIM), BF16),
                pltpu.VMEM((k_tiles, HDIM, width), F32),
                pltpu.VMEM((k_tiles, HDIM, width), F32),
            ],
        ),
        out_shape=shape((k_tiles, 3 * HDIM, width), BF16),
        compiler_params=params(),
        cost_estimate=cost(22),
        name="attend_back",
    )(*tables, *tiles, q_mask, k_mask, grads, out, log_norm, cosine, sine)


def row_scale(pieces, width):
    squares = 0.0
    for piece in pieces:
        values = piece[...].astype(F32)
        squares = squares + jnp.sum(values * values, axis=1, keepdims=True)
    return lax.rsqrt(squares / width + eps_norm)


def aligned(start, size):
    return pl.ds(pl.multiple_of(start, size), size)


def block_of(where, k):
    return where[0] ^ k


def half_columns(where, h, wide):
    return aligned((h ^ where[1]) * wide, wide)


def put_normed(where, pieces, rstd, gain, normed):
    cols = pieces[0].shape[1]
    half = cols // 2
    for k, piece in enumerate(pieces):
        block = block_of(where, k)
        values = piece[...].astype(F32) * rstd * gain[:, aligned(block * cols, cols)]
        for part in range(2):
            columns = aligned((part * 4 + block) * half, half)
            normed[:, columns] = values[:, part * half : (part + 1) * half].astype(BF16)


def qkv_kernel(where, *refs):
    pieces, (gain, w_first, w_second, cosine, sine) = refs[:4], refs[4:9]
    normed, mine, other, scale = refs[-4:]
    rows, cols = pieces[0].shape
    half = cols // 2
    rstd = row_scale(pieces, 4 * cols)
    scale[...] = rstd
    put_normed(where, pieces, rstd, gain, normed)
    c, s = cosine[...], sine[...]
    features = 3 * HDIM
    for out, head in ((mine, where[2]), (other, 1 - where[2])):
        span = aligned(head * features, features)
        lin = 0.0
        for h, weights in enumerate((w_first, w_second)):
            for z in range(4):
                columns = aligned(((h ^ where[1]) * 4 + z) * half, half)
                lin = lin + dot(weights[z, span, :], normed[:, columns], 1, 1)
        for part, factor in ((0, HDIM ** (-0.5)), (1, 1.0)):
            base = part * HDIM
            first, second = lin[base : base + HALF], lin[base + HALF : base + HDIM]
            out[base : base + HALF] = ((first * c - second * s) * factor).astype(BF16)
            out[base + HALF : base + HDIM] = ((second * c + first * s) * factor).astype(BF16)
        out[2 * HDIM :] = lin[2 * HDIM :].astype(BF16)


def chunk_call(
    kernel, name, time, where, s, inputs, buffers, whole_shapes, out_shapes, scratch=(), out_there=0
):
    def spec(dims, how):
        rest = (0,) * (len(dims) - 1)
        if how == "whole":
            return full(dims)
        if how == "there":
            return pl.BlockSpec(memory_space=pl.ANY)
        block = (dims[0] // 4, *dims[1:])
        if how == "chunk":
            return pl.BlockSpec(block, lambda i, where: (s, *rest))
        return pl.BlockSpec(block, lambda i, where: (where[3], *rest))

    in_specs = [spec(a.shape, how) for a, how in inputs]
    arrays = [a for a, _ in inputs]
    aliases = {}
    if buffers is not None:
        for n, buffer in enumerate(buffers):
            aliases[1 + len(arrays)] = n
            in_specs.append(pl.BlockSpec(memory_space=pl.ANY))
            arrays.append(buffer)
    out_specs = [spec(dims, how) for dims, how in whole_shapes]
    out_specs += [
        pl.BlockSpec(memory_space=pl.ANY) if n < out_there else full(a.shape)
        for n, a in enumerate(out_shapes)
    ]
    return pl.pallas_call(
        kernel,
        grid_spec=pltpu.PrefetchScalarGridSpec(
            num_scalar_prefetch=1,
            grid=(1,),
            in_specs=in_specs,
            out_specs=out_specs,
            scratch_shapes=list(scratch),
        ),
        out_shape=[shape(dims, BF16) for dims, _ in whole_shapes] + list(out_shapes),
        input_output_aliases=aliases,
        compiler_params=params(),
        cost_estimate=cost(time),
        name=name,
    )(where, *arrays)


def fetch(weights, held, sems, first=0, start=0):
    copies = []
    for n, weight in enumerate(weights):
        rows = weight.shape[0]
        copies.append(
            pltpu.make_async_copy(weight, held.at[pl.ds(start, rows)], sems.at[first + n])
        )
        copies[-1].start()
        start += rows
    return copies


class Sends:
    def __init__(self, sems):
        self.sems, self.copies = sems, []

    def start(self, source, target):
        self.copies.append(pltpu.make_async_copy(source, target, self.sems.at[len(self.copies)]))
        self.copies[-1].start()

    def wait(self):
        for copy in self.copies:
            copy.wait()


def load(pairs, sems, first):
    copies = [
        pltpu.make_async_copy(source, target, sems.at[first + n])
        for n, (source, target) in enumerate(pairs)
    ]
    for copy in copies:
        copy.start()
    return copies


def wait_all(copies):
    for copy in copies:
        copy.wait()


def ffn_kernel(chunks, count, where, *refs):
    pieces, gain, weights = refs[:8], refs[8], refs[9 : 9 + count]
    outs = refs[-16:-8]
    mids, normed_all, hidden_all, gates_all, ups_all, held, sems, out_sems = refs[-8:]
    normed_out, hidden_out, scales = outs[0], outs[1], outs[6:]
    rows, cols = mids.shape[2:]
    units, wide = hidden_all.shape[2], 2 * cols
    come = [
        load([(pieces[4 * i + k], mids.at[i, k]) for k in range(4)], sems, count + 4 * i)
        for i in range(2)
    ]
    copies = fetch(weights, held, sems)
    sends = Sends(out_sems)
    step = 256
    for i in range(2):
        chunk = pl.ds(chunks[i] * rows, rows)
        normed, hidden = normed_all.at[i], hidden_all.at[i]
        gates, ups = gates_all.at[i], ups_all.at[i]
        gates_out, ups_out = outs[2 + 2 * i], outs[3 + 2 * i]
        wait_all(come[i])
        blocks = [mids.at[i, k] for k in range(4)]
        rstd = row_scale(blocks, 4 * cols)
        scales[i][...] = rstd
        put_normed(where, blocks, rstd, gain, normed)
        sends.start(normed, normed_out.at[chunk])
        if i == 0:
            wait_all(copies)
        for n in range(0, units, step):
            span = slice(n, n + step)
            columns = pl.ds(n, step)
            gate = up = 0.0
            for h in range(2):
                values = normed[:, half_columns(where, h, wide)]
                gate = gate + dot(values, held[h * wide : (h + 1) * wide, span], 1, 0)
                up = up + dot(values, held[(h + 2) * wide : (h + 3) * wide, span], 1, 0)
            gates[:, span] = gate
            ups[:, span] = up
            sends.start(gates.at[:, columns], gates_out.at[:, columns])
            sends.start(ups.at[:, columns], ups_out.at[:, columns])
            hidden[:, span] = (gate * jax.nn.sigmoid(gate) * up).astype(BF16)
            sends.start(hidden.at[:, columns], hidden_out.at[chunk, columns])
    sends.wait()


def arrange_kernel(zs, cots, cot_rows):
    cols = cots.shape[2]
    half = cols // 2
    for block in range(4):
        for part in range(2):
            start = (part * 4 + block) * half
            cot_rows[:, start : start + half] = cots[block, :, part * half : (part + 1) * half]


def arrange(cot, zs):
    blocks, rows, cols = cot.shape
    return pl.pallas_call(
        arrange_kernel,
        grid_spec=pltpu.PrefetchScalarGridSpec(
            num_scalar_prefetch=1,
            grid=(4,),
            in_specs=[pl.BlockSpec((blocks // 4, rows, cols), lambda s, zs: (zs[s], 0, 0))],
            out_specs=pl.BlockSpec((rows, 4 * cols), lambda s, zs: (s, 0)),
        ),
        out_shape=shape((4 * rows, 4 * cols), BF16),
        compiler_params=params(),
        cost_estimate=cost(5),
        name="arrange",
    )(zs, cot)


def ffn_back_kernel(chunks, downs, count, where, *refs):
    weights, kept = refs[:count], refs[count : count + 4]
    all_cot, all_hidden, all_normed = refs[count + 4 : count + 7]
    grad_gate_out, grad_up_out, out = refs[-21:-18]
    backs, gain_term = refs[-18:-14], refs[-14]
    held, cot_all, gate_up, hidden_in, normed_in, sems = refs[-13:-7]
    grad_gates, grad_ups, out_held, back_held, lines, out_sems, line_sems = refs[-7:]
    rows, units = grad_gates.shape[1:]
    cols = out_held.shape[3]
    half, wide = cols // 2, 2 * cols
    step = 256
    spans = [pl.ds(s * rows, rows) for s in chunks]
    early = load([(all_cot.at[spans[0]], cot_all.at[0])], sems, count)
    early += fetch(weights[:downs], held, sems)
    early += load([(kept[0], gate_up.at[0, 0]), (kept[1], gate_up.at[0, 1])], sems, count + 1)
    late = load(
        [(all_hidden.at[spans[0]], hidden_in.at[0]), (all_normed.at[spans[0]], normed_in.at[0])],
        sems,
        count + 3,
    )
    late += fetch(weights[downs:], held, sems, downs, 2 * wide)
    second = load(
        [
            (all_cot.at[spans[1]], cot_all.at[1]),
            (kept[2], gate_up.at[1, 0]),
            (kept[3], gate_up.at[1, 1]),
            (all_hidden.at[spans[1]], hidden_in.at[1]),
            (all_normed.at[spans[1]], normed_in.at[1]),
        ],
        sems,
        count + 5,
    )
    sends, tails = Sends(out_sems), Sends(line_sems)
    for i in range(2):
        cot_rows, hidden, normed = cot_all.at[i], hidden_in.at[i], normed_in.at[i]
        gates, ups = gate_up.at[i, 0], gate_up.at[i, 1]
        grad_gate, grad_up = grad_gates.at[i], grad_ups.at[i]
        place = where[3 + i]
        wait_all(early if i == 0 else second)
        for n in range(0, units, step):
            span = slice(n, n + step)
            columns = pl.ds(n, step)
            grad_hidden = 0.0
            for h in range(2):
                grad_hidden = grad_hidden + dot(
                    cot_rows[:, half_columns(where, h, wide)],
                    held[h * wide : (h + 1) * wide, span],
                    1,
                    0,
                )
            gate, up = gates[:, span], ups[:, span]
            sigmoid = jax.nn.sigmoid(gate)
            grad_gate[:, span] = (
                grad_hidden * up * sigmoid * (1.0 + gate * (1.0 - sigmoid))
            ).astype(BF16)
            grad_up[:, span] = (grad_hidden * (gate * sigmoid)).astype(BF16)
            sends.start(grad_gate.at[:, columns], grad_gate_out.at[spans[i], columns])
            sends.start(grad_up.at[:, columns], grad_up_out.at[spans[i], columns])
        if i == 0:
            wait_all(late)
        row_term = 0.0
        for k in range(4):
            block = block_of(where, k)
            back = backs[2 * i + k % 2]
            for h in range(2):
                part = aligned((h ^ where[1]) * half, half)
                of_down, of_gate, of_up = [
                    held[aligned((n + h) * wide + block * half, half), :] for n in (0, 2, 4)
                ]
                out_held[i, k, :, part] = dot(hidden[...], of_down, 1, 1).astype(BF16)
                partial = dot(grad_gate[...], of_gate, 1, 1) + dot(grad_up[...], of_up, 1, 1)
                back_held[i, k, :, part] = partial.astype(BF16)
                columns = aligned(((h ^ where[1]) * 4 + block) * half, half)
                terms = partial * normed[:, columns].astype(F32)
                column_term = jnp.sum(terms, axis=0, keepdims=True)
                if i == 0:
                    gain_term[:, columns] = column_term
                else:
                    gain_term[:, columns] += column_term
                row_term = row_term + jnp.sum(terms, axis=1, keepdims=True)
            sends.start(out_held.at[i, k], out.at[place * 4 + block])
            sends.start(back_held.at[i, k], back.at[k // 2, pl.ds(0, rows)])
        lines[i] = row_line(row_term, cols)
        for back in backs[2 * i : 2 * i + 2]:
            for x in range(2):
                tails.start(lines.at[i], back.at[x, pl.ds(rows, EXTRA)])
    sends.wait()
    tails.wait()


def row_line(row_term, cols):
    rows = row_term.shape[0]
    line = jnp.broadcast_to(row_term, (rows, 128)).T[:EXTRA]
    return jnp.concatenate([line, jnp.zeros((EXTRA, cols - rows), F32)], axis=1).astype(BF16)


def put_row_term(row_term, cols, keep, send):
    rows = row_term.shape[0]
    line = row_line(row_term, cols)
    for ref in (keep, send):
        ref[0, rows:] = line
        ref[1, rows:] = line


def qkv_back_kernel(where, normed, mine, other, w_first, w_second, keep, send, gain_term):
    rows, cols = normed.shape[0], keep.shape[2]
    half = cols // 2
    features = 3 * HDIM
    row_term = 0.0
    for k in range(4):
        block = block_of(where, k)
        back = (keep, send)[k % 2]
        for h, weights in enumerate((w_first, w_second)):
            part = aligned((h ^ where[1]) * half, half)
            partial = 0.0
            for grads, head in ((mine, where[2]), (other, 1 - where[2])):
                span = aligned(head * features, features)
                partial = partial + dot(grads[0], weights[block, span, :], 0, 0)
            back[k // 2, :rows, part] = partial.astype(BF16)
            columns = aligned(((h ^ where[1]) * 4 + block) * half, half)
            terms = partial * normed[:, columns].astype(F32)
            gain_term[:, columns] = jnp.sum(terms, axis=0, keepdims=True)
            row_term = row_term + jnp.sum(terms, axis=1, keepdims=True)
    put_row_term(row_term, cols, keep, send)


def qkv_weights_kernel(where, normed, *refs):
    own, other, outs = refs[0], refs[1], refs[2:]
    count = other.shape[0]
    half = outs[0].shape[2]
    rows, features = own.shape[2], 3 * HDIM
    for h, out in enumerate(outs):
        for z in range(4):
            columns = aligned(((h ^ where[1]) * 4 + z) * half, half)
            for grads, head in ((own, where[2]), (other, 1 - where[2])):
                total = 0.0
                for s in range(count):
                    total = total + dot(
                        grads[s], normed[s * rows : (s + 1) * rows, columns], 1, 0
                    )
                out[z, aligned(head * features, features), :] = total.astype(BF16)


def project_kernel(where, attended, weights, keep, send):
    half = weights.shape[2]
    for k in range(4):
        for part in range(2):
            (keep, send)[k % 2][k // 2, :, part * half : (part + 1) * half] = dot(
                attended[...], weights[block_of(where, k) * 2 + part], 0, 0
            ).astype(BF16)


def project_back_kernel(where, p0, p1, p2, p3, attended, weights, grad_att, grad_weights):
    half = weights.shape[2]
    total = 0.0
    for k, piece in enumerate((p0, p1, p2, p3)):
        for part in range(2):
            b = block_of(where, k) * 2 + part
            values = piece[:, part * half : (part + 1) * half]
            total = total + dot(weights[b], values, 1, 1)
            grad_weights[b] = dot(attended[...], values, 1, 0).astype(BF16)
    grad_att[...] = total.astype(BF16)


def columns_kernel(parts, out):
    out[...] = parts[0].astype(F32)


def turned_kernel(parts, out):
    out[...] = parts[0].astype(F32).T


def lay_out(parts, turned):
    nz, n, m = parts.shape
    if turned:
        kernel, dims, block, place = turned_kernel, (nz * m, n), (m, n), lambda z: (z, 0)
    else:
        kernel, dims, block, place = columns_kernel, (n, nz * m), (n, m), lambda z: (0, z)
    return pl.pallas_call(
        kernel,
        grid=(nz,),
        in_specs=[pl.BlockSpec((1, n, m), lambda z: (z, 0, 0))],
        out_specs=pl.BlockSpec(block, place),
        out_shape=shape(dims, F32),
        compiler_params=params(),
        cost_estimate=cost(2),
        name="lay_out",
    )(parts)


def qkv_out_kernel(where, parts, *outs):
    features = 3 * HDIM
    for z in range(parts.shape[0]):
        for n, out in enumerate(outs):
            heads = [parts[z, h * features + n * HDIM : h * features + (n + 1) * HDIM] for h in (0, 1)]
            both = jnp.concatenate(heads, axis=0).astype(F32)
            out[:, z * 2 * HDIM : (z + 1) * 2 * HDIM] = both.T


def small_call(kernel, name, time, where, inputs, out_shapes, specs=None):
    specs = specs or {}
    return pl.pallas_call(
        kernel,
        grid_spec=pltpu.PrefetchScalarGridSpec(
            num_scalar_prefetch=1,
            grid=(1,),
            in_specs=[specs.get(n) or full(a.shape) for n, a in enumerate(inputs)],
            out_specs=[full(s.shape) for s in out_shapes],
        ),
        out_shape=list(out_shapes),
        compiler_params=params(),
        cost_estimate=cost(time),
        name=name,
    )(where, *inputs)


def on_device(
    sizes,
    hidden_in,
    gain_attn,
    w_query,
    w_key,
    w_value,
    w_out,
    gain_ffn,
    w_gate,
    w_up,
    w_down,
    cotangent,
    segment_ids,
    parents,
):
    nz, nq, ny, nx, nc = sizes
    rows, cols = hidden_in.shape
    groups = nq * ny
    group_rows = nz * rows
    width = cols * nx * nc
    half = cols // 2
    slab = gain_attn.shape[0]
    head = 3 * HDIM
    units = w_gate.shape[1] // nz

    zi, qi, yi, xi, ci = [lax.axis_index(a) for a in ("z", "q", "y", "x", "c")]
    group = qi * ny + yi
    own_columns = xi * nc + ci
    zs = [(zi - s) % nz for s in range(nz)]
    flip = yi if nq == 1 else 0 * yi
    where = [jnp.stack([own_columns, flip, yi, z]).astype(jnp.int32) for z in zs]

    def scatter_narrow(keep, send):
        held = keep.astype(F32) + swap(send, "c").astype(F32)
        return held[0] + swap(held[1].astype(BF16), "x").astype(F32)

    def first_sum(keep, received):
        held = keep.astype(F32) + received.astype(F32)
        return held[0], held[1].astype(BF16)

    def spread_z(parts):
        return lax.all_to_all(parts, "z", split_axis=0, concat_axis=0, tiled=True)

    def gather_rows(parts):
        n = parts.shape[2]
        if nq == 1:
            return parts.reshape(-1, n), swap(parts, "y").reshape(-1, n)
        got = lax.all_gather(parts, GROUP, axis=0, tiled=False)
        got = got.reshape(2, groups // 2, nz, slab, n).transpose(0, 2, 1, 3, 4)
        return tuple(got.reshape(2, nz * half, n))

    def swap_part(parts, n):
        part = parts[n * nz // 2 : (n + 1) * nz // 2]
        return swap(part, "y") if nq == 1 else part

    def join_rows(parts, swapped):
        if nq > 1:
            return gather_rows(parts)
        return [a.reshape(-1, units) for a in (parts, *swapped)]

    def gather_lanes(parts):
        n = parts.shape[1]
        if nq == 1:
            return parts, swap(parts, "y")
        got = lax.all_gather(parts, GROUP, axis=0, tiled=False)
        got = got.reshape(2, groups // 2, nz, n, slab).transpose(0, 2, 3, 1, 4)
        return tuple(got.reshape(2, nz, n, half))

    def exchange_rows(grad):
        if nq == 1:
            return swap(take(grad.reshape(2, -1, grad.shape[1]), 1 - yi), "y")
        n = grad.shape[1]
        parts = grad.reshape(2, nz, groups // 2, slab, n).transpose(0, 2, 1, 3, 4)
        return lax.psum_scatter(
            parts.reshape(groups, nz, slab, n), GROUP, scatter_dimension=0, tiled=False
        )

    def add_rows(grad, received):
        if nq == 1:
            own = take(grad.reshape(2, -1, grad.shape[1]), yi)
            received = (own.astype(F32) + received.astype(F32)).astype(BF16)
        return received.reshape(nz, slab, -1)

    def exchange_lanes(second):
        return swap(second, "y") if nq == 1 else second

    def scatter_lanes(first, second):
        n = first.shape[1]
        if nq == 1:
            return (first.astype(F32) + second.astype(F32)).astype(BF16)
        both = jnp.stack([first, second]).reshape(2, nz, n, groups // 2, slab)
        both = both.transpose(0, 3, 1, 2, 4).reshape(groups, nz, n, slab)
        return lax.psum_scatter(both, GROUP, scatter_dimension=0, tiled=False)

    def sum_small(values, axes):
        for axis in axes:
            if axis == "z":
                for bit in (1, 2):
                    values = values + lax.ppermute(values, "z", [(i, i ^ bit) for i in range(nz)])
            elif axis == "q":
                values = lax.psum(values, "q") if nq > 1 else values
            else:
                values = values + swap(values, axis)
        return values

    stacked = jnp.stack([w_query, w_key, w_value]).reshape(3, slab, nz, ny, HDIM)
    stacked = stacked.transpose(2, 3, 0, 4, 1).reshape(nz, ny * head, slab)
    both_gains = jnp.concatenate(
        [gain_attn[None], gain_ffn[None], jnp.zeros((EXTRA - 2, slab), BF16)], axis=0
    )
    both_gains = jnp.broadcast_to(both_gains[None], (nz, EXTRA, slab))
    stacked = jnp.concatenate([stacked, both_gains], axis=1)
    z1, x0, c0, stacked, segment_ids, parents = together(
        ring(hidden_in, nz),
        swap(hidden_in, "x"),
        swap(hidden_in, "c"),
        stacked,
        segment_ids,
        parents,
    )

    ancestor, starts, parent_len, ancestor_len = segment_tables(segment_ids, parents)
    q_blocks = [(z * nq + qi) * ny + (yi ^ dy) for dy in range(ny) for z in zs]
    k_blocks = [(z * nq + q) * ny + (yi ^ dy) for q in range(nq) for dy in range(ny) for z in zs]
    segments = segment_ids.reshape(-1, rows)
    k_seg = jnp.stack([take(segments, b) for b in k_blocks])
    k_pos = jnp.stack(k_blocks).astype(jnp.int32)
    q_tiles, k_tiles = len(q_blocks), len(k_blocks)
    of_queries = lambda a: lax.dynamic_slice_in_dim(a, qi * q_tiles, q_tiles, 0)
    flat = k_seg.reshape(-1)
    labels = jnp.arange(-(-parents.shape[0] // 16) * 16, dtype=jnp.int32)[None, :, None]
    places = k_pos[:, None] * rows + jnp.arange(rows, dtype=jnp.int32)[None]
    places = places + lookup(parent_len + ancestor_len - starts, flat).reshape(k_tiles, rows)
    k_own = labels == k_seg[:, None]
    q_seen = of_queries(
        k_own
        | (labels == lookup(parents, flat).reshape(k_tiles, 1, rows))
        | (labels == lookup(ancestor, flat).reshape(k_tiles, 1, rows))
    )
    q_mask = jnp.where(q_seen, 0.0, masked_fill).astype(BF16)
    k_mask = k_own.astype(BF16)
    q_pos = of_queries(k_pos)
    shown = jnp.any(jnp.any(q_seen, axis=2)[:, None] & jnp.any(k_own, axis=2)[None], axis=2)
    shown = shown & (k_pos[None, :] < q_pos[:, None])
    number = jnp.arange(k_tiles, dtype=jnp.int32)
    earlier = number[None, None, :] < number[None, :, None]
    before = jnp.sum((shown[:, None, :] & earlier).astype(jnp.int32), axis=2)
    chosen = shown[:, None, :] & (before[:, None, :] == number[None, :, None])
    visible = jnp.sum(jnp.where(chosen, number[None, None, :], 0), axis=2, dtype=jnp.int32)
    slots = jnp.stack([z * ny + (yi ^ dy) for dy in range(ny) for z in zs]).astype(jnp.int32)
    q_info = jnp.concatenate([q_pos, slots, (qi * q_tiles).reshape(1).astype(jnp.int32)])
    tables = (
        visible.reshape(-1),
        jnp.sum(shown.astype(jnp.int32), axis=1, dtype=jnp.int32),
        q_info,
        k_pos,
    )
    frequency = rope_base ** (-2.0 * jnp.arange(HALF, dtype=F32) / HDIM)
    angles = places.astype(F32)[:, None, :] * frequency[None, :, None]
    cosine, sine = jnp.cos(angles), jnp.sin(angles)
    cos_q, sin_q = of_queries(cosine), of_queries(sine)

    z2, x1, c1, cx0, w_qkv, (tables, q_mask, k_mask, cosine, sine, cos_q, sin_q) = together(
        ring(z1, nz),
        swap(z1, "x"),
        swap(z1, "c"),
        swap(x0, "c"),
        spread_z(stacked),
        (tables, q_mask, k_mask, cosine, sine, cos_q, sin_q),
    )
    z3, x2, c2, cx1, w_qkv, w_gate_, cotangent_, w_out_ = together(
        ring(z2, nz),
        swap(z2, "x"),
        swap(z2, "c"),
        swap(x1, "c"),
        gather_lanes(w_qkv),
        w_gate,
        cotangent,
        w_out,
    )
    x3, c3, cx2 = swap(z3, "x"), swap(z3, "c"), swap(x2, "c")
    x_chunks = [
        (hidden_in, c0, x0, cx0),
        (z1, c1, x1, cx1),
        (z2, c2, x2, cx2),
        (z3, c3, x3, swap(x3, "c")),
    ]
    gains = [w[:, ny * head : ny * head + 2].astype(F32) for w in w_qkv]
    gains = jnp.stack([pick(flip, *gains), pick(flip, gains[1], gains[0])], axis=1)
    gains = gains.transpose(2, 0, 1, 3).reshape(2, width)
    gain1, gain2 = gains[:1], gains[1:]

    wo = lax.all_gather(w_out_, WIDE, axis=0, tiled=False)
    if nq > 1:
        wo = wo.reshape(nz * 2, groups // 2, -1, slab).transpose(0, 2, 1, 3)
        wo = wo.reshape(nz * 2, -1, half)
    of_units = lambda w: spread_z(w.reshape(slab, nz, units).transpose(1, 0, 2))
    cot = lax.all_gather(cotangent_, ("z", *NARROW), axis=0, tiled=False)

    buffers, mine, theirs, scale1 = None, [], [], []
    for s in range(nz):
        normed1, own, other, scale = chunk_call(
            qkv_kernel,
            "qkv",
            5,
            where[s],
            s,
            [(a, "whole") for a in (*x_chunks[s], gain1, *w_qkv, cos_q[s], sin_q[s])],
            buffers,
            [((group_rows, width), "chunk")],
            [shape((head, rows), BF16), shape((head, rows), BF16), shape((rows, 1), F32)],
        )
        buffers = [normed1]
        mine.append(own)
        theirs.append(swap(other, "y"))
        scale1.append(scale)
    tiles, gate_parts, w_up_, w_down_ = together(
        mine + theirs, of_units(w_gate_), w_up, w_down.T
    )
    if nq > 1:
        tiles = [lax.all_gather(jnp.stack(tiles), "q", axis=0, tiled=True)]
    (att_low, att, log_norm, peak), up_parts, w_gates, w_down_ = together(
        attend(tables, tiles, q_mask, k_mask), of_units(w_up_), gather_rows(gate_parts), w_down_
    )

    att_t = lax.all_to_all(att_low, ("z", "y"), split_axis=0, concat_axis=0, tiled=True)
    att_t, w_down_ = together(att_t, w_down_)
    att_t = att_t.reshape(nz * ny * HDIM, rows)
    keep, send = small_call(
        project_kernel,
        "project",
        4,
        where[0],
        (att_t, wo),
        [shape((2, rows, cols), BF16)] * 2,
    )
    residual_mid = hidden_in.astype(F32) + scatter_narrow(keep, send)
    down_parts = of_units(w_down_)
    mid_block = residual_mid.astype(BF16)

    def forward(chunks, pieces, buffers):
        results = chunk_call(
            functools.partial(ffn_kernel, chunks, len(w_gates) + len(w_ups)),
            "feed_forward",
            9,
            where[0],
            0,
            [(a, "there") for a in pieces]
            + [(gain2, "whole")]
            + [(w, "there") for w in (*w_gates, *w_ups)],
            buffers,
            [((group_rows, width), "there"), ((group_rows, units), "there")],
            [shape((rows, units), F32)] * 4 + [shape((rows, 1), F32)] * 2,
            [
                pltpu.VMEM((2, 4, rows, cols), BF16),
                pltpu.VMEM((2, rows, width), BF16),
                pltpu.VMEM((2, rows, units), BF16),
                pltpu.VMEM((2, rows, units), F32),
                pltpu.VMEM((2, rows, units), F32),
                pltpu.VMEM((8 * cols, units), BF16),
                pltpu.SemaphoreType.DMA((len(w_gates) + len(w_ups) + 8,)),
                pltpu.SemaphoreType.DMA((2 + 6 * units // 256,)),
            ],
            4,
        )
        return results[:2], results[2:]

    def backward(chunks, saved, kept, buffers):
        weights = (*w_downs, *w_gates, *w_ups)
        places = jnp.concatenate([where[0][:3], jnp.stack([zs[s] for s in chunks]).astype(jnp.int32)])
        results = chunk_call(
            functools.partial(ffn_back_kernel, chunks, len(w_downs), len(weights)),
            "feed_forward_back",
            15,
            places,
            0,
            [(a, "there") for a in (*weights, *kept, cot_rows, saved[1], saved[0])],
            buffers,
            [
                ((group_rows, units), "there"),
                ((group_rows, units), "there"),
                ((nz * nx * nc, rows, cols), "there"),
            ],
            [shape((2, rows + EXTRA, cols), BF16)] * 4 + [shape((1, width), F32)],
            [
                pltpu.VMEM((12 * cols, units), BF16),
                pltpu.VMEM((2, rows, width), BF16),
                pltpu.VMEM((2, 2, rows, units), F32),
                pltpu.VMEM((2, rows, units), BF16),
                pltpu.VMEM((2, rows, width), BF16),
                pltpu.SemaphoreType.DMA((len(weights) + 10,)),
                pltpu.VMEM((2, rows, units), BF16),
                pltpu.VMEM((2, rows, units), BF16),
                pltpu.VMEM((2, 4, rows, cols), BF16),
                pltpu.VMEM((2, 4, rows, cols), BF16),
                pltpu.VMEM((2, EXTRA, cols), BF16),
                pltpu.SemaphoreType.DMA((16 + 4 * units // 256,)),
                pltpu.SemaphoreType.DMA((8,)),
            ],
            4,
        )
        return results[:3], results[3:7], results[7]

    z0 = mid_block
    z1, x0, c0, up_a = together(
        ring(z0, nz), swap(z0, "x"), swap(z0, "c"), swap_part(up_parts, 0)
    )
    z2, x1, c1, cx0, up_b, down_parts = together(
        ring(z1, nz),
        swap(z1, "x"),
        swap(z1, "c"),
        swap(x0, "c"),
        swap_part(up_parts, 1),
        down_parts,
    )
    w_ups = join_rows(up_parts, (up_a, up_b))
    z3, x2, c2, cx1, down_a, cot_rows = together(
        ring(z2, nz),
        swap(z2, "x"),
        swap(z2, "c"),
        swap(x1, "c"),
        swap_part(down_parts, 0),
        arrange(cot, jnp.stack(zs).astype(jnp.int32)),
    )
    x3, c3, cx2, down_b, (saved, kept01) = together(
        swap(z3, "x"),
        swap(z3, "c"),
        swap(x2, "c"),
        swap_part(down_parts, 1),
        forward((0, 1), (z0, c0, x0, cx0, z1, c1, x1, cx1), None),
    )
    w_downs = join_rows(down_parts, (down_a, down_b))
    cx3 = swap(x3, "c")
    saved, kept23 = forward((2, 3), (z2, c2, x2, cx2, z3, c3, x3, cx3), saved)
    buffers, back12, terms12 = backward((1, 2), saved, (*kept01[2:4], *kept23[:2]), None)
    part1, part2 = back12[:2], back12[2:]
    got1, part1, part2 = together(swap(part1[1], "c"), part1, part2)
    normed2, hidden = saved
    own1, send1 = first_sum(part1[0], got1)
    own1, got1, got2, (buffers, back30, terms30) = together(
        own1,
        swap(send1, "x"),
        swap(part2[1], "c"),
        backward((3, 0), saved, (*kept23[2:4], *kept01[:2]), buffers),
    )
    part3, part0 = back30[:2], back30[2:]
    own2, send2 = first_sum(part2[0], got2)
    sum1 = (own1 + got1.astype(F32)).astype(BF16)
    carried, own2, got2, got3, down = together(
        ring(sum1, nz),
        own2,
        swap(send2, "x"),
        swap(part3[1], "c"),
        dot(cot_rows, hidden, 0, 0).astype(BF16),
    )
    grad_gate_lin, grad_up_lin, out_parts = buffers
    own3, send3 = first_sum(part3[0], got3)
    sum2 = (own2 + got2.astype(F32) + carried.astype(F32)).astype(BF16)
    carried, own3, got3, got0, down_got, gate, grad_up_lin = together(
        ring(sum2, nz),
        own3,
        swap(send3, "x"),
        swap(part0[1], "c"),
        exchange_rows(down),
        dot(normed2, grad_gate_lin, 0, 0).astype(BF16),
        grad_up_lin,
    )
    own0, send0 = first_sum(part0[0], got0)
    sum3 = (own3 + got3.astype(F32) + carried.astype(F32)).astype(BF16)
    down = add_rows(down, down_got)
    gate_got = exchange_rows(gate)
    carried, own0, got0, up = together(
        ring(sum3, nz),
        own0,
        swap(send0, "x"),
        dot(normed2, grad_up_lin, 0, 0).astype(BF16),
    )
    summed2 = own0 + got0.astype(F32) + carried.astype(F32)
    scale2 = kept01[4]
    terms2 = terms12 + terms30

    def norm_back(summed, gain, block, rstd):
        gain = lax.dynamic_slice_in_dim(gain, own_columns * cols, cols, 1)
        mean = summed[rows, :rows].reshape(rows, 1) / width
        return rstd * (summed[:rows] * gain - block.astype(F32) * rstd * mean)

    grad_mid = cotangent.astype(F32) + norm_back(summed2, gain2, mid_block, scale2)
    branch = grad_mid.astype(BF16)
    branch_x = swap(branch, "x")
    branch_c, branch_cx = swap(branch, "c"), swap(branch_x, "c")
    branch_x, branch_c, branch_cx, gate_got, up = together(
        branch_x, branch_c, branch_cx, gate_got, up
    )
    gate = add_rows(gate, gate_got)
    up_got = exchange_rows(up)
    pieces = (branch, branch_c, branch_x, branch_cx)

    grad_att, wo_back = small_call(
        project_back_kernel,
        "project_back",
        6,
        where[0],
        (*pieces, att_t, wo),
        [shape(att_t.shape, BF16), shape(wo.shape, BF16)],
    )
    grad_att = grad_att.reshape(nz * ny, HDIM, rows)
    grad_att, down = together(
        lax.all_to_all(grad_att, ("z", "y"), split_axis=0, concat_axis=0, tiled=True), down
    )
    back, down, up_got, gate = together(
        attend_back(tables, tiles, q_mask, k_mask, grad_att, att, log_norm, cosine, sine),
        spread_z(down),
        up_got,
        gate,
    )
    up = add_rows(up, up_got)
    if nq > 1:
        grad_q = of_queries(back)[:, :HDIM]
        grad_kv = lax.psum_scatter(back[:, HDIM:], "q", scatter_dimension=0, tiled=True)
        back = jnp.concatenate([grad_q, grad_kv], axis=1)
    def qkv_back(s, place):
        chunk = pl.BlockSpec((1, head, rows), lambda i, where: (s, 0, 0))
        specs = {0: pl.BlockSpec((rows, width), lambda i, where: (s, 0)), 1: chunk, 2: chunk}
        return small_call(
            qkv_back_kernel,
            "qkv_back",
            5,
            place,
            (normed1, back, other_back, *w_qkv),
            [shape((2, rows + EXTRA, cols), BF16)] * 2 + [shape((1, width), F32)],
            specs,
        )

    other_back, place = together(swap(back[nz:], "y"), where[1])
    part1, place = together(qkv_back(1, place), where[2])
    got1, part2, qkv_grads, gate, place = together(
        swap(part1[1], "c"),
        qkv_back(2, place),
        small_call(
            qkv_weights_kernel,
            "qkv_weights",
            8,
            place,
            (normed1, back, other_back),
            [shape((nz, ny * head, half), BF16)] * 2,
        ),
        spread_z(gate),
        where[3],
    )
    own1, send1 = first_sum(part1[0], got1)
    own1, got1, got2, part3, qkv_own, qkv_got, place = together(
        own1,
        swap(send1, "x"),
        swap(part2[1], "c"),
        qkv_back(3, place),
        qkv_grads[0],
        exchange_lanes(qkv_grads[1]),
        where[0],
    )
    own2, send2 = first_sum(part2[0], got2)
    sum1 = (own1 + got1.astype(F32)).astype(BF16)
    carried, own2, got2, got3, part0, qkv_grads, up = together(
        ring(sum1, nz),
        own2,
        swap(send2, "x"),
        swap(part3[1], "c"),
        qkv_back(0, place),
        scatter_lanes(qkv_own, qkv_got),
        spread_z(up),
    )
    qkv_grads = spread_z(qkv_grads)
    own3, send3 = first_sum(part3[0], got3)
    sum2 = (own2 + got2.astype(F32) + carried.astype(F32)).astype(BF16)
    terms1 = part0[2] + part1[2] + part2[2] + part3[2]
    terms1 = jnp.concatenate([terms1, terms2], axis=0)
    terms1 = terms1 + swap(terms1, "c")
    carried, own3, got3, got0, terms1, terms1_x = together(
        ring(sum2, nz),
        own3,
        swap(send3, "x"),
        swap(part0[1], "c"),
        terms1,
        swap(terms1, "x"),
    )
    own0, send0 = first_sum(part0[0], got0)
    sum3 = (own3 + got3.astype(F32) + carried.astype(F32)).astype(BF16)
    peak_slots = jnp.zeros((nz * groups, 2 * width // (nz * groups)), F32)
    peak_slots = lax.dynamic_update_slice(
        peak_slots, jnp.broadcast_to(jnp.max(peak), (1, peak_slots.shape[1])), (zi * groups + group, 0)
    )
    terms1 = jnp.stack([terms1 + terms1_x, peak_slots.reshape(2, width)])
    terms1 = sum_small(terms1, ("y", "q"))
    terms1_z = lax.ppermute(terms1, "z", [(i, i ^ 1) for i in range(nz)])
    carried, own0, got0, terms1, terms1_z = together(
        ring(sum3, nz), own0, swap(send0, "x"), terms1, terms1_z
    )
    terms1 = terms1 + terms1_z
    terms1 = terms1 + lax.ppermute(terms1, "z", [(i, i ^ 2) for i in range(nz)])
    summed1 = own0 + got0.astype(F32) + carried.astype(F32)
    grad_in = (grad_mid + norm_back(summed1, gain1, hidden_in, scale1[0])).astype(BF16)

    grad_wd = lay_out(down, True)
    grad_wg = lay_out(gate, False)
    grad_wu = lay_out(up, False)
    branch_ffn = lax.psum_scatter(out_parts, ("z", *NARROW), scatter_dimension=0, tiled=False)
    hidden_out = (residual_mid + branch_ffn.astype(F32)).astype(BF16)
    if nq > 1:
        wo_back = wo_back.reshape(nz * 2, -1, groups // 2, slab).transpose(0, 2, 1, 3)
        wo_back = wo_back.reshape(nz * groups, -1, slab)
    grad_wo = lax.psum_scatter(wo_back, WIDE, scatter_dimension=0, tiled=False).astype(F32)
    grad_qkv = small_call(
        qkv_out_kernel,
        "lay_out_qkv",
        3,
        where[0],
        (qkv_grads,),
        [shape((slab, nz * ny * HDIM), F32)] * 3,
    )

    peaks = terms1[1].reshape(nz * groups, -1)[:, 0]
    gain_terms = terms1[0].reshape(2, 2, nz, half)
    gain_terms = gain_terms.transpose(0, 2, 1, 3).reshape(2, width) / gains
    terms = lax.dynamic_slice_in_dim(gain_terms, (zi * groups + group) * slab, slab, 1)
    peaks = peaks.reshape(nz, nq, ny)
    head_peaks = jnp.max(peaks, axis=1).reshape(nz * ny)
    factor = jnp.sqrt(clip_limit / jnp.maximum(head_peaks, clip_limit))
    column_factor = jnp.repeat(factor, HDIM)
    return (
        hidden_out,
        grad_in,
        grad_qkv[0],
        grad_qkv[1],
        grad_qkv[2],
        grad_wo,
        grad_wg,
        grad_wu,
        grad_wd,
        terms[0],
        terms[1],
        w_query.astype(F32) * column_factor[None, :],
        w_key.astype(F32) * column_factor[None, :],
        head_peaks,
    )


def solution(mesh):
    wide, narrow = mesh.devices.shape
    sizes = (4, wide // 8, 2, narrow // 2, 2)
    fine = Mesh(mesh.devices.reshape(sizes), ("z", "q", "y", "x", "c"))
    both = P(WIDE, NARROW)
    turned = P(NARROW, WIDE)
    return jax.shard_map(
        functools.partial(on_device, sizes),
        mesh=fine,
        in_specs=(
            both, P(WIDE), both, both, both, turned, P(WIDE), both, both, turned, both, P(), P()
        ),
        out_specs=(
            both, both, both, both, both, turned, both, both, turned,
            P(WIDE), P(WIDE), both, both, P(NARROW),
        ),
        check_vma=False,
    )
```

```python
import functools

import jax
import jax.numpy as jnp
from jax import lax
from jax.experimental import pallas as pl
from jax.experimental.pallas import tpu as pltpu
from jax.sharding import Mesh
from jax.sharding import PartitionSpec as P

HDIM = 64
HALF = HDIM // 2

eps_norm = 1e-05
rope_base = 130000.0
clip_limit = 5.0
masked_fill = -1e30

F32 = jnp.float32
BF16 = jnp.bfloat16
WIDE = ("z", "q", "y")
GROUP = ("q", "y")
NARROW = ("x", "c")
VMEM_BYTES = 60 * 2**20
EXTRA = 16


def lookup(lookup_table, indices):
    labels = jnp.arange(lookup_table.shape[0], dtype=jnp.int32)
    return jnp.sum(
        jnp.where(indices[:, None] == labels[None, :], lookup_table[None, :], 0),
        axis=1,
        dtype=jnp.int32,
    )


def segment_tables(segment_ids, parents):
    labels = jnp.arange(parents.shape[0], dtype=jnp.int32)
    counts = jnp.sum(
        (segment_ids[:, None] == labels[None, :]).astype(jnp.int32), axis=0, dtype=jnp.int32
    )
    starts = jnp.sum(
        jnp.where(labels[None, :] < labels[:, None], counts[None, :], 0), axis=1, dtype=jnp.int32
    )
    ancestor = lookup(parents, parents)
    parent_len = jnp.where(parents != labels, lookup(counts, parents), 0)
    ancestor_len = jnp.where(ancestor != parents, lookup(counts, ancestor), 0)
    return (ancestor, starts, parent_len, ancestor_len)


def dot(left, right, left_dim, right_dim):
    return lax.dot_general(
        left, right, (((left_dim,), (right_dim,)), ((), ())), preferred_element_type=F32
    )


def take(array, index, axis=0):
    return lax.dynamic_index_in_dim(array, index, axis, keepdims=False)


def swap(array, axis):
    return lax.ppermute(array, axis, [(0, 1), (1, 0)])


def ring(array, size):
    return lax.ppermute(array, "z", [(i, (i + 1) % size) for i in range(size)])


def pick(flag, first, second):
    return jnp.where(flag == 0, first, second)


def together(*values):
    return lax.optimization_barrier(values)


def params():
    return pltpu.CompilerParams(vmem_limit_bytes=VMEM_BYTES)


def cost(time):
    return pl.CostEstimate(flops=int(time * 1e9), bytes_accessed=1000, transcendentals=0)


def shape(dims, dtype):
    return jax.ShapeDtypeStruct(dims, dtype)


def full(dims):
    return pl.BlockSpec(dims, lambda *_: (0,) * len(dims))


def fill_tiles(sources, mask, held, k_ext, values_t):
    if len(sources) == 1:
        held[...] = sources[0][...]
    else:
        for t, source in enumerate(sources):
            held[t] = source[...]
    for t in range(held.shape[0]):
        tile = held[t].astype(F32)
        spare = k_ext.shape[2] - HDIM - mask.shape[1]
        parts = [tile[HDIM : 2 * HDIM], mask[t].astype(F32)]
        parts.append(jnp.zeros((spare, tile.shape[1]), F32))
        k_ext[t] = jnp.concatenate(parts, axis=0).T.astype(BF16)
        if values_t is not None:
            values_t[t] = jnp.concatenate(
                [tile[2 * HDIM :], jnp.zeros((HDIM, tile.shape[1]), F32)], axis=0
            ).T.astype(BF16)


def query_ext(q, mask, depth):
    spare = depth - HDIM - mask.shape[1]
    return jnp.concatenate([q, mask[0], jnp.zeros((spare, q.shape[1]), BF16)], axis=0)


def attend_kernel(visible, counts, q_pos, k_pos, *refs):
    q_mask, k_mask, low, out, log_norm, peak, held, k_ext = refs[-8:]
    i = pl.program_id(0)
    tiles, _, width = held.shape

    @pl.when(i == 0)
    def _():
        fill_tiles(refs[:-8], k_mask, held, k_ext, None)

    mine = q_pos[pl.num_programs(0) * 2]
    q_tile = query_ext(held[mine + i, :HDIM], q_mask, k_ext.shape[2])
    relative = lax.broadcasted_iota(jnp.int32, (width, width), 0) - lax.broadcasted_iota(
        jnp.int32, (width, width), 1
    )

    def one_tile(j, carry, diagonal):
        high, total, acc = carry
        scores = dot(k_ext[j], q_tile, 1, 0)
        if diagonal:
            scores = jnp.where(relative <= 0, scores, masked_fill)
        new_high = jnp.maximum(high, jnp.max(scores, axis=0, keepdims=True))
        weights = jnp.exp(scores - new_high)
        shrink = jnp.exp(high - new_high)
        total = total * shrink + jnp.sum(weights, axis=0, keepdims=True)
        acc = acc * shrink + dot(held[j, 2 * HDIM :], weights.astype(BF16), 1, 0)
        return new_high, total, acc

    start = (
        jnp.full((1, width), masked_fill, F32),
        jnp.zeros((1, width), F32),
        jnp.zeros((HDIM, width), F32),
    )
    high, total, acc = lax.fori_loop(
        0,
        counts[i],
        lambda n, carry: one_tile(visible[i * tiles + n], carry, False),
        one_tile(mine + i, start, True),
    )
    result = acc / total
    out[0] = result
    low[0] = result.astype(BF16)
    log_norm[0] = high + jnp.log(total)
    peak[0] = high


def attend(tables, tiles, q_mask, k_mask):
    q_tiles, labels, width = q_mask.shape
    k_tiles = k_mask.shape[0]
    part = lambda i, *_: (i, 0, 0)
    placed = lambda i, visible, counts, q_pos, k_pos: (q_pos[i + q_tiles], 0, 0)
    return pl.pallas_call(
        attend_kernel,
        grid_spec=pltpu.PrefetchScalarGridSpec(
            num_scalar_prefetch=4,
            grid=(q_tiles,),
            in_specs=[full(a.shape) for a in tiles]
            + [pl.BlockSpec((1, labels, width), part), full(k_mask.shape)],
            out_specs=[
                pl.BlockSpec((1, HDIM, width), placed),
                pl.BlockSpec((1, HDIM, width), part),
                pl.BlockSpec((1, 1, width), part),
                pl.BlockSpec((1, 1, width), part),
            ],
            scratch_shapes=[
                pltpu.VMEM((k_tiles, 3 * HDIM, width), BF16),
                pltpu.VMEM((k_tiles, width, 2 * HDIM), BF16),
            ],
        ),
        out_shape=[
            shape((q_tiles, HDIM, width), BF16),
            shape((q_tiles, HDIM, width), F32),
            shape((q_tiles, 1, width), F32),
            shape((q_tiles, 1, width), F32),
        ],
        compiler_params=params(),
        cost_estimate=cost(18),
        name="attend",
    )(*tables, *tiles, q_mask, k_mask)


def attend_back_kernel(visible, counts, q_pos, k_pos, *refs):
    q_mask, k_mask, grads, out, log_norm, cosine, sine, back = refs[-13:-5]
    held, k_ext, values_t, acc_k, acc_v = refs[-5:]
    i = pl.program_id(0)
    tiles, _, width = held.shape

    @pl.when(i == 0)
    def _():
        fill_tiles(refs[:-13], k_mask, held, k_ext, values_t)
        acc_k[...] = jnp.zeros_like(acc_k)
        acc_v[...] = jnp.zeros_like(acc_v)

    mine = q_pos[pl.num_programs(0) * 2]
    q_rows = held[mine + i, :HDIM]
    q_tile = query_ext(q_rows, q_mask, k_ext.shape[2])
    g_tile = grads[0]
    g_ext = jnp.concatenate([g_tile, jnp.zeros_like(g_tile)], axis=0)
    lse = log_norm[0]
    delta = jnp.sum(g_tile.astype(F32) * out[0], axis=0, keepdims=True)
    relative = lax.broadcasted_iota(jnp.int32, (width, width), 0) - lax.broadcasted_iota(
        jnp.int32, (width, width), 1
    )

    def one_tile(j, acc, diagonal):
        scores = dot(k_ext[j], q_tile, 1, 0)
        if diagonal:
            scores = jnp.where(relative <= 0, scores, masked_fill)
        probs = jnp.exp(scores - lse)
        grad_probs = dot(values_t[j], g_ext, 1, 0)
        grad_scores = (probs * (grad_probs - delta)).astype(BF16)
        acc_v[j] += dot(g_tile, probs.astype(BF16), 1, 1)
        acc_k[j] += dot(q_rows, grad_scores, 1, 1)
        return acc + dot(held[j, HDIM : 2 * HDIM], grad_scores, 1, 0)

    acc = lax.fori_loop(
        0,
        counts[i],
        lambda n, acc: one_tile(visible[i * tiles + n], acc, False),
        one_tile(mine + i, jnp.zeros((HDIM, width), F32), True),
    )

    def put_unrotated(grad, t, base):
        first, second, c, s = grad[:HALF], grad[HALF:], cosine[t], sine[t]
        back[t, base : base + HALF] = (first * c + second * s).astype(BF16)
        back[t, base + HALF : base + HDIM] = (second * c - first * s).astype(BF16)

    put_unrotated(acc * HDIM ** (-0.5), mine + i, 0)

    @pl.when(i == pl.num_programs(0) - 1)
    def _():
        for t in range(tiles):
            put_unrotated(acc_k[t], t, HDIM)
            back[t, 2 * HDIM :] = acc_v[t].astype(BF16)


def attend_back(tables, tiles, q_mask, k_mask, grads, out, log_norm, cosine, sine):
    q_tiles, labels, width = q_mask.shape
    k_tiles = k_mask.shape[0]
    part = lambda i, *_: (i, 0, 0)
    placed = lambda i, visible, counts, q_pos, k_pos: (q_pos[i + q_tiles], 0, 0)
    return pl.pallas_call(
        attend_back_kernel,
        grid_spec=pltpu.PrefetchScalarGridSpec(
            num_scalar_prefetch=4,
            grid=(q_tiles,),
            in_specs=[full(a.shape) for a in tiles]
            + [
                pl.BlockSpec((1, labels, width), part),
                full(k_mask.shape),
                pl.BlockSpec((1, HDIM, width), placed),
                pl.BlockSpec((1, HDIM, width), part),
                pl.BlockSpec((1, 1, width), part),
                full(cosine.shape),
                full(sine.shape),
            ],
            out_specs=full((k_tiles, 3 * HDIM, width)),
            scratch_shapes=[
                pltpu.VMEM((k_tiles, 3 * HDIM, width), BF16),
                pltpu.VMEM((k_tiles, width, 2 * HDIM), BF16),
                pltpu.VMEM((k_tiles, width, 2 * HDIM), BF16),
                pltpu.VMEM((k_tiles, HDIM, width), F32),
                pltpu.VMEM((k_tiles, HDIM, width), F32),
            ],
        ),
        out_shape=shape((k_tiles, 3 * HDIM, width), BF16),
        compiler_params=params(),
        cost_estimate=cost(22),
        name="attend_back",
    )(*tables, *tiles, q_mask, k_mask, grads, out, log_norm, cosine, sine)


def row_scale(pieces, width):
    squares = 0.0
    for piece in pieces:
        values = piece[...].astype(F32)
        squares = squares + jnp.sum(values * values, axis=1, keepdims=True)
    return lax.rsqrt(squares / width + eps_norm)


def aligned(start, size):
    return pl.ds(pl.multiple_of(start, size), size)


def block_of(where, k):
    return where[0] ^ k


def half_columns(where, h, wide):
    return aligned((h ^ where[1]) * wide, wide)


def put_normed(where, pieces, rstd, gain, normed):
    cols = pieces[0].shape[1]
    half = cols // 2
    for k, piece in enumerate(pieces):
        block = block_of(where, k)
        values = piece[...].astype(F32) * rstd * gain[:, aligned(block * cols, cols)]
        for part in range(2):
            columns = aligned((part * 4 + block) * half, half)
            normed[:, columns] = values[:, part * half : (part + 1) * half].astype(BF16)


def qkv_kernel(where, *refs):
    pieces, (gain, w_first, w_second, cosine, sine) = refs[:4], refs[4:9]
    normed, mine, other, scale = refs[-4:]
    rows, cols = pieces[0].shape
    half = cols // 2
    rstd = row_scale(pieces, 4 * cols)
    scale[...] = rstd
    put_normed(where, pieces, rstd, gain, normed)
    c, s = cosine[...], sine[...]
    features = 3 * HDIM
    for out, head in ((mine, where[2]), (other, 1 - where[2])):
        span = aligned(head * features, features)
        lin = 0.0
        for h, weights in enumerate((w_first, w_second)):
            for z in range(4):
                columns = aligned(((h ^ where[1]) * 4 + z) * half, half)
                lin = lin + dot(weights[z, span, :], normed[:, columns], 1, 1)
        for part, factor in ((0, HDIM ** (-0.5)), (1, 1.0)):
            base = part * HDIM
            first, second = lin[base : base + HALF], lin[base + HALF : base + HDIM]
            out[base : base + HALF] = ((first * c - second * s) * factor).astype(BF16)
            out[base + HALF : base + HDIM] = ((second * c + first * s) * factor).astype(BF16)
        out[2 * HDIM :] = lin[2 * HDIM :].astype(BF16)


def chunk_call(
    kernel, name, time, where, s, inputs, buffers, whole_shapes, out_shapes, scratch=(), out_there=0
):
    def spec(dims, how):
        rest = (0,) * (len(dims) - 1)
        if how == "whole":
            return full(dims)
        if how == "there":
            return pl.BlockSpec(memory_space=pl.ANY)
        block = (dims[0] // 4, *dims[1:])
        if how == "chunk":
            return pl.BlockSpec(block, lambda i, where: (s, *rest))
        return pl.BlockSpec(block, lambda i, where: (where[3], *rest))

    in_specs = [spec(a.shape, how) for a, how in inputs]
    arrays = [a for a, _ in inputs]
    aliases = {}
    if buffers is not None:
        for n, buffer in enumerate(buffers):
            aliases[1 + len(arrays)] = n
            in_specs.append(pl.BlockSpec(memory_space=pl.ANY))
            arrays.append(buffer)
    out_specs = [spec(dims, how) for dims, how in whole_shapes]
    out_specs += [
        pl.BlockSpec(memory_space=pl.ANY) if n < out_there else full(a.shape)
        for n, a in enumerate(out_shapes)
    ]
    return pl.pallas_call(
        kernel,
        grid_spec=pltpu.PrefetchScalarGridSpec(
            num_scalar_prefetch=1,
            grid=(1,),
            in_specs=in_specs,
            out_specs=out_specs,
            scratch_shapes=list(scratch),
        ),
        out_shape=[shape(dims, BF16) for dims, _ in whole_shapes] + list(out_shapes),
        input_output_aliases=aliases,
        compiler_params=params(),
        cost_estimate=cost(time),
        name=name,
    )(where, *arrays)


def fetch(weights, held, sems, first=0, start=0):
    copies = []
    for n, weight in enumerate(weights):
        rows = weight.shape[0]
        copies.append(
            pltpu.make_async_copy(weight, held.at[pl.ds(start, rows)], sems.at[first + n])
        )
        copies[-1].start()
        start += rows
    return copies


class Sends:
    def __init__(self, sems):
        self.sems, self.copies = sems, []

    def start(self, source, target):
        self.copies.append(pltpu.make_async_copy(source, target, self.sems.at[len(self.copies)]))
        self.copies[-1].start()

    def wait(self):
        for copy in self.copies:
            copy.wait()


def load(pairs, sems, first):
    copies = [
        pltpu.make_async_copy(source, target, sems.at[first + n])
        for n, (source, target) in enumerate(pairs)
    ]
    for copy in copies:
        copy.start()
    return copies


def wait_all(copies):
    for copy in copies:
        copy.wait()


def ffn_kernel(chunks, count, where, *refs):
    pieces, gain, weights = refs[:8], refs[8], refs[9 : 9 + count]
    outs = refs[-16:-8]
    mids, normed_all, hidden_all, gates_all, ups_all, held, sems, out_sems = refs[-8:]
    normed_out, hidden_out, scales = outs[0], outs[1], outs[6:]
    rows, cols = mids.shape[2:]
    units, wide = hidden_all.shape[2], 2 * cols
    come = [
        load([(pieces[4 * i + k], mids.at[i, k]) for k in range(4)], sems, count + 4 * i)
        for i in range(2)
    ]
    copies = fetch(weights, held, sems)
    sends = Sends(out_sems)
    step = 256
    for i in range(2):
        chunk = pl.ds(chunks[i] * rows, rows)
        normed, hidden = normed_all.at[i], hidden_all.at[i]
        gates, ups = gates_all.at[i], ups_all.at[i]
        gates_out, ups_out = outs[2 + 2 * i], outs[3 + 2 * i]
        wait_all(come[i])
        blocks = [mids.at[i, k] for k in range(4)]
        rstd = row_scale(blocks, 4 * cols)
        scales[i][...] = rstd
        put_normed(where, blocks, rstd, gain, normed)
        sends.start(normed, normed_out.at[chunk])
        if i == 0:
            wait_all(copies)
        for n in range(0, units, step):
            span = slice(n, n + step)
            columns = pl.ds(n, step)
            gate = up = 0.0
            for h in range(2):
                values = normed[:, half_columns(where, h, wide)]
                gate = gate + dot(values, held[h * wide : (h + 1) * wide, span], 1, 0)
                up = up + dot(values, held[(h + 2) * wide : (h + 3) * wide, span], 1, 0)
            gates[:, span] = gate
            ups[:, span] = up
            sends.start(gates.at[:, columns], gates_out.at[:, columns])
            sends.start(ups.at[:, columns], ups_out.at[:, columns])
            hidden[:, span] = (gate * jax.nn.sigmoid(gate) * up).astype(BF16)
            sends.start(hidden.at[:, columns], hidden_out.at[chunk, columns])
    sends.wait()


def arrange_kernel(zs, cots, cot_rows):
    cols = cots.shape[2]
    half = cols // 2
    for block in range(4):
        for part in range(2):
            start = (part * 4 + block) * half
            cot_rows[:, start : start + half] = cots[block, :, part * half : (part + 1) * half]


def arrange(cot, zs):
    blocks, rows, cols = cot.shape
    return pl.pallas_call(
        arrange_kernel,
        grid_spec=pltpu.PrefetchScalarGridSpec(
            num_scalar_prefetch=1,
            grid=(4,),
            in_specs=[pl.BlockSpec((blocks // 4, rows, cols), lambda s, zs: (zs[s], 0, 0))],
            out_specs=pl.BlockSpec((rows, 4 * cols), lambda s, zs: (s, 0)),
        ),
        out_shape=shape((4 * rows, 4 * cols), BF16),
        compiler_params=params(),
        cost_estimate=cost(5),
        name="arrange",
    )(zs, cot)


def ffn_back_kernel(chunks, downs, count, where, *refs):
    weights, kept = refs[:count], refs[count : count + 4]
    all_cot, all_hidden, all_normed = refs[count + 4 : count + 7]
    grad_gate_out, grad_up_out = refs[-20:-18]
    backs, gain_term = refs[-18:-14], refs[-14]
    held, cot_all, gate_up, hidden_in, normed_in, sems = refs[-13:-7]
    grad_gates, grad_ups, out_held, back_held, lines, out_sems, line_sems = refs[-7:]
    rows, units = grad_gates.shape[1:]
    cols = out_held.shape[3]
    half, wide = cols // 2, 2 * cols
    step = 256
    spans = [pl.ds(s * rows, rows) for s in chunks]
    early = load([(all_cot.at[spans[0]], cot_all.at[0])], sems, count)
    early += fetch(weights[:downs], held, sems)
    early += load([(kept[0], gate_up.at[0, 0]), (kept[1], gate_up.at[0, 1])], sems, count + 1)
    late = load(
        [(all_hidden.at[spans[0]], hidden_in.at[0]), (all_normed.at[spans[0]], normed_in.at[0])],
        sems,
        count + 3,
    )
    late += fetch(weights[downs:], held, sems, downs, 2 * wide)
    second = load(
        [
            (all_cot.at[spans[1]], cot_all.at[1]),
            (kept[2], gate_up.at[1, 0]),
            (kept[3], gate_up.at[1, 1]),
            (all_hidden.at[spans[1]], hidden_in.at[1]),
            (all_normed.at[spans[1]], normed_in.at[1]),
        ],
        sems,
        count + 5,
    )
    sends, tails = Sends(out_sems), Sends(line_sems)
    for i in range(2):
        cot_rows, hidden, normed = cot_all.at[i], hidden_in.at[i], normed_in.at[i]
        gates, ups = gate_up.at[i, 0], gate_up.at[i, 1]
        grad_gate, grad_up = grad_gates.at[i], grad_ups.at[i]
        wait_all(early if i == 0 else second)
        for n in range(0, units, step):
            span = slice(n, n + step)
            columns = pl.ds(n, step)
            grad_hidden = 0.0
            for h in range(2):
                grad_hidden = grad_hidden + dot(
                    cot_rows[:, half_columns(where, h, wide)],
                    held[h * wide : (h + 1) * wide, span],
                    1,
                    0,
                )
            gate, up = gates[:, span], ups[:, span]
            sigmoid = jax.nn.sigmoid(gate)
            grad_gate[:, span] = (
                grad_hidden * up * sigmoid * (1.0 + gate * (1.0 - sigmoid))
            ).astype(BF16)
            grad_up[:, span] = (grad_hidden * (gate * sigmoid)).astype(BF16)
            sends.start(grad_gate.at[:, columns], grad_gate_out.at[spans[i], columns])
            sends.start(grad_up.at[:, columns], grad_up_out.at[spans[i], columns])
        if i == 0:
            wait_all(late)
        row_term = 0.0
        for k in range(4):
            block = block_of(where, k)
            back = backs[2 * i + k % 2]
            for h in range(2):
                part = aligned((h ^ where[1]) * half, half)
                of_down, of_gate, of_up = [
                    held[aligned((n + h) * wide + block * half, half), :] for n in (0, 2, 4)
                ]
                out_held[i, k, :, part] = dot(hidden[...], of_down, 1, 1).astype(BF16)
                partial = dot(grad_gate[...], of_gate, 1, 1) + dot(grad_up[...], of_up, 1, 1)
                back_held[i, k, :, part] = partial.astype(BF16)
                columns = aligned(((h ^ where[1]) * 4 + block) * half, half)
                terms = partial * normed[:, columns].astype(F32)
                column_term = jnp.sum(terms, axis=0, keepdims=True)
                if i == 0:
                    gain_term[:, columns] = column_term
                else:
                    gain_term[:, columns] += column_term
                row_term = row_term + jnp.sum(terms, axis=1, keepdims=True)
            sends.start(out_held.at[i, k], back.at[k // 2, pl.ds(rows + EXTRA, rows)])
            sends.start(back_held.at[i, k], back.at[k // 2, pl.ds(0, rows)])
        lines[i] = row_line(row_term, cols)
        for back in backs[2 * i : 2 * i + 2]:
            for x in range(2):
                tails.start(lines.at[i], back.at[x, pl.ds(rows, EXTRA)])
    sends.wait()
    tails.wait()


def row_line(row_term, cols):
    rows = row_term.shape[0]
    line = jnp.broadcast_to(row_term, (rows, 128)).T[:EXTRA]
    return jnp.concatenate([line, jnp.zeros((EXTRA, cols - rows), F32)], axis=1).astype(BF16)


def put_row_term(row_term, cols, keep, send):
    rows = row_term.shape[0]
    line = row_line(row_term, cols)
    for ref in (keep, send):
        ref[0, rows:] = line
        ref[1, rows:] = line


def qkv_back_kernel(where, normed, mine, other, w_first, w_second, keep, send, gain_term):
    rows, cols = normed.shape[0], keep.shape[2]
    half = cols // 2
    features = 3 * HDIM
    row_term = 0.0
    for k in range(4):
        block = block_of(where, k)
        back = (keep, send)[k % 2]
        for h, weights in enumerate((w_first, w_second)):
            part = aligned((h ^ where[1]) * half, half)
            partial = 0.0
            for grads, head in ((mine, where[2]), (other, 1 - where[2])):
                span = aligned(head * features, features)
                partial = partial + dot(grads[0], weights[block, span, :], 0, 0)
            back[k // 2, :rows, part] = partial.astype(BF16)
            columns = aligned(((h ^ where[1]) * 4 + block) * half, half)
            terms = partial * normed[:, columns].astype(F32)
            gain_term[:, columns] = jnp.sum(terms, axis=0, keepdims=True)
            row_term = row_term + jnp.sum(terms, axis=1, keepdims=True)
    put_row_term(row_term, cols, keep, send)


def qkv_weights_kernel(where, normed, *refs):
    own, other, outs = refs[0], refs[1], refs[2:]
    count = other.shape[0]
    half = outs[0].shape[2]
    rows, features = own.shape[2], 3 * HDIM
    for h, out in enumerate(outs):
        for z in range(4):
            columns = aligned(((h ^ where[1]) * 4 + z) * half, half)
            for grads, head in ((own, where[2]), (other, 1 - where[2])):
                total = 0.0
                for s in range(count):
                    total = total + dot(
                        grads[s], normed[s * rows : (s + 1) * rows, columns], 1, 0
                    )
                out[z, aligned(head * features, features), :] = total.astype(BF16)


def project_kernel(where, attended, weights, keep, send):
    half = weights.shape[2]
    for k in range(4):
        for part in range(2):
            (keep, send)[k % 2][k // 2, :, part * half : (part + 1) * half] = dot(
                attended[...], weights[block_of(where, k) * 2 + part], 0, 0
            ).astype(BF16)


def project_back_kernel(where, p0, p1, p2, p3, attended, weights, grad_att, grad_weights):
    half = weights.shape[2]
    total = 0.0
    for k, piece in enumerate((p0, p1, p2, p3)):
        for part in range(2):
            b = block_of(where, k) * 2 + part
            values = piece[:, part * half : (part + 1) * half]
            total = total + dot(weights[b], values, 1, 1)
            grad_weights[b] = dot(attended[...], values, 1, 0).astype(BF16)
    grad_att[...] = total.astype(BF16)


def columns_kernel(parts, out):
    out[...] = parts[0].astype(F32)


def turned_kernel(parts, out):
    out[...] = parts[0].astype(F32).T


def lay_out(parts, turned):
    nz, n, m = parts.shape
    if turned:
        kernel, dims, block, place = turned_kernel, (nz * m, n), (m, n), lambda z: (z, 0)
    else:
        kernel, dims, block, place = columns_kernel, (n, nz * m), (n, m), lambda z: (0, z)
    return pl.pallas_call(
        kernel,
        grid=(nz,),
        in_specs=[pl.BlockSpec((1, n, m), lambda z: (z, 0, 0))],
        out_specs=pl.BlockSpec(block, place),
        out_shape=shape(dims, F32),
        compiler_params=params(),
        cost_estimate=cost(2),
        name="lay_out",
    )(parts)


def qkv_out_kernel(where, parts, *outs):
    features = 3 * HDIM
    for z in range(parts.shape[0]):
        for n, out in enumerate(outs):
            heads = [parts[z, h * features + n * HDIM : h * features + (n + 1) * HDIM] for h in (0, 1)]
            both = jnp.concatenate(heads, axis=0).astype(F32)
            out[:, z * 2 * HDIM : (z + 1) * 2 * HDIM] = both.T


def small_call(kernel, name, time, where, inputs, out_shapes, specs=None):
    specs = specs or {}
    return pl.pallas_call(
        kernel,
        grid_spec=pltpu.PrefetchScalarGridSpec(
            num_scalar_prefetch=1,
            grid=(1,),
            in_specs=[specs.get(n) or full(a.shape) for n, a in enumerate(inputs)],
            out_specs=[full(s.shape) for s in out_shapes],
        ),
        out_shape=list(out_shapes),
        compiler_params=params(),
        cost_estimate=cost(time),
        name=name,
    )(where, *inputs)


def on_device(
    sizes,
    hidden_in,
    gain_attn,
    w_query,
    w_key,
    w_value,
    w_out,
    gain_ffn,
    w_gate,
    w_up,
    w_down,
    cotangent,
    segment_ids,
    parents,
):
    nz, nq, ny, nx, nc = sizes
    rows, cols = hidden_in.shape
    groups = nq * ny
    group_rows = nz * rows
    width = cols * nx * nc
    half = cols // 2
    slab = gain_attn.shape[0]
    head = 3 * HDIM
    units = w_gate.shape[1] // nz

    zi, qi, yi, xi, ci = [lax.axis_index(a) for a in ("z", "q", "y", "x", "c")]
    group = qi * ny + yi
    own_columns = xi * nc + ci
    zs = [(zi - s) % nz for s in range(nz)]
    flip = yi if nq == 1 else 0 * yi
    where = [jnp.stack([own_columns, flip, yi, z]).astype(jnp.int32) for z in zs]

    def scatter_narrow(keep, send):
        held = keep.astype(F32) + swap(send, "c").astype(F32)
        return held[0] + swap(held[1].astype(BF16), "x").astype(F32)

    def first_sum(keep, received):
        held = keep.astype(F32) + received.astype(F32)
        return held[0], held[1].astype(BF16)

    def spread_z(parts):
        return lax.all_to_all(parts, "z", split_axis=0, concat_axis=0, tiled=True)

    def gather_rows(parts):
        n = parts.shape[2]
        if nq == 1:
            return parts.reshape(-1, n), swap(parts, "y").reshape(-1, n)
        got = lax.all_gather(parts, GROUP, axis=0, tiled=False)
        got = got.reshape(2, groups // 2, nz, slab, n).transpose(0, 2, 1, 3, 4)
        return tuple(got.reshape(2, nz * half, n))

    def swap_part(parts, n):
        part = parts[n * nz // 2 : (n + 1) * nz // 2]
        return swap(part, "y") if nq == 1 else part

    def join_rows(parts, swapped):
        if nq > 1:
            return gather_rows(parts)
        return [a.reshape(-1, units) for a in (parts, *swapped)]

    def gather_lanes(parts):
        n = parts.shape[1]
        if nq == 1:
            return parts, swap(parts, "y")
        got = lax.all_gather(parts, GROUP, axis=0, tiled=False)
        got = got.reshape(2, groups // 2, nz, n, slab).transpose(0, 2, 3, 1, 4)
        return tuple(got.reshape(2, nz, n, half))

    def exchange_rows(grad):
        if nq == 1:
            return swap(take(grad.reshape(2, -1, grad.shape[1]), 1 - yi), "y")
        n = grad.shape[1]
        parts = grad.reshape(2, nz, groups // 2, slab, n).transpose(0, 2, 1, 3, 4)
        return lax.psum_scatter(
            parts.reshape(groups, nz, slab, n), GROUP, scatter_dimension=0, tiled=False
        )

    def add_rows(grad, received):
        if nq == 1:
            own = take(grad.reshape(2, -1, grad.shape[1]), yi)
            received = (own.astype(F32) + received.astype(F32)).astype(BF16)
        return received.reshape(nz, slab, -1)

    def exchange_lanes(second):
        return swap(second, "y") if nq == 1 else second

    def scatter_lanes(first, second):
        n = first.shape[1]
        if nq == 1:
            return (first.astype(F32) + second.astype(F32)).astype(BF16)
        both = jnp.stack([first, second]).reshape(2, nz, n, groups // 2, slab)
        both = both.transpose(0, 3, 1, 2, 4).reshape(groups, nz, n, slab)
        return lax.psum_scatter(both, GROUP, scatter_dimension=0, tiled=False)

    def sum_small(values, axes):
        for axis in axes:
            if axis == "z":
                for bit in (1, 2):
                    values = values + lax.ppermute(values, "z", [(i, i ^ bit) for i in range(nz)])
            elif axis == "q":
                values = lax.psum(values, "q") if nq > 1 else values
            else:
                values = values + swap(values, axis)
        return values

    stacked = jnp.stack([w_query, w_key, w_value]).reshape(3, slab, nz, ny, HDIM)
    stacked = stacked.transpose(2, 3, 0, 4, 1).reshape(nz, ny * head, slab)
    both_gains = jnp.concatenate(
        [gain_attn[None], gain_ffn[None], jnp.zeros((EXTRA - 2, slab), BF16)], axis=0
    )
    both_gains = jnp.broadcast_to(both_gains[None], (nz, EXTRA, slab))
    stacked = jnp.concatenate([stacked, both_gains], axis=1)
    z1, x0, c0, stacked, segment_ids, parents = together(
        ring(hidden_in, nz),
        swap(hidden_in, "x"),
        swap(hidden_in, "c"),
        stacked,
        segment_ids,
        parents,
    )

    ancestor, starts, parent_len, ancestor_len = segment_tables(segment_ids, parents)
    q_blocks = [(z * nq + qi) * ny + (yi ^ dy) for dy in range(ny) for z in zs]
    k_blocks = [(z * nq + q) * ny + (yi ^ dy) for q in range(nq) for dy in range(ny) for z in zs]
    segments = segment_ids.reshape(-1, rows)
    k_seg = jnp.stack([take(segments, b) for b in k_blocks])
    k_pos = jnp.stack(k_blocks).astype(jnp.int32)
    q_tiles, k_tiles = len(q_blocks), len(k_blocks)
    of_queries = lambda a: lax.dynamic_slice_in_dim(a, qi * q_tiles, q_tiles, 0)
    flat = k_seg.reshape(-1)
    labels = jnp.arange(-(-parents.shape[0] // 16) * 16, dtype=jnp.int32)[None, :, None]
    places = k_pos[:, None] * rows + jnp.arange(rows, dtype=jnp.int32)[None]
    places = places + lookup(parent_len + ancestor_len - starts, flat).reshape(k_tiles, rows)
    k_own = labels == k_seg[:, None]
    q_seen = of_queries(
        k_own
        | (labels == lookup(parents, flat).reshape(k_tiles, 1, rows))
        | (labels == lookup(ancestor, flat).reshape(k_tiles, 1, rows))
    )
    q_mask = jnp.where(q_seen, 0.0, masked_fill).astype(BF16)
    k_mask = k_own.astype(BF16)
    q_pos = of_queries(k_pos)
    shown = jnp.any(jnp.any(q_seen, axis=2)[:, None] & jnp.any(k_own, axis=2)[None], axis=2)
    shown = shown & (k_pos[None, :] < q_pos[:, None])
    number = jnp.arange(k_tiles, dtype=jnp.int32)
    earlier = number[None, None, :] < number[None, :, None]
    before = jnp.sum((shown[:, None, :] & earlier).astype(jnp.int32), axis=2)
    chosen = shown[:, None, :] & (before[:, None, :] == number[None, :, None])
    visible = jnp.sum(jnp.where(chosen, number[None, None, :], 0), axis=2, dtype=jnp.int32)
    slots = jnp.stack([z * ny + (yi ^ dy) for dy in range(ny) for z in zs]).astype(jnp.int32)
    q_info = jnp.concatenate([q_pos, slots, (qi * q_tiles).reshape(1).astype(jnp.int32)])
    tables = (
        visible.reshape(-1),
        jnp.sum(shown.astype(jnp.int32), axis=1, dtype=jnp.int32),
        q_info,
        k_pos,
    )
    frequency = rope_base ** (-2.0 * jnp.arange(HALF, dtype=F32) / HDIM)
    angles = places.astype(F32)[:, None, :] * frequency[None, :, None]
    cosine, sine = jnp.cos(angles), jnp.sin(angles)
    cos_q, sin_q = of_queries(cosine), of_queries(sine)

    z2, x1, c1, cx0, w_qkv, (tables, q_mask, k_mask, cosine, sine, cos_q, sin_q) = together(
        ring(z1, nz),
        swap(z1, "x"),
        swap(z1, "c"),
        swap(x0, "c"),
        spread_z(stacked),
        (tables, q_mask, k_mask, cosine, sine, cos_q, sin_q),
    )
    z3, x2, c2, cx1, w_qkv, w_gate_, cotangent_, w_out_ = together(
        ring(z2, nz),
        swap(z2, "x"),
        swap(z2, "c"),
        swap(x1, "c"),
        gather_lanes(w_qkv),
        w_gate,
        cotangent,
        w_out,
    )
    x3, c3, cx2 = swap(z3, "x"), swap(z3, "c"), swap(x2, "c")
    x_chunks = [
        (hidden_in, c0, x0, cx0),
        (z1, c1, x1, cx1),
        (z2, c2, x2, cx2),
        (z3, c3, x3, swap(x3, "c")),
    ]
    gains = [w[:, ny * head : ny * head + 2].astype(F32) for w in w_qkv]
    gains = jnp.stack([pick(flip, *gains), pick(flip, gains[1], gains[0])], axis=1)
    gains = gains.transpose(2, 0, 1, 3).reshape(2, width)
    gain1, gain2 = gains[:1], gains[1:]

    wo = lax.all_gather(w_out_, WIDE, axis=0, tiled=False)
    if nq > 1:
        wo = wo.reshape(nz * 2, groups // 2, -1, slab).transpose(0, 2, 1, 3)
        wo = wo.reshape(nz * 2, -1, half)
    of_units = lambda w: spread_z(w.reshape(slab, nz, units).transpose(1, 0, 2))
    cot = lax.all_gather(cotangent_, ("z", *NARROW), axis=0, tiled=False)

    buffers, mine, theirs, scale1 = None, [], [], []
    for s in range(nz):
        normed1, own, other, scale = chunk_call(
            qkv_kernel,
            "qkv",
            5,
            where[s],
            s,
            [(a, "whole") for a in (*x_chunks[s], gain1, *w_qkv, cos_q[s], sin_q[s])],
            buffers,
            [((group_rows, width), "chunk")],
            [shape((head, rows), BF16), shape((head, rows), BF16), shape((rows, 1), F32)],
        )
        buffers = [normed1]
        mine.append(own)
        theirs.append(swap(other, "y"))
        scale1.append(scale)
    tiles, gate_parts, w_up_, w_down_ = together(
        mine + theirs, of_units(w_gate_), w_up, w_down.T
    )
    if nq > 1:
        tiles = [lax.all_gather(jnp.stack(tiles), "q", axis=0, tiled=True)]
    (att_low, att, log_norm, peak), up_parts, w_gates, w_down_ = together(
        attend(tables, tiles, q_mask, k_mask), of_units(w_up_), gather_rows(gate_parts), w_down_
    )

    att_t = lax.all_to_all(att_low, ("z", "y"), split_axis=0, concat_axis=0, tiled=True)
    att_t, w_down_ = together(att_t, w_down_)
    att_t = att_t.reshape(nz * ny * HDIM, rows)
    keep, send = small_call(
        project_kernel,
        "project",
        4,
        where[0],
        (att_t, wo),
        [shape((2, rows, cols), BF16)] * 2,
    )
    residual_mid = hidden_in.astype(F32) + scatter_narrow(keep, send)
    down_parts = of_units(w_down_)
    mid_block = residual_mid.astype(BF16)

    def forward(chunks, pieces, buffers):
        results = chunk_call(
            functools.partial(ffn_kernel, chunks, len(w_gates) + len(w_ups)),
            "feed_forward",
            9,
            where[0],
            0,
            [(a, "there") for a in pieces]
            + [(gain2, "whole")]
            + [(w, "there") for w in (*w_gates, *w_ups)],
            buffers,
            [((group_rows, width), "there"), ((group_rows, units), "there")],
            [shape((rows, units), F32)] * 4 + [shape((rows, 1), F32)] * 2,
            [
                pltpu.VMEM((2, 4, rows, cols), BF16),
                pltpu.VMEM((2, rows, width), BF16),
                pltpu.VMEM((2, rows, units), BF16),
                pltpu.VMEM((2, rows, units), F32),
                pltpu.VMEM((2, rows, units), F32),
                pltpu.VMEM((8 * cols, units), BF16),
                pltpu.SemaphoreType.DMA((len(w_gates) + len(w_ups) + 8,)),
                pltpu.SemaphoreType.DMA((2 + 6 * units // 256,)),
            ],
            4,
        )
        return results[:2], results[2:]

    def backward(chunks, saved, kept, buffers):
        weights = (*w_downs, *w_gates, *w_ups)
        results = chunk_call(
            functools.partial(ffn_back_kernel, chunks, len(w_downs), len(weights)),
            "feed_forward_back",
            15,
            where[0],
            0,
            [(a, "there") for a in (*weights, *kept, cot_rows, saved[1], saved[0])],
            buffers,
            [
                ((group_rows, units), "there"),
                ((group_rows, units), "there"),
            ],
            [shape((2, 2 * rows + EXTRA, cols), BF16)] * 4 + [shape((1, width), F32)],
            [
                pltpu.VMEM((12 * cols, units), BF16),
                pltpu.VMEM((2, rows, width), BF16),
                pltpu.VMEM((2, 2, rows, units), F32),
                pltpu.VMEM((2, rows, units), BF16),
                pltpu.VMEM((2, rows, width), BF16),
                pltpu.SemaphoreType.DMA((len(weights) + 10,)),
                pltpu.VMEM((2, rows, units), BF16),
                pltpu.VMEM((2, rows, units), BF16),
                pltpu.VMEM((2, 4, rows, cols), BF16),
                pltpu.VMEM((2, 4, rows, cols), BF16),
                pltpu.VMEM((2, EXTRA, cols), BF16),
                pltpu.SemaphoreType.DMA((16 + 4 * units // 256,)),
                pltpu.SemaphoreType.DMA((8,)),
            ],
            4,
        )
        return results[:2], results[2:6], results[6]

    z0 = mid_block
    z1, x0, c0, up_a = together(
        ring(z0, nz), swap(z0, "x"), swap(z0, "c"), swap_part(up_parts, 0)
    )
    z2, x1, c1, cx0, up_b, down_parts = together(
        ring(z1, nz),
        swap(z1, "x"),
        swap(z1, "c"),
        swap(x0, "c"),
        swap_part(up_parts, 1),
        down_parts,
    )
    w_ups = join_rows(up_parts, (up_a, up_b))
    z3, x2, c2, cx1, down_a, cot_rows = together(
        ring(z2, nz),
        swap(z2, "x"),
        swap(z2, "c"),
        swap(x1, "c"),
        swap_part(down_parts, 0),
        arrange(cot, jnp.stack(zs).astype(jnp.int32)),
    )
    x3, c3, cx2, down_b, (saved, kept01) = together(
        swap(z3, "x"),
        swap(z3, "c"),
        swap(x2, "c"),
        swap_part(down_parts, 1),
        forward((0, 1), (z0, c0, x0, cx0, z1, c1, x1, cx1), None),
    )
    w_downs = join_rows(down_parts, (down_a, down_b))
    cx3 = swap(x3, "c")
    saved, kept23 = forward((2, 3), (z2, c2, x2, cx2, z3, c3, x3, cx3), saved)
    buffers, back12, terms12 = backward((1, 2), saved, (*kept01[2:4], *kept23[:2]), None)
    part1, part2 = back12[:2], back12[2:]
    got1, part1, part2 = together(swap(part1[1], "c"), part1, part2)
    normed2, hidden = saved
    own1, send1 = first_sum(part1[0], got1)
    own1, got1, got2, (buffers, back30, terms30) = together(
        own1,
        swap(send1, "x"),
        swap(part2[1], "c"),
        backward((3, 0), saved, (*kept23[2:4], *kept01[:2]), buffers),
    )
    part3, part0 = back30[:2], back30[2:]
    own2, send2 = first_sum(part2[0], got2)
    sum1 = (own1 + got1.astype(F32)).astype(BF16)
    carried, own2, got2, got3, down = together(
        ring(sum1, nz),
        own2,
        swap(send2, "x"),
        swap(part3[1], "c"),
        dot(cot_rows, hidden, 0, 0).astype(BF16),
    )
    grad_gate_lin, grad_up_lin = buffers
    own3, send3 = first_sum(part3[0], got3)
    sum2 = (own2 + got2.astype(F32) + carried.astype(F32)).astype(BF16)
    carried, own3, got3, got0, down_got, gate, grad_up_lin = together(
        ring(sum2, nz),
        own3,
        swap(send3, "x"),
        swap(part0[1], "c"),
        exchange_rows(down),
        dot(normed2, grad_gate_lin, 0, 0).astype(BF16),
        grad_up_lin,
    )
    own0, send0 = first_sum(part0[0], got0)
    sum3 = (own3 + got3.astype(F32) + carried.astype(F32)).astype(BF16)
    down = add_rows(down, down_got)
    gate_got = exchange_rows(gate)
    carried, own0, got0, up = together(
        ring(sum3, nz),
        own0,
        swap(send0, "x"),
        dot(normed2, grad_up_lin, 0, 0).astype(BF16),
    )
    summed2 = own0 + got0.astype(F32) + carried.astype(F32)
    scale2 = kept01[4]
    terms2 = terms12 + terms30

    def norm_back(summed, gain, block, rstd):
        gain = lax.dynamic_slice_in_dim(gain, own_columns * cols, cols, 1)
        mean = summed[rows, :rows].reshape(rows, 1) / width
        return rstd * (summed[:rows] * gain - block.astype(F32) * rstd * mean)

    grad_mid = cotangent.astype(F32) + norm_back(summed2, gain2, mid_block, scale2)
    branch = grad_mid.astype(BF16)
    branch_x = swap(branch, "x")
    branch_c, branch_cx = swap(branch, "c"), swap(branch_x, "c")
    branch_x, branch_c, branch_cx, gate_got, up = together(
        branch_x, branch_c, branch_cx, gate_got, up
    )
    gate = add_rows(gate, gate_got)
    up_got = exchange_rows(up)
    pieces = (branch, branch_c, branch_x, branch_cx)

    grad_att, wo_back = small_call(
        project_back_kernel,
        "project_back",
        6,
        where[0],
        (*pieces, att_t, wo),
        [shape(att_t.shape, BF16), shape(wo.shape, BF16)],
    )
    grad_att, wo_back, down = together(grad_att, wo_back, spread_z(down))
    grad_att = grad_att.reshape(nz * ny, HDIM, rows)
    grad_att, gate = together(
        lax.all_to_all(grad_att, ("z", "y"), split_axis=0, concat_axis=0, tiled=True), gate
    )
    gate = spread_z(gate)
    back, up_got, up = together(
        attend_back(tables, tiles, q_mask, k_mask, grad_att, att, log_norm, cosine, sine),
        up_got,
        up,
    )
    up = add_rows(up, up_got)
    if nq > 1:
        grad_q = of_queries(back)[:, :HDIM]
        grad_kv = lax.psum_scatter(back[:, HDIM:], "q", scatter_dimension=0, tiled=True)
        back = jnp.concatenate([grad_q, grad_kv], axis=1)
    def qkv_back(s, place):
        chunk = pl.BlockSpec((1, head, rows), lambda i, where: (s, 0, 0))
        specs = {0: pl.BlockSpec((rows, width), lambda i, where: (s, 0)), 1: chunk, 2: chunk}
        return small_call(
            qkv_back_kernel,
            "qkv_back",
            5,
            place,
            (normed1, back, other_back, *w_qkv),
            [shape((2, rows + EXTRA, cols), BF16)] * 2 + [shape((1, width), F32)],
            specs,
        )

    other_back, place, gate = together(swap(back[nz:], "y"), where[1], gate)
    part1, place = together(qkv_back(1, place), where[2])
    got1, part2, qkv_grads, up, place = together(
        swap(part1[1], "c"),
        qkv_back(2, place),
        small_call(
            qkv_weights_kernel,
            "qkv_weights",
            8,
            place,
            (normed1, back, other_back),
            [shape((nz, ny * head, half), BF16)] * 2,
        ),
        spread_z(up),
        where[3],
    )
    own1, send1 = first_sum(part1[0], got1)
    own1, got1, got2, part3, qkv_own, qkv_got, place = together(
        own1,
        swap(send1, "x"),
        swap(part2[1], "c"),
        qkv_back(3, place),
        qkv_grads[0],
        exchange_lanes(qkv_grads[1]),
        where[0],
    )
    own2, send2 = first_sum(part2[0], got2)
    sum1 = (own1 + got1.astype(F32)).astype(BF16)
    carried, own2, got2, got3, part0 = together(
        ring(sum1, nz),
        own2,
        swap(send2, "x"),
        swap(part3[1], "c"),
        qkv_back(0, place),
    )
    qkv_grads = spread_z(scatter_lanes(qkv_own, qkv_got))
    own3, send3 = first_sum(part3[0], got3)
    sum2 = (own2 + got2.astype(F32) + carried.astype(F32)).astype(BF16)
    terms1 = part0[2] + part1[2] + part2[2] + part3[2]
    terms1 = jnp.concatenate([terms1, terms2], axis=0)
    terms1 = terms1 + swap(terms1, "c")
    carried, own3, got3, got0, terms1, terms1_x, qkv_grads = together(
        ring(sum2, nz),
        own3,
        swap(send3, "x"),
        swap(part0[1], "c"),
        terms1,
        swap(terms1, "x"),
        qkv_grads,
    )
    own0, send0 = first_sum(part0[0], got0)
    sum3 = (own3 + got3.astype(F32) + carried.astype(F32)).astype(BF16)
    peak_slots = jnp.zeros((nz * groups, 2 * width // (nz * groups)), F32)
    peak_slots = lax.dynamic_update_slice(
        peak_slots, jnp.broadcast_to(jnp.max(peak), (1, peak_slots.shape[1])), (zi * groups + group, 0)
    )
    terms1 = jnp.stack([terms1 + terms1_x, peak_slots.reshape(2, width)])
    terms1 = sum_small(terms1, ("y", "q"))
    terms1_z = lax.ppermute(terms1, "z", [(i, i ^ 1) for i in range(nz)])
    carried, own0, got0, terms1, terms1_z = together(
        ring(sum3, nz), own0, swap(send0, "x"), terms1, terms1_z
    )
    terms1 = terms1 + terms1_z
    terms1 = terms1 + lax.ppermute(terms1, "z", [(i, i ^ 2) for i in range(nz)])
    summed1 = own0 + got0.astype(F32) + carried.astype(F32)
    grad_in = (grad_mid + norm_back(summed1, gain1, hidden_in, scale1[0])).astype(BF16)

    grad_wd = lay_out(down, True)
    grad_wg = lay_out(gate, False)
    grad_wu = lay_out(up, False)
    branch_ffn = summed2[rows + EXTRA :]
    hidden_out = (residual_mid + branch_ffn.astype(F32)).astype(BF16)
    if nq > 1:
        wo_back = wo_back.reshape(nz * 2, -1, groups // 2, slab).transpose(0, 2, 1, 3)
        wo_back = wo_back.reshape(nz * groups, -1, slab)
    grad_wo = lax.psum_scatter(wo_back, WIDE, scatter_dimension=0, tiled=False).astype(F32)
    grad_qkv = small_call(
        qkv_out_kernel,
        "lay_out_qkv",
        3,
        where[0],
        (qkv_grads,),
        [shape((slab, nz * ny * HDIM), F32)] * 3,
    )

    peaks = terms1[1].reshape(nz * groups, -1)[:, 0]
    gain_terms = terms1[0].reshape(2, 2, nz, half)
    gain_terms = gain_terms.transpose(0, 2, 1, 3).reshape(2, width) / gains
    terms = lax.dynamic_slice_in_dim(gain_terms, (zi * groups + group) * slab, slab, 1)
    peaks = peaks.reshape(nz, nq, ny)
    head_peaks = jnp.max(peaks, axis=1).reshape(nz * ny)
    factor = jnp.sqrt(clip_limit / jnp.maximum(head_peaks, clip_limit))
    column_factor = jnp.repeat(factor, HDIM)
    return (
        hidden_out,
        grad_in,
        grad_qkv[0],
        grad_qkv[1],
        grad_qkv[2],
        grad_wo,
        grad_wg,
        grad_wu,
        grad_wd,
        terms[0],
        terms[1],
        w_query.astype(F32) * column_factor[None, :],
        w_key.astype(F32) * column_factor[None, :],
        head_peaks,
    )


def solution(mesh):
    wide, narrow = mesh.devices.shape
    sizes = (4, wide // 8, 2, narrow // 2, 2)
    fine = Mesh(mesh.devices.reshape(sizes), ("z", "q", "y", "x", "c"))
    both = P(WIDE, NARROW)
    turned = P(NARROW, WIDE)
    return jax.shard_map(
        functools.partial(on_device, sizes),
        mesh=fine,
        in_specs=(
            both, P(WIDE), both, both, both, turned, P(WIDE), both, both, turned, both, P(), P()
        ),
        out_specs=(
            both, both, both, both, both, turned, both, both, turned,
            P(WIDE), P(WIDE), both, both, P(NARROW),
        ),
        check_vma=False,
    )
```

```python
import functools

import jax
import jax.numpy as jnp
from jax import lax
from jax.experimental import pallas as pl
from jax.experimental.pallas import tpu as pltpu
from jax.sharding import Mesh
from jax.sharding import PartitionSpec as P

HDIM = 64
HALF = HDIM // 2

eps_norm = 1e-05
rope_base = 130000.0
clip_limit = 5.0
masked_fill = -1e30

F32 = jnp.float32
BF16 = jnp.bfloat16
WIDE = ("z", "q", "y")
GROUP = ("q", "y")
NARROW = ("x", "c")
VMEM_BYTES = 60 * 2**20
EXTRA = 16


def lookup(lookup_table, indices):
    labels = jnp.arange(lookup_table.shape[0], dtype=jnp.int32)
    return jnp.sum(
        jnp.where(indices[:, None] == labels[None, :], lookup_table[None, :], 0),
        axis=1,
        dtype=jnp.int32,
    )


def segment_tables(segment_ids, parents):
    labels = jnp.arange(parents.shape[0], dtype=jnp.int32)
    counts = jnp.sum(
        (segment_ids[:, None] == labels[None, :]).astype(jnp.int32), axis=0, dtype=jnp.int32
    )
    starts = jnp.sum(
        jnp.where(labels[None, :] < labels[:, None], counts[None, :], 0), axis=1, dtype=jnp.int32
    )
    ancestor = lookup(parents, parents)
    parent_len = jnp.where(parents != labels, lookup(counts, parents), 0)
    ancestor_len = jnp.where(ancestor != parents, lookup(counts, ancestor), 0)
    return (ancestor, starts, parent_len, ancestor_len)


def dot(left, right, left_dim, right_dim):
    return lax.dot_general(
        left, right, (((left_dim,), (right_dim,)), ((), ())), preferred_element_type=F32
    )


def take(array, index, axis=0):
    return lax.dynamic_index_in_dim(array, index, axis, keepdims=False)


def swap(array, axis):
    return lax.ppermute(array, axis, [(0, 1), (1, 0)])


def ring(array, size):
    return lax.ppermute(array, "z", [(i, (i + 1) % size) for i in range(size)])


def pick(flag, first, second):
    return jnp.where(flag == 0, first, second)


def together(*values):
    return lax.optimization_barrier(values)


def params():
    return pltpu.CompilerParams(vmem_limit_bytes=VMEM_BYTES)


def cost(time):
    return pl.CostEstimate(flops=int(time * 1e9), bytes_accessed=1000, transcendentals=0)


def shape(dims, dtype):
    return jax.ShapeDtypeStruct(dims, dtype)


def full(dims):
    return pl.BlockSpec(dims, lambda *_: (0,) * len(dims))


def fill_tiles(sources, mask, held, k_ext, values_t):
    if len(sources) == 1:
        held[...] = sources[0][...]
    else:
        for t, source in enumerate(sources):
            held[t] = source[...]
    for t in range(held.shape[0]):
        tile = held[t].astype(F32)
        spare = k_ext.shape[2] - HDIM - mask.shape[1]
        parts = [tile[HDIM : 2 * HDIM], mask[t].astype(F32)]
        parts.append(jnp.zeros((spare, tile.shape[1]), F32))
        k_ext[t] = jnp.concatenate(parts, axis=0).T.astype(BF16)
        if values_t is not None:
            values_t[t] = jnp.concatenate(
                [tile[2 * HDIM :], jnp.zeros((HDIM, tile.shape[1]), F32)], axis=0
            ).T.astype(BF16)


def query_ext(q, mask, depth):
    spare = depth - HDIM - mask.shape[1]
    return jnp.concatenate([q, mask[0], jnp.zeros((spare, q.shape[1]), BF16)], axis=0)


def attend_kernel(visible, counts, q_pos, k_pos, *refs):
    q_mask, k_mask, low, out, log_norm, peak, held, k_ext = refs[-8:]
    i = pl.program_id(0)
    tiles, _, width = held.shape

    @pl.when(i == 0)
    def _():
        fill_tiles(refs[:-8], k_mask, held, k_ext, None)

    mine = q_pos[pl.num_programs(0) * 2]
    q_tile = query_ext(held[mine + i, :HDIM], q_mask, k_ext.shape[2])
    relative = lax.broadcasted_iota(jnp.int32, (width, width), 0) - lax.broadcasted_iota(
        jnp.int32, (width, width), 1
    )

    def one_tile(j, carry, diagonal):
        high, total, acc = carry
        scores = dot(k_ext[j], q_tile, 1, 0)
        if diagonal:
            scores = jnp.where(relative <= 0, scores, masked_fill)
        new_high = jnp.maximum(high, jnp.max(scores, axis=0, keepdims=True))
        weights = jnp.exp(scores - new_high)
        shrink = jnp.exp(high - new_high)
        total = total * shrink + jnp.sum(weights, axis=0, keepdims=True)
        acc = acc * shrink + dot(held[j, 2 * HDIM :], weights.astype(BF16), 1, 0)
        return new_high, total, acc

    start = (
        jnp.full((1, width), masked_fill, F32),
        jnp.zeros((1, width), F32),
        jnp.zeros((HDIM, width), F32),
    )
    high, total, acc = lax.fori_loop(
        0,
        counts[i],
        lambda n, carry: one_tile(visible[i * tiles + n], carry, False),
        one_tile(mine + i, start, True),
    )
    result = acc / total
    out[0] = result
    low[0] = result.astype(BF16)
    log_norm[0] = high + jnp.log(total)
    peak[0] = high


def attend(tables, tiles, q_mask, k_mask):
    q_tiles, labels, width = q_mask.shape
    k_tiles = k_mask.shape[0]
    part = lambda i, *_: (i, 0, 0)
    placed = lambda i, visible, counts, q_pos, k_pos: (q_pos[i + q_tiles], 0, 0)
    return pl.pallas_call(
        attend_kernel,
        grid_spec=pltpu.PrefetchScalarGridSpec(
            num_scalar_prefetch=4,
            grid=(q_tiles,),
            in_specs=[full(a.shape) for a in tiles]
            + [pl.BlockSpec((1, labels, width), part), full(k_mask.shape)],
            out_specs=[
                pl.BlockSpec((1, HDIM, width), placed),
                pl.BlockSpec((1, HDIM, width), part),
                pl.BlockSpec((1, 1, width), part),
                pl.BlockSpec((1, 1, width), part),
            ],
            scratch_shapes=[
                pltpu.VMEM((k_tiles, 3 * HDIM, width), BF16),
                pltpu.VMEM((k_tiles, width, 2 * HDIM), BF16),
            ],
        ),
        out_shape=[
            shape((q_tiles, HDIM, width), BF16),
            shape((q_tiles, HDIM, width), F32),
            shape((q_tiles, 1, width), F32),
            shape((q_tiles, 1, width), F32),
        ],
        compiler_params=params(),
        cost_estimate=cost(18),
        name="attend",
    )(*tables, *tiles, q_mask, k_mask)


def attend_back_kernel(visible, counts, q_pos, k_pos, *refs):
    q_mask, k_mask, grads, out, log_norm, cosine, sine, back = refs[-13:-5]
    held, k_ext, values_t, acc_k, acc_v = refs[-5:]
    i = pl.program_id(0)
    tiles, _, width = held.shape

    @pl.when(i == 0)
    def _():
        fill_tiles(refs[:-13], k_mask, held, k_ext, values_t)
        acc_k[...] = jnp.zeros_like(acc_k)
        acc_v[...] = jnp.zeros_like(acc_v)

    mine = q_pos[pl.num_programs(0) * 2]
    q_rows = held[mine + i, :HDIM]
    q_tile = query_ext(q_rows, q_mask, k_ext.shape[2])
    g_tile = grads[0]
    g_ext = jnp.concatenate([g_tile, jnp.zeros_like(g_tile)], axis=0)
    lse = log_norm[0]
    delta = jnp.sum(g_tile.astype(F32) * out[0], axis=0, keepdims=True)
    relative = lax.broadcasted_iota(jnp.int32, (width, width), 0) - lax.broadcasted_iota(
        jnp.int32, (width, width), 1
    )

    def one_tile(j, acc, diagonal):
        scores = dot(k_ext[j], q_tile, 1, 0)
        if diagonal:
            scores = jnp.where(relative <= 0, scores, masked_fill)
        probs = jnp.exp(scores - lse)
        grad_probs = dot(values_t[j], g_ext, 1, 0)
        grad_scores = (probs * (grad_probs - delta)).astype(BF16)
        acc_v[j] += dot(g_tile, probs.astype(BF16), 1, 1)
        acc_k[j] += dot(q_rows, grad_scores, 1, 1)
        return acc + dot(held[j, HDIM : 2 * HDIM], grad_scores, 1, 0)

    acc = lax.fori_loop(
        0,
        counts[i],
        lambda n, acc: one_tile(visible[i * tiles + n], acc, False),
        one_tile(mine + i, jnp.zeros((HDIM, width), F32), True),
    )

    def put_unrotated(grad, t, base):
        first, second, c, s = grad[:HALF], grad[HALF:], cosine[t], sine[t]
        back[t, base : base + HALF] = (first * c + second * s).astype(BF16)
        back[t, base + HALF : base + HDIM] = (second * c - first * s).astype(BF16)

    put_unrotated(acc * HDIM ** (-0.5), mine + i, 0)

    @pl.when(i == pl.num_programs(0) - 1)
    def _():
        for t in range(tiles):
            put_unrotated(acc_k[t], t, HDIM)
            back[t, 2 * HDIM :] = acc_v[t].astype(BF16)


def attend_back(tables, tiles, q_mask, k_mask, grads, out, log_norm, cosine, sine):
    q_tiles, labels, width = q_mask.shape
    k_tiles = k_mask.shape[0]
    part = lambda i, *_: (i, 0, 0)
    placed = lambda i, visible, counts, q_pos, k_pos: (q_pos[i + q_tiles], 0, 0)
    return pl.pallas_call(
        attend_back_kernel,
        grid_spec=pltpu.PrefetchScalarGridSpec(
            num_scalar_prefetch=4,
            grid=(q_tiles,),
            in_specs=[full(a.shape) for a in tiles]
            + [
                pl.BlockSpec((1, labels, width), part),
                full(k_mask.shape),
                pl.BlockSpec((1, HDIM, width), placed),
                pl.BlockSpec((1, HDIM, width), part),
                pl.BlockSpec((1, 1, width), part),
                full(cosine.shape),
                full(sine.shape),
            ],
            out_specs=full((k_tiles, 3 * HDIM, width)),
            scratch_shapes=[
                pltpu.VMEM((k_tiles, 3 * HDIM, width), BF16),
                pltpu.VMEM((k_tiles, width, 2 * HDIM), BF16),
                pltpu.VMEM((k_tiles, width, 2 * HDIM), BF16),
                pltpu.VMEM((k_tiles, HDIM, width), F32),
                pltpu.VMEM((k_tiles, HDIM, width), F32),
            ],
        ),
        out_shape=shape((k_tiles, 3 * HDIM, width), BF16),
        compiler_params=params(),
        cost_estimate=cost(22),
        name="attend_back",
    )(*tables, *tiles, q_mask, k_mask, grads, out, log_norm, cosine, sine)


def row_scale(pieces, width):
    squares = 0.0
    for piece in pieces:
        values = piece[...].astype(F32)
        squares = squares + jnp.sum(values * values, axis=1, keepdims=True)
    return lax.rsqrt(squares / width + eps_norm)


def aligned(start, size):
    return pl.ds(pl.multiple_of(start, size), size)


def block_of(where, k):
    return where[0] ^ k


def half_columns(where, h, wide):
    return aligned((h ^ where[1]) * wide, wide)


def put_normed(where, pieces, rstd, gain, normed):
    cols = pieces[0].shape[1]
    half = cols // 2
    for k, piece in enumerate(pieces):
        block = block_of(where, k)
        values = piece[...].astype(F32) * rstd * gain[:, aligned(block * cols, cols)]
        for part in range(2):
            columns = aligned((part * 4 + block) * half, half)
            normed[:, columns] = values[:, part * half : (part + 1) * half].astype(BF16)


def qkv_kernel(where, *refs):
    pieces, (gain, w_first, w_second, cosine, sine) = refs[:4], refs[4:9]
    normed, mine, other, scale = refs[-4:]
    rows, cols = pieces[0].shape
    half = cols // 2
    rstd = row_scale(pieces, 4 * cols)
    scale[...] = rstd
    put_normed(where, pieces, rstd, gain, normed)
    c, s = cosine[...], sine[...]
    features = 3 * HDIM
    for out, head in ((mine, where[2]), (other, 1 - where[2])):
        span = aligned(head * features, features)
        lin = 0.0
        for h, weights in enumerate((w_first, w_second)):
            for z in range(4):
                columns = aligned(((h ^ where[1]) * 4 + z) * half, half)
                lin = lin + dot(weights[z, span, :], normed[:, columns], 1, 1)
        for part, factor in ((0, HDIM ** (-0.5)), (1, 1.0)):
            base = part * HDIM
            first, second = lin[base : base + HALF], lin[base + HALF : base + HDIM]
            out[base : base + HALF] = ((first * c - second * s) * factor).astype(BF16)
            out[base + HALF : base + HDIM] = ((second * c + first * s) * factor).astype(BF16)
        out[2 * HDIM :] = lin[2 * HDIM :].astype(BF16)


def chunk_call(
    kernel, name, time, where, s, inputs, buffers, whole_shapes, out_shapes, scratch=(), out_there=0
):
    def spec(dims, how):
        rest = (0,) * (len(dims) - 1)
        if how == "whole":
            return full(dims)
        if how == "there":
            return pl.BlockSpec(memory_space=pl.ANY)
        block = (dims[0] // 4, *dims[1:])
        if how == "chunk":
            return pl.BlockSpec(block, lambda i, where: (s, *rest))
        return pl.BlockSpec(block, lambda i, where: (where[3], *rest))

    in_specs = [spec(a.shape, how) for a, how in inputs]
    arrays = [a for a, _ in inputs]
    aliases = {}
    if buffers is not None:
        for n, buffer in enumerate(buffers):
            aliases[1 + len(arrays)] = n
            in_specs.append(pl.BlockSpec(memory_space=pl.ANY))
            arrays.append(buffer)
    out_specs = [spec(dims, how) for dims, how in whole_shapes]
    out_specs += [
        pl.BlockSpec(memory_space=pl.ANY) if n < out_there else full(a.shape)
        for n, a in enumerate(out_shapes)
    ]
    return pl.pallas_call(
        kernel,
        grid_spec=pltpu.PrefetchScalarGridSpec(
            num_scalar_prefetch=1,
            grid=(1,),
            in_specs=in_specs,
            out_specs=out_specs,
            scratch_shapes=list(scratch),
        ),
        out_shape=[shape(dims, BF16) for dims, _ in whole_shapes] + list(out_shapes),
        input_output_aliases=aliases,
        compiler_params=params(),
        cost_estimate=cost(time),
        name=name,
    )(where, *arrays)


def fetch(weights, held, sems, first=0, start=0):
    copies = []
    for n, weight in enumerate(weights):
        rows = weight.shape[0]
        copies.append(
            pltpu.make_async_copy(weight, held.at[pl.ds(start, rows)], sems.at[first + n])
        )
        copies[-1].start()
        start += rows
    return copies


class Sends:
    def __init__(self, sems):
        self.sems, self.copies = sems, []

    def start(self, source, target):
        self.copies.append(pltpu.make_async_copy(source, target, self.sems.at[len(self.copies)]))
        self.copies[-1].start()

    def wait(self):
        for copy in self.copies:
            copy.wait()


def load(pairs, sems, first):
    copies = [
        pltpu.make_async_copy(source, target, sems.at[first + n])
        for n, (source, target) in enumerate(pairs)
    ]
    for copy in copies:
        copy.start()
    return copies


def wait_all(copies):
    for copy in copies:
        copy.wait()


def ffn_kernel(chunks, count, where, *refs):
    pieces, gain, weights = refs[:8], refs[8], refs[9 : 9 + count]
    outs = refs[-16:-8]
    mids, normed_all, hidden_all, gates_all, ups_all, held, sems, out_sems = refs[-8:]
    normed_out, hidden_out, scales = outs[0], outs[1], outs[6:]
    rows, cols = mids.shape[2:]
    units, wide = hidden_all.shape[2], 2 * cols
    come = [
        load([(pieces[4 * i + k], mids.at[i, k]) for k in range(4)], sems, count + 4 * i)
        for i in range(2)
    ]
    copies = fetch(weights, held, sems)
    sends = Sends(out_sems)
    step = 256
    for i in range(2):
        chunk = pl.ds(chunks[i] * rows, rows)
        normed, hidden = normed_all.at[i], hidden_all.at[i]
        gates, ups = gates_all.at[i], ups_all.at[i]
        gates_out, ups_out = outs[2 + 2 * i], outs[3 + 2 * i]
        wait_all(come[i])
        blocks = [mids.at[i, k] for k in range(4)]
        rstd = row_scale(blocks, 4 * cols)
        scales[i][...] = rstd
        put_normed(where, blocks, rstd, gain, normed)
        sends.start(normed, normed_out.at[chunk])
        if i == 0:
            wait_all(copies)
        for n in range(0, units, step):
            span = slice(n, n + step)
            columns = pl.ds(n, step)
            gate = up = 0.0
            for h in range(2):
                values = normed[:, half_columns(where, h, wide)]
                gate = gate + dot(values, held[h * wide : (h + 1) * wide, span], 1, 0)
                up = up + dot(values, held[(h + 2) * wide : (h + 3) * wide, span], 1, 0)
            gates[:, span] = gate
            ups[:, span] = up
            sends.start(gates.at[:, columns], gates_out.at[:, columns])
            sends.start(ups.at[:, columns], ups_out.at[:, columns])
            hidden[:, span] = (gate * jax.nn.sigmoid(gate) * up).astype(BF16)
            sends.start(hidden.at[:, columns], hidden_out.at[chunk, columns])
    sends.wait()


def arrange_kernel(zs, cots, cot_rows):
    cols = cots.shape[2]
    half = cols // 2
    for block in range(4):
        for part in range(2):
            start = (part * 4 + block) * half
            cot_rows[:, start : start + half] = cots[block, :, part * half : (part + 1) * half]


def arrange(cot, zs):
    blocks, rows, cols = cot.shape
    return pl.pallas_call(
        arrange_kernel,
        grid_spec=pltpu.PrefetchScalarGridSpec(
            num_scalar_prefetch=1,
            grid=(4,),
            in_specs=[pl.BlockSpec((blocks // 4, rows, cols), lambda s, zs: (zs[s], 0, 0))],
            out_specs=pl.BlockSpec((rows, 4 * cols), lambda s, zs: (s, 0)),
        ),
        out_shape=shape((4 * rows, 4 * cols), BF16),
        compiler_params=params(),
        cost_estimate=cost(5),
        name="arrange",
    )(zs, cot)


def ffn_back_kernel(chunks, downs, count, where, *refs):
    weights, kept = refs[:count], refs[count : count + 4]
    all_cot, all_hidden, all_normed = refs[count + 4 : count + 7]
    grad_gate_out, grad_up_out = refs[-20:-18]
    backs, gain_term = refs[-18:-14], refs[-14]
    held, cot_all, gate_up, hidden_in, normed_in, sems = refs[-13:-7]
    grad_gates, grad_ups, out_held, back_held, lines, out_sems, line_sems = refs[-7:]
    rows, units = grad_gates.shape[1:]
    cols = out_held.shape[3]
    half, wide = cols // 2, 2 * cols
    step = 256
    spans = [pl.ds(s * rows, rows) for s in chunks]
    early = load([(all_cot.at[spans[0]], cot_all.at[0])], sems, count)
    early += fetch(weights[:downs], held, sems)
    early += load([(kept[0], gate_up.at[0, 0]), (kept[1], gate_up.at[0, 1])], sems, count + 1)
    late = load(
        [(all_hidden.at[spans[0]], hidden_in.at[0]), (all_normed.at[spans[0]], normed_in.at[0])],
        sems,
        count + 3,
    )
    late += fetch(weights[downs:], held, sems, downs, 2 * wide)
    second = load(
        [
            (all_cot.at[spans[1]], cot_all.at[1]),
            (kept[2], gate_up.at[1, 0]),
            (kept[3], gate_up.at[1, 1]),
            (all_hidden.at[spans[1]], hidden_in.at[1]),
            (all_normed.at[spans[1]], normed_in.at[1]),
        ],
        sems,
        count + 5,
    )
    sends, tails = Sends(out_sems), Sends(line_sems)
    for i in range(2):
        cot_rows, hidden, normed = cot_all.at[i], hidden_in.at[i], normed_in.at[i]
        gates, ups = gate_up.at[i, 0], gate_up.at[i, 1]
        grad_gate, grad_up = grad_gates.at[i], grad_ups.at[i]
        wait_all(early if i == 0 else second)
        for n in range(0, units, step):
            span = slice(n, n + step)
            columns = pl.ds(n, step)
            grad_hidden = 0.0
            for h in range(2):
                grad_hidden = grad_hidden + dot(
                    cot_rows[:, half_columns(where, h, wide)],
                    held[h * wide : (h + 1) * wide, span],
                    1,
                    0,
                )
            gate, up = gates[:, span], ups[:, span]
            sigmoid = jax.nn.sigmoid(gate)
            grad_gate[:, span] = (
                grad_hidden * up * sigmoid * (1.0 + gate * (1.0 - sigmoid))
            ).astype(BF16)
            grad_up[:, span] = (grad_hidden * (gate * sigmoid)).astype(BF16)
            sends.start(grad_gate.at[:, columns], grad_gate_out.at[spans[i], columns])
            sends.start(grad_up.at[:, columns], grad_up_out.at[spans[i], columns])
        if i == 0:
            wait_all(late)
        row_term = 0.0
        for k in range(4):
            block = block_of(where, k)
            back = backs[2 * i + k % 2]
            for h in range(2):
                part = aligned((h ^ where[1]) * half, half)
                of_down, of_gate, of_up = [
                    held[aligned((n + h) * wide + block * half, half), :] for n in (0, 2, 4)
                ]
                out_held[i, k, :, part] = dot(hidden[...], of_down, 1, 1).astype(BF16)
                partial = dot(grad_gate[...], of_gate, 1, 1) + dot(grad_up[...], of_up, 1, 1)
                back_held[i, k, :, part] = partial.astype(BF16)
                columns = aligned(((h ^ where[1]) * 4 + block) * half, half)
                terms = partial * normed[:, columns].astype(F32)
                column_term = jnp.sum(terms, axis=0, keepdims=True)
                if i == 0:
                    gain_term[:, columns] = column_term
                else:
                    gain_term[:, columns] += column_term
                row_term = row_term + jnp.sum(terms, axis=1, keepdims=True)
            sends.start(out_held.at[i, k], back.at[k // 2, pl.ds(rows + EXTRA, rows)])
            sends.start(back_held.at[i, k], back.at[k // 2, pl.ds(0, rows)])
        lines[i] = row_line(row_term, cols)
        for back in backs[2 * i : 2 * i + 2]:
            for x in range(2):
                tails.start(lines.at[i], back.at[x, pl.ds(rows, EXTRA)])
    sends.wait()
    tails.wait()


def row_line(row_term, cols):
    rows = row_term.shape[0]
    line = jnp.broadcast_to(row_term, (rows, 128)).T[:EXTRA]
    return jnp.concatenate([line, jnp.zeros((EXTRA, cols - rows), F32)], axis=1).astype(BF16)


def put_row_term(row_term, cols, keep, send):
    rows = row_term.shape[0]
    line = row_line(row_term, cols)
    for ref in (keep, send):
        ref[0, rows:] = line
        ref[1, rows:] = line


def qkv_back_kernel(where, normed, mine, other, w_first, w_second, keep, send, gain_term):
    rows, cols = normed.shape[0], keep.shape[2]
    half = cols // 2
    features = 3 * HDIM
    row_term = 0.0
    for k in range(4):
        block = block_of(where, k)
        back = (keep, send)[k % 2]
        for h, weights in enumerate((w_first, w_second)):
            part = aligned((h ^ where[1]) * half, half)
            partial = 0.0
            for grads, head in ((mine, where[2]), (other, 1 - where[2])):
                span = aligned(head * features, features)
                partial = partial + dot(grads[0], weights[block, span, :], 0, 0)
            back[k // 2, :rows, part] = partial.astype(BF16)
            columns = aligned(((h ^ where[1]) * 4 + block) * half, half)
            terms = partial * normed[:, columns].astype(F32)
            gain_term[:, columns] = jnp.sum(terms, axis=0, keepdims=True)
            row_term = row_term + jnp.sum(terms, axis=1, keepdims=True)
    put_row_term(row_term, cols, keep, send)


def qkv_weights_kernel(where, normed, *refs):
    own, other, outs = refs[0], refs[1], refs[2:]
    count = other.shape[0]
    half = outs[0].shape[2]
    rows, features = own.shape[2], 3 * HDIM
    for h, out in enumerate(outs):
        for z in range(4):
            columns = aligned(((h ^ where[1]) * 4 + z) * half, half)
            for grads, head in ((own, where[2]), (other, 1 - where[2])):
                total = 0.0
                for s in range(count):
                    total = total + dot(
                        grads[s], normed[s * rows : (s + 1) * rows, columns], 1, 0
                    )
                out[z, aligned(head * features, features), :] = total.astype(BF16)


def project_kernel(where, attended, weights, keep, send):
    half = weights.shape[2]
    for k in range(4):
        for part in range(2):
            (keep, send)[k % 2][k // 2, :, part * half : (part + 1) * half] = dot(
                attended[...], weights[block_of(where, k) * 2 + part], 0, 0
            ).astype(BF16)


def project_back_kernel(where, p0, p1, p2, p3, attended, weights, grad_att, grad_weights):
    half = weights.shape[2]
    total = 0.0
    for k, piece in enumerate((p0, p1, p2, p3)):
        for part in range(2):
            b = block_of(where, k) * 2 + part
            values = piece[:, part * half : (part + 1) * half]
            total = total + dot(weights[b], values, 1, 1)
            grad_weights[b] = dot(attended[...], values, 1, 0).astype(BF16)
    grad_att[...] = total.astype(BF16)


def columns_kernel(parts, out):
    out[...] = parts[0].astype(F32)


def turned_kernel(parts, out):
    out[...] = parts[0].astype(F32).T


def lay_out(parts, turned):
    nz, n, m = parts.shape
    if turned:
        kernel, dims, block, place = turned_kernel, (nz * m, n), (m, n), lambda z: (z, 0)
    else:
        kernel, dims, block, place = columns_kernel, (n, nz * m), (n, m), lambda z: (0, z)
    return pl.pallas_call(
        kernel,
        grid=(nz,),
        in_specs=[pl.BlockSpec((1, n, m), lambda z: (z, 0, 0))],
        out_specs=pl.BlockSpec(block, place),
        out_shape=shape(dims, F32),
        compiler_params=params(),
        cost_estimate=cost(2),
        name="lay_out",
    )(parts)


def qkv_out_kernel(where, parts, *outs):
    features = 3 * HDIM
    for z in range(parts.shape[0]):
        for n, out in enumerate(outs):
            heads = [parts[z, h * features + n * HDIM : h * features + (n + 1) * HDIM] for h in (0, 1)]
            both = jnp.concatenate(heads, axis=0).astype(F32)
            out[:, z * 2 * HDIM : (z + 1) * 2 * HDIM] = both.T


def small_call(kernel, name, time, where, inputs, out_shapes, specs=None):
    specs = specs or {}
    return pl.pallas_call(
        kernel,
        grid_spec=pltpu.PrefetchScalarGridSpec(
            num_scalar_prefetch=1,
            grid=(1,),
            in_specs=[specs.get(n) or full(a.shape) for n, a in enumerate(inputs)],
            out_specs=[full(s.shape) for s in out_shapes],
        ),
        out_shape=list(out_shapes),
        compiler_params=params(),
        cost_estimate=cost(time),
        name=name,
    )(where, *inputs)


def on_device(
    sizes,
    hidden_in,
    gain_attn,
    w_query,
    w_key,
    w_value,
    w_out,
    gain_ffn,
    w_gate,
    w_up,
    w_down,
    cotangent,
    segment_ids,
    parents,
):
    nz, nq, ny, nx, nc = sizes
    rows, cols = hidden_in.shape
    groups = nq * ny
    group_rows = nz * rows
    width = cols * nx * nc
    half = cols // 2
    slab = gain_attn.shape[0]
    head = 3 * HDIM
    units = w_gate.shape[1] // nz

    zi, qi, yi, xi, ci = [lax.axis_index(a) for a in ("z", "q", "y", "x", "c")]
    group = qi * ny + yi
    own_columns = xi * nc + ci
    zs = [(zi - s) % nz for s in range(nz)]
    flip = yi if nq == 1 else 0 * yi
    where = [jnp.stack([own_columns, flip, yi, z]).astype(jnp.int32) for z in zs]

    def scatter_narrow(keep, send):
        held = keep.astype(F32) + swap(send, "c").astype(F32)
        return held[0] + swap(held[1].astype(BF16), "x").astype(F32)

    def first_sum(keep, received):
        held = keep.astype(F32) + received.astype(F32)
        return held[0], held[1].astype(BF16)

    def spread_z(parts):
        return lax.all_to_all(parts, "z", split_axis=0, concat_axis=0, tiled=True)

    def gather_rows(parts):
        n = parts.shape[2]
        if nq == 1:
            return parts.reshape(-1, n), swap(parts, "y").reshape(-1, n)
        got = lax.all_gather(parts, GROUP, axis=0, tiled=False)
        got = got.reshape(2, groups // 2, nz, slab, n).transpose(0, 2, 1, 3, 4)
        return tuple(got.reshape(2, nz * half, n))

    def swap_part(parts, n):
        part = parts[n * nz // 2 : (n + 1) * nz // 2]
        return swap(part, "y") if nq == 1 else part

    def join_rows(parts, swapped):
        if nq > 1:
            return gather_rows(parts)
        return [a.reshape(-1, units) for a in (parts, *swapped)]

    def gather_lanes(parts):
        n = parts.shape[1]
        if nq == 1:
            return parts, swap(parts, "y")
        got = lax.all_gather(parts, GROUP, axis=0, tiled=False)
        got = got.reshape(2, groups // 2, nz, n, slab).transpose(0, 2, 3, 1, 4)
        return tuple(got.reshape(2, nz, n, half))

    def exchange_rows(grad):
        if nq == 1:
            return swap(take(grad.reshape(2, -1, grad.shape[1]), 1 - yi), "y")
        n = grad.shape[1]
        parts = grad.reshape(2, nz, groups // 2, slab, n).transpose(0, 2, 1, 3, 4)
        return lax.psum_scatter(
            parts.reshape(groups, nz, slab, n), GROUP, scatter_dimension=0, tiled=False
        )

    def add_rows(grad, received):
        if nq == 1:
            own = take(grad.reshape(2, -1, grad.shape[1]), yi)
            received = (own.astype(F32) + received.astype(F32)).astype(BF16)
        return received.reshape(nz, slab, -1)

    def exchange_lanes(second):
        return swap(second, "y") if nq == 1 else second

    def scatter_lanes(first, second):
        n = first.shape[1]
        if nq == 1:
            return (first.astype(F32) + second.astype(F32)).astype(BF16)
        both = jnp.stack([first, second]).reshape(2, nz, n, groups // 2, slab)
        both = both.transpose(0, 3, 1, 2, 4).reshape(groups, nz, n, slab)
        return lax.psum_scatter(both, GROUP, scatter_dimension=0, tiled=False)

    def sum_small(values, axes):
        for axis in axes:
            if axis == "z":
                for bit in (1, 2):
                    values = values + lax.ppermute(values, "z", [(i, i ^ bit) for i in range(nz)])
            elif axis == "q":
                values = lax.psum(values, "q") if nq > 1 else values
            else:
                values = values + swap(values, axis)
        return values

    stacked = jnp.stack([w_query, w_key, w_value]).reshape(3, slab, nz, ny, HDIM)
    stacked = stacked.transpose(2, 3, 0, 4, 1).reshape(nz, ny * head, slab)
    both_gains = jnp.concatenate(
        [gain_attn[None], gain_ffn[None], jnp.zeros((EXTRA - 2, slab), BF16)], axis=0
    )
    both_gains = jnp.broadcast_to(both_gains[None], (nz, EXTRA, slab))
    stacked = jnp.concatenate([stacked, both_gains], axis=1)
    z1, x0, c0, stacked, segment_ids, parents = together(
        ring(hidden_in, nz),
        swap(hidden_in, "x"),
        swap(hidden_in, "c"),
        stacked,
        segment_ids,
        parents,
    )

    ancestor, starts, parent_len, ancestor_len = segment_tables(segment_ids, parents)
    q_blocks = [(z * nq + qi) * ny + (yi ^ dy) for dy in range(ny) for z in zs]
    k_blocks = [(z * nq + q) * ny + (yi ^ dy) for q in range(nq) for dy in range(ny) for z in zs]
    segments = segment_ids.reshape(-1, rows)
    k_seg = jnp.stack([take(segments, b) for b in k_blocks])
    k_pos = jnp.stack(k_blocks).astype(jnp.int32)
    q_tiles, k_tiles = len(q_blocks), len(k_blocks)
    of_queries = lambda a: lax.dynamic_slice_in_dim(a, qi * q_tiles, q_tiles, 0)
    flat = k_seg.reshape(-1)
    labels = jnp.arange(-(-parents.shape[0] // 16) * 16, dtype=jnp.int32)[None, :, None]
    places = k_pos[:, None] * rows + jnp.arange(rows, dtype=jnp.int32)[None]
    places = places + lookup(parent_len + ancestor_len - starts, flat).reshape(k_tiles, rows)
    k_own = labels == k_seg[:, None]
    q_seen = of_queries(
        k_own
        | (labels == lookup(parents, flat).reshape(k_tiles, 1, rows))
        | (labels == lookup(ancestor, flat).reshape(k_tiles, 1, rows))
    )
    q_mask = jnp.where(q_seen, 0.0, masked_fill).astype(BF16)
    k_mask = k_own.astype(BF16)
    q_pos = of_queries(k_pos)
    shown = jnp.any(jnp.any(q_seen, axis=2)[:, None] & jnp.any(k_own, axis=2)[None], axis=2)
    shown = shown & (k_pos[None, :] < q_pos[:, None])
    number = jnp.arange(k_tiles, dtype=jnp.int32)
    earlier = number[None, None, :] < number[None, :, None]
    before = jnp.sum((shown[:, None, :] & earlier).astype(jnp.int32), axis=2)
    chosen = shown[:, None, :] & (before[:, None, :] == number[None, :, None])
    visible = jnp.sum(jnp.where(chosen, number[None, None, :], 0), axis=2, dtype=jnp.int32)
    slots = jnp.stack([z * ny + (yi ^ dy) for dy in range(ny) for z in zs]).astype(jnp.int32)
    q_info = jnp.concatenate([q_pos, slots, (qi * q_tiles).reshape(1).astype(jnp.int32)])
    tables = (
        visible.reshape(-1),
        jnp.sum(shown.astype(jnp.int32), axis=1, dtype=jnp.int32),
        q_info,
        k_pos,
    )
    frequency = rope_base ** (-2.0 * jnp.arange(HALF, dtype=F32) / HDIM)
    angles = places.astype(F32)[:, None, :] * frequency[None, :, None]
    cosine, sine = jnp.cos(angles), jnp.sin(angles)
    cos_q, sin_q = of_queries(cosine), of_queries(sine)

    z2, x1, c1, cx0, w_qkv, (tables, q_mask, k_mask, cosine, sine, cos_q, sin_q) = together(
        ring(z1, nz),
        swap(z1, "x"),
        swap(z1, "c"),
        swap(x0, "c"),
        spread_z(stacked),
        (tables, q_mask, k_mask, cosine, sine, cos_q, sin_q),
    )
    z3, x2, c2, cx1, w_qkv, w_gate_, cotangent_, w_out_ = together(
        ring(z2, nz),
        swap(z2, "x"),
        swap(z2, "c"),
        swap(x1, "c"),
        gather_lanes(w_qkv),
        w_gate,
        cotangent,
        w_out,
    )
    x3, c3, cx2 = swap(z3, "x"), swap(z3, "c"), swap(x2, "c")
    x_chunks = [
        (hidden_in, c0, x0, cx0),
        (z1, c1, x1, cx1),
        (z2, c2, x2, cx2),
        (z3, c3, x3, swap(x3, "c")),
    ]
    gains = [w[:, ny * head : ny * head + 2].astype(F32) for w in w_qkv]
    gains = jnp.stack([pick(flip, *gains), pick(flip, gains[1], gains[0])], axis=1)
    gains = gains.transpose(2, 0, 1, 3).reshape(2, width)
    gain1, gain2 = gains[:1], gains[1:]

    wo = lax.all_gather(w_out_, WIDE, axis=0, tiled=False)
    if nq > 1:
        wo = wo.reshape(nz * 2, groups // 2, -1, slab).transpose(0, 2, 1, 3)
        wo = wo.reshape(nz * 2, -1, half)
    of_units = lambda w: spread_z(w.reshape(slab, nz, units).transpose(1, 0, 2))
    cot = lax.all_gather(cotangent_, ("z", *NARROW), axis=0, tiled=False)

    buffers, mine, theirs, scale1 = None, [], [], []
    for s in range(nz):
        normed1, own, other, scale = chunk_call(
            qkv_kernel,
            "qkv",
            5,
            where[s],
            s,
            [(a, "whole") for a in (*x_chunks[s], gain1, *w_qkv, cos_q[s], sin_q[s])],
            buffers,
            [((group_rows, width), "chunk")],
            [shape((head, rows), BF16), shape((head, rows), BF16), shape((rows, 1), F32)],
        )
        buffers = [normed1]
        mine.append(own)
        theirs.append(swap(other, "y"))
        scale1.append(scale)
    tiles, gate_parts, w_up_, w_down_ = together(
        mine + theirs, of_units(w_gate_), w_up, w_down.T
    )
    if nq > 1:
        tiles = [lax.all_gather(jnp.stack(tiles), "q", axis=0, tiled=True)]
    (att_low, att, log_norm, peak), up_parts, w_gates, w_down_ = together(
        attend(tables, tiles, q_mask, k_mask), of_units(w_up_), gather_rows(gate_parts), w_down_
    )

    att_t = lax.all_to_all(att_low, ("z", "y"), split_axis=0, concat_axis=0, tiled=True)
    att_t, w_down_ = together(att_t, w_down_)
    att_t = att_t.reshape(nz * ny * HDIM, rows)
    keep, send = small_call(
        project_kernel,
        "project",
        4,
        where[0],
        (att_t, wo),
        [shape((2, rows, cols), BF16)] * 2,
    )
    residual_mid = hidden_in.astype(F32) + scatter_narrow(keep, send)
    down_parts = of_units(w_down_)
    mid_block = residual_mid.astype(BF16)

    def forward(chunks, pieces, buffers):
        results = chunk_call(
            functools.partial(ffn_kernel, chunks, len(w_gates) + len(w_ups)),
            "feed_forward",
            9,
            where[0],
            0,
            [(a, "there") for a in pieces]
            + [(gain2, "whole")]
            + [(w, "there") for w in (*w_gates, *w_ups)],
            buffers,
            [((group_rows, width), "there"), ((group_rows, units), "there")],
            [shape((rows, units), F32)] * 4 + [shape((rows, 1), F32)] * 2,
            [
                pltpu.VMEM((2, 4, rows, cols), BF16),
                pltpu.VMEM((2, rows, width), BF16),
                pltpu.VMEM((2, rows, units), BF16),
                pltpu.VMEM((2, rows, units), F32),
                pltpu.VMEM((2, rows, units), F32),
                pltpu.VMEM((8 * cols, units), BF16),
                pltpu.SemaphoreType.DMA((len(w_gates) + len(w_ups) + 8,)),
                pltpu.SemaphoreType.DMA((2 + 6 * units // 256,)),
            ],
            4,
        )
        return results[:2], results[2:]

    def backward(chunks, saved, kept, buffers):
        weights = (*w_downs, *w_gates, *w_ups)
        results = chunk_call(
            functools.partial(ffn_back_kernel, chunks, len(w_downs), len(weights)),
            "feed_forward_back",
            15,
            where[0],
            0,
            [(a, "there") for a in (*weights, *kept, cot_rows, saved[1], saved[0])],
            buffers,
            [
                ((group_rows, units), "there"),
                ((group_rows, units), "there"),
            ],
            [shape((2, 2 * rows + EXTRA, cols), BF16)] * 4 + [shape((1, width), F32)],
            [
                pltpu.VMEM((12 * cols, units), BF16),
                pltpu.VMEM((2, rows, width), BF16),
                pltpu.VMEM((2, 2, rows, units), F32),
                pltpu.VMEM((2, rows, units), BF16),
                pltpu.VMEM((2, rows, width), BF16),
                pltpu.SemaphoreType.DMA((len(weights) + 10,)),
                pltpu.VMEM((2, rows, units), BF16),
                pltpu.VMEM((2, rows, units), BF16),
                pltpu.VMEM((2, 4, rows, cols), BF16),
                pltpu.VMEM((2, 4, rows, cols), BF16),
                pltpu.VMEM((2, EXTRA, cols), BF16),
                pltpu.SemaphoreType.DMA((16 + 4 * units // 256,)),
                pltpu.SemaphoreType.DMA((8,)),
            ],
            4,
        )
        return results[:2], results[2:6], results[6]

    z0 = mid_block
    z1, x0, c0, up_a = together(
        ring(z0, nz), swap(z0, "x"), swap(z0, "c"), swap_part(up_parts, 0)
    )
    z2, x1, c1, cx0, up_b, down_parts = together(
        ring(z1, nz),
        swap(z1, "x"),
        swap(z1, "c"),
        swap(x0, "c"),
        swap_part(up_parts, 1),
        down_parts,
    )
    w_ups = join_rows(up_parts, (up_a, up_b))
    z3, x2, c2, cx1, down_a, cot_rows = together(
        ring(z2, nz),
        swap(z2, "x"),
        swap(z2, "c"),
        swap(x1, "c"),
        swap_part(down_parts, 0),
        arrange(cot, jnp.stack(zs).astype(jnp.int32)),
    )
    x3, c3, cx2, down_b, (saved, kept01) = together(
        swap(z3, "x"),
        swap(z3, "c"),
        swap(x2, "c"),
        swap_part(down_parts, 1),
        forward((0, 1), (z0, c0, x0, cx0, z1, c1, x1, cx1), None),
    )
    w_downs = join_rows(down_parts, (down_a, down_b))
    cx3 = swap(x3, "c")
    saved, kept23 = forward((2, 3), (z2, c2, x2, cx2, z3, c3, x3, cx3), saved)
    buffers, back12, terms12 = backward((1, 2), saved, (*kept01[2:4], *kept23[:2]), None)
    part1, part2 = back12[:2], back12[2:]
    got1, part1, part2 = together(swap(part1[1], "c"), part1, part2)
    normed2, hidden = saved
    own1, send1 = first_sum(part1[0], got1)
    own1, got1, got2, (buffers, back30, terms30) = together(
        own1,
        swap(send1, "x"),
        swap(part2[1], "c"),
        backward((3, 0), saved, (*kept23[2:4], *kept01[:2]), buffers),
    )
    part3, part0 = back30[:2], back30[2:]
    own2, send2 = first_sum(part2[0], got2)
    sum1 = (own1 + got1.astype(F32)).astype(BF16)
    carried, own2, got2, got3, down = together(
        ring(sum1, nz),
        own2,
        swap(send2, "x"),
        swap(part3[1], "c"),
        dot(cot_rows, hidden, 0, 0).astype(BF16),
    )
    grad_gate_lin, grad_up_lin = buffers
    own3, send3 = first_sum(part3[0], got3)
    sum2 = (own2 + got2.astype(F32) + carried.astype(F32)).astype(BF16)
    carried, own3, got3, got0, down_got, gate, grad_up_lin = together(
        ring(sum2, nz),
        own3,
        swap(send3, "x"),
        swap(part0[1], "c"),
        exchange_rows(down),
        dot(normed2, grad_gate_lin, 0, 0).astype(BF16),
        grad_up_lin,
    )
    own0, send0 = first_sum(part0[0], got0)
    sum3 = (own3 + got3.astype(F32) + carried.astype(F32)).astype(BF16)
    down = add_rows(down, down_got)
    gate_got = exchange_rows(gate)
    carried, own0, got0, up = together(
        ring(sum3, nz),
        own0,
        swap(send0, "x"),
        dot(normed2, grad_up_lin, 0, 0).astype(BF16),
    )
    summed2 = own0 + got0.astype(F32) + carried.astype(F32)
    scale2 = kept01[4]
    terms2 = terms12 + terms30

    def norm_back(summed, gain, block, rstd):
        gain = lax.dynamic_slice_in_dim(gain, own_columns * cols, cols, 1)
        mean = summed[rows, :rows].reshape(rows, 1) / width
        return rstd * (summed[:rows] * gain - block.astype(F32) * rstd * mean)

    grad_mid = cotangent.astype(F32) + norm_back(summed2, gain2, mid_block, scale2)
    branch = grad_mid.astype(BF16)
    branch_x = swap(branch, "x")
    branch_c, branch_cx = swap(branch, "c"), swap(branch_x, "c")
    branch_x, branch_c, branch_cx, gate_got, up = together(
        branch_x, branch_c, branch_cx, gate_got, up
    )
    gate = add_rows(gate, gate_got)
    up_got = exchange_rows(up)
    pieces = (branch, branch_c, branch_x, branch_cx)

    grad_att, wo_back = small_call(
        project_back_kernel,
        "project_back",
        6,
        where[0],
        (*pieces, att_t, wo),
        [shape(att_t.shape, BF16), shape(wo.shape, BF16)],
    )
    grad_att, wo_back, down = together(grad_att, wo_back, spread_z(down))
    grad_att = grad_att.reshape(nz * ny, HDIM, rows)
    grad_att, gate = together(
        lax.all_to_all(grad_att, ("z", "y"), split_axis=0, concat_axis=0, tiled=True), gate
    )
    gate = spread_z(gate)
    back, up_got, up = together(
        attend_back(tables, tiles, q_mask, k_mask, grad_att, att, log_norm, cosine, sine),
        up_got,
        up,
    )
    up = add_rows(up, up_got)
    if nq > 1:
        grad_q = of_queries(back)[:, :HDIM]
        grad_kv = lax.psum_scatter(back[:, HDIM:], "q", scatter_dimension=0, tiled=True)
        back = jnp.concatenate([grad_q, grad_kv], axis=1)
    def qkv_back(s, place):
        chunk = pl.BlockSpec((1, head, rows), lambda i, where: (s, 0, 0))
        specs = {0: pl.BlockSpec((rows, width), lambda i, where: (s, 0)), 1: chunk, 2: chunk}
        return small_call(
            qkv_back_kernel,
            "qkv_back",
            5,
            place,
            (normed1, back, other_back, *w_qkv),
            [shape((2, rows + EXTRA, cols), BF16)] * 2 + [shape((1, width), F32)],
            specs,
        )

    other_back, place, gate = together(swap(back[nz:], "y"), where[1], gate)
    part1, place = together(qkv_back(1, place), where[2])
    up = spread_z(up)
    got1, part2, qkv_grads, place = together(
        swap(part1[1], "c"),
        qkv_back(2, place),
        small_call(
            qkv_weights_kernel,
            "qkv_weights",
            8,
            place,
            (normed1, back, other_back),
            [shape((nz, ny * head, half), BF16)] * 2,
        ),
        where[3],
    )
    own1, send1 = first_sum(part1[0], got1)
    own1, got1, got2, part3, qkv_own, qkv_got, place, up = together(
        own1,
        swap(send1, "x"),
        swap(part2[1], "c"),
        qkv_back(3, place),
        qkv_grads[0],
        exchange_lanes(qkv_grads[1]),
        where[0],
        up,
    )
    own2, send2 = first_sum(part2[0], got2)
    sum1 = (own1 + got1.astype(F32)).astype(BF16)
    carried, own2, got2, got3, part0 = together(
        ring(sum1, nz),
        own2,
        swap(send2, "x"),
        swap(part3[1], "c"),
        qkv_back(0, place),
    )
    qkv_grads = spread_z(scatter_lanes(qkv_own, qkv_got))
    own3, send3 = first_sum(part3[0], got3)
    sum2 = (own2 + got2.astype(F32) + carried.astype(F32)).astype(BF16)
    terms1 = part0[2] + part1[2] + part2[2] + part3[2]
    terms1 = jnp.concatenate([terms1, terms2], axis=0)
    terms1 = terms1 + swap(terms1, "c")
    carried, own3, got3, got0, terms1, terms1_x, qkv_grads = together(
        ring(sum2, nz),
        own3,
        swap(send3, "x"),
        swap(part0[1], "c"),
        terms1,
        swap(terms1, "x"),
        qkv_grads,
    )
    own0, send0 = first_sum(part0[0], got0)
    sum3 = (own3 + got3.astype(F32) + carried.astype(F32)).astype(BF16)
    peak_slots = jnp.zeros((nz * groups, 2 * width // (nz * groups)), F32)
    peak_slots = lax.dynamic_update_slice(
        peak_slots, jnp.broadcast_to(jnp.max(peak), (1, peak_slots.shape[1])), (zi * groups + group, 0)
    )
    terms1 = jnp.stack([terms1 + terms1_x, peak_slots.reshape(2, width)])
    terms1 = sum_small(terms1, ("y", "q"))
    terms1_z = lax.ppermute(terms1, "z", [(i, i ^ 1) for i in range(nz)])
    carried, own0, got0, terms1, terms1_z = together(
        ring(sum3, nz), own0, swap(send0, "x"), terms1, terms1_z
    )
    terms1 = terms1 + terms1_z
    terms1 = terms1 + lax.ppermute(terms1, "z", [(i, i ^ 2) for i in range(nz)])
    summed1 = own0 + got0.astype(F32) + carried.astype(F32)
    grad_in = (grad_mid + norm_back(summed1, gain1, hidden_in, scale1[0])).astype(BF16)

    grad_wd = lay_out(down, True)
    grad_wg = lay_out(gate, False)
    grad_wu = lay_out(up, False)
    branch_ffn = summed2[rows + EXTRA :]
    hidden_out = (residual_mid + branch_ffn.astype(F32)).astype(BF16)
    if nq > 1:
        wo_back = wo_back.reshape(nz * 2, -1, groups // 2, slab).transpose(0, 2, 1, 3)
        wo_back = wo_back.reshape(nz * groups, -1, slab)
    grad_wo = lax.psum_scatter(wo_back, WIDE, scatter_dimension=0, tiled=False).astype(F32)
    grad_qkv = small_call(
        qkv_out_kernel,
        "lay_out_qkv",
        3,
        where[0],
        (qkv_grads,),
        [shape((slab, nz * ny * HDIM), F32)] * 3,
    )

    peaks = terms1[1].reshape(nz * groups, -1)[:, 0]
    gain_terms = terms1[0].reshape(2, 2, nz, half)
    gain_terms = gain_terms.transpose(0, 2, 1, 3).reshape(2, width) / gains
    terms = lax.dynamic_slice_in_dim(gain_terms, (zi * groups + group) * slab, slab, 1)
    peaks = peaks.reshape(nz, nq, ny)
    head_peaks = jnp.max(peaks, axis=1).reshape(nz * ny)
    factor = jnp.sqrt(clip_limit / jnp.maximum(head_peaks, clip_limit))
    column_factor = jnp.repeat(factor, HDIM)
    return (
        hidden_out,
        grad_in,
        grad_qkv[0],
        grad_qkv[1],
        grad_qkv[2],
        grad_wo,
        grad_wg,
        grad_wu,
        grad_wd,
        terms[0],
        terms[1],
        w_query.astype(F32) * column_factor[None, :],
        w_key.astype(F32) * column_factor[None, :],
        head_peaks,
    )


def solution(mesh):
    wide, narrow = mesh.devices.shape
    sizes = (4, wide // 8, 2, narrow // 2, 2)
    fine = Mesh(mesh.devices.reshape(sizes), ("z", "q", "y", "x", "c"))
    both = P(WIDE, NARROW)
    turned = P(NARROW, WIDE)
    return jax.shard_map(
        functools.partial(on_device, sizes),
        mesh=fine,
        in_specs=(
            both, P(WIDE), both, both, both, turned, P(WIDE), both, both, turned, both, P(), P()
        ),
        out_specs=(
            both, both, both, both, both, turned, both, both, turned,
            P(WIDE), P(WIDE), both, both, P(NARROW),
        ),
        check_vma=False,
    )
```
